32 devices in a mesh: wide: 4 (over z), narrow: 8 (over y, x, core).
Axes of the slice: x: 2, y: 2, z: 4, core: 2. Of those that a mesh axis runs over, the one named last changes fastest.
Arguments:
- layer_in: bfloat16 [8, 1024, 1536], P('wide', 'narrow'), may hold values from -6 to 6
- seg_ids: int32 [8, 1024], P('wide', 'narrow'), may hold values from 1 to 1025, as said below
- pad_mask: int32 [8, 1024], P('wide', 'narrow'), may hold values from 0 to 1, as said below
- gain_attn: bfloat16 [1536], P(('wide', 'narrow')), may hold values from 0.5 to 1.5
- w_query: bfloat16 [1536, 1536], P(('wide', 'narrow')), may hold values from -0.15625 to 0.15625
- b_query: bfloat16 [1536], P(('wide', 'narrow')), may hold values from -3 to 3
- w_key: bfloat16 [1536, 256], P(('wide', 'narrow')), may hold values from -0.15625 to 0.15625
- b_key: bfloat16 [256], P(('wide', 'narrow')), may hold values from -3 to 3
- w_value: bfloat16 [1536, 256], P(('wide', 'narrow')), may hold values from -0.15625 to 0.15625
- b_value: bfloat16 [256], P(('wide', 'narrow')), may hold values from -3 to 3
- w_out: bfloat16 [1536, 1536], P(('wide', 'narrow')), may hold values from -1.25 to 1.25
- gain_mlp: bfloat16 [1536], P(('wide', 'narrow')), may hold values from 0.5 to 1.5
- w_gate: bfloat16 [1536, 8960], P('wide', 'narrow'), may hold values from -0.15625 to 0.15625
- w_up: bfloat16 [1536, 8960], P('wide', 'narrow'), may hold values from -0.15625 to 0.15625
- w_down: bfloat16 [8960, 1536], P('narrow', 'wide'), may hold values from -0.09375 to 0.09375
- grad_out: bfloat16 [8, 1024, 1536], P('wide', 'narrow'), may hold values from -6 to 6
Outputs:
- layer_out: bfloat16 [8, 1024, 1536], P('wide', 'narrow')
- grad_in: bfloat16 [8, 1024, 1536], P('wide', 'narrow')
- grad_gain_attn: float32 [1536], P(('wide', 'narrow'))
- grad_w_query: float32 [1536, 1536], P(('wide', 'narrow'))
- grad_b_query: float32 [1536], P(('wide', 'narrow'))
- grad_w_key: float32 [1536, 256], P(('wide', 'narrow'))
- grad_b_key: float32 [256], P(('wide', 'narrow'))
- grad_w_value: float32 [1536, 256], P(('wide', 'narrow'))
- grad_b_value: float32 [256], P(('wide', 'narrow'))
- grad_w_out: float32 [1536, 1536], P(('wide', 'narrow'))
- grad_gain_mlp: float32 [1536], P(('wide', 'narrow'))
- grad_w_gate: float32 [1536, 8960], P('wide', 'narrow')
- grad_w_up: float32 [1536, 8960], P('wide', 'narrow')
- grad_w_down: float32 [8960, 1536], P('narrow', 'wide')
The draws below stay inside these ranges and needn't reach their ends.
Inputs may be any that keep to these rules, and one draw needn't show every extreme that they name: `seg_ids`: along each row the numbers start at 1 and never fall; padding tokens carry the number 1024 + 1, above every real document. Among the 2 rows of each index of wide, one row is a single document covering all but 1 to 127 of its tokens. `pad_mask`: each row is 1 up to its valid length and 0 after it.
All inputs are finite; a program needn't handle non-finite values.
Results may differ from the reference program's by a relative error of at most 0.023.
Values may be sent and summed in bfloat16 or wider, within the bound.
No kernel may reach another device: no remote copies, remote signals or barrier semaphores. Data moves between devices by JAX's collectives and lax.ppermute only.
A program may use at most 384 MiB of HBM per device.

```python
import math
import jax
import jax.numpy as jnp
from jax import lax

D = 1536
FF = 8960
Q_HEADS = 12
KV_HEADS = 2
HEAD = 128
SEG = 128
ROWS = 2
LEN = 1024
BATCH = 8
HQ = 1536
HK = 256


def doc_layout(key):
    keys = jax.random.split(key, 5)
    tokens = jnp.arange(LEN, dtype=jnp.int32)[None, :]
    row = jnp.arange(BATCH, dtype=jnp.int32)[:, None]
    chosen = jax.random.randint(keys[0], (BATCH // ROWS,), 0, ROWS)
    long_row = row % ROWS == chosen[row // ROWS]
    slack = jax.random.randint(keys[1], (BATCH, 1), 1, SEG)
    short_valid = jax.random.randint(keys[2], (BATCH, 1), LEN // 4, LEN + 1)
    valid = jnp.where(long_row, LEN - slack, short_valid)
    shift = jax.random.randint(keys[3], (BATCH, 1), 2, 6)
    spacing = jnp.maximum(LEN // 2 ** shift, 2)
    marks = jax.random.randint(keys[4], (BATCH, LEN), 0, 1 << 20) % spacing == 0
    starts = marks & jnp.logical_not(long_row) | (tokens == 0)
    docs = jnp.cumsum(starts.astype(jnp.int32), axis=1)
    seg = jnp.where(tokens >= valid, LEN + 1, docs)
    pad = (tokens < valid).astype(jnp.int32)
    return (seg, pad)


def draw_seg_ids(key, part):
    seg, pad = doc_layout(key)
    return seg


def draw_pad_mask(key, part):
    seg, pad = doc_layout(key)
    return pad


def spiked(drawn, key, source, target, shards_of, factor):
    def block_of(dim):
        return (jnp.arange(drawn.shape[dim]) // (drawn.shape[dim] // shards_of)).reshape((-1,) + (1,) * (drawn.ndim - 1 - dim))

    first = jax.random.permutation(key, shards_of)[block_of(target)]
    second = (block_of(target) + shards_of // 2) % shards_of
    return jnp.where((block_of(source) == first) | (block_of(source) == second), factor * drawn, drawn)


def levels(rng, extent, pieces, least, high):
    gain, own = 1.0, jax.random.fold_in(rng, 6)
    for axis_at, blocks in pieces:
        draws = jnp.exp(jax.random.uniform(jax.random.fold_in(own, axis_at), (blocks,), jnp.float32, least / len(pieces), high / len(pieces)))
        gain = gain * jnp.repeat(draws, extent[axis_at] // blocks).reshape([-1 if axis == axis_at else 1 for axis in range(len(extent))])
    return gain


def bell_draw(stream_key, shape, scale, most, cuts=(), kind=jnp.bfloat16):
    level = levels(stream_key, shape, cuts, -0.22, 0.18) if cuts else 1.0
    array = jax.random.normal(stream_key, shape, jnp.float32) * scale * level
    return jnp.minimum(jnp.maximum(array, -most), most).astype(kind)


def heavy_noise(key, dims, width, bound, cuts, heavy, kind=jnp.bfloat16):
    drawn = width * jax.random.normal(key, dims, jnp.float32)
    if cuts:
        drawn = drawn * levels(key, dims, cuts, -0.22, 0.18)
    return jnp.clip(spiked(drawn, jax.random.fold_in(key, 3), *heavy), -bound, bound).astype(kind)


def setup_inputs(seed: int = 0) -> dict:
    key_list = jax.random.split(jax.random.key(seed), 17)
    return {
        "layer_in": bell_draw(key_list[0], (BATCH, LEN, D), 1.0, 6.0, ((0, 4), (1, 8))),
        "seg_ids": draw_seg_ids(jax.random.fold_in(key_list[16], 71), 0),
        "pad_mask": draw_pad_mask(jax.random.fold_in(key_list[16], 71), 0),
        "gain_attn": jnp.clip(1.0 + 0.1 * jax.random.normal(key_list[3], (D,), jnp.float32), 0.5, 1.5).astype(jnp.bfloat16),
        "w_query": bell_draw(key_list[4], (D, HQ), D ** -0.5, 0.15625, ((0, 32),)),
        "b_query": bell_draw(key_list[5], (HQ,), 0.5, 3.0, ((0, 32),)),
        "w_key": bell_draw(key_list[6], (D, HK), D ** -0.5, 0.15625, ((0, 32),)),
        "b_key": bell_draw(key_list[7], (HK,), 0.5, 3.0, ((0, 32),)),
        "w_value": bell_draw(key_list[8], (D, HK), D ** -0.5, 0.15625, ((0, 32),)),
        "b_value": bell_draw(key_list[9], (HK,), 0.5, 3.0, ((0, 32),)),
        "w_out": bell_draw(key_list[10], (HQ, D), (HQ // 64) ** -0.5, 1.25, ((0, 32),)),
        "gain_mlp": jnp.clip(1.0 + 0.1 * jax.random.normal(key_list[11], (D,), jnp.float32), 0.5, 1.5).astype(jnp.bfloat16),
        "w_gate": bell_draw(key_list[12], (D, FF), D ** -0.5, 0.15625, ((0, 4), (1, 8))),
        "w_up": bell_draw(key_list[13], (D, FF), D ** -0.5, 0.15625, ((0, 4), (1, 8))),
        "w_down": heavy_noise(key_list[14], (FF, D), FF ** -0.5, 0.09375, ((0, 8), (1, 4)), (0, 1, 8, 2.0)),
        "grad_out": bell_draw(key_list[15], (BATCH, LEN, D), 1.0, 6.0, ((0, 4), (1, 8))),
    }


EPS = 1e-06
THETA = 10000.0

@jax.custom_vjp
def low(v):
    return lax.optimization_barrier(v.astype(jnp.bfloat16)).astype(jnp.float32)

@jax.custom_vjp
def low_back(v):
    return v

def low_keep(v):
    return (low(v), None)

def low_pass(kept, grad):
    return (grad,)

def back_keep(v):
    return (v, None)

def back_low(kept, grad):
    return (low(grad),)
low.defvjp(low_keep, low_pass)
low_back.defvjp(back_keep, back_low)

def matmul(left, right):
    return jnp.dot(left, right, precision=lax.Precision.HIGHEST)

def normed(value):
    return value * lax.rsqrt(lax.optimization_barrier(jnp.mean(value * value, axis=-1, keepdims=True)) + EPS)

def rotate(value, cosine, sine):
    half = value.shape[-1] // 2
    first = value[..., :half]
    second = value[..., half:]
    return jnp.concatenate([first * cosine - second * sine, second * cosine + first * sine], axis=-1)

def angles(places):
    freq = jnp.exp(jnp.arange(HEAD // 2, dtype=jnp.float32) * (-2.0 * math.log(THETA) / HEAD))
    turn = places.astype(jnp.float32)[..., None] * freq
    return (jnp.cos(turn), jnp.sin(turn))

def row_layer(row_x, params, seg_row, pad_row):
    g_one, wq, bq, wk, bk, wv, bv, wo, g_two, wg, wu, wd = params
    group = Q_HEADS // KV_HEADS
    scale = 1.0 / math.sqrt(HEAD)
    index = jnp.arange(LEN, dtype=jnp.int32)
    begins = lax.optimization_barrier(jnp.sum((seg_row[None, :] < seg_row[:, None]).astype(jnp.int32), axis=-1))
    cosine, sine = angles(index - begins)
    cosine = cosine[:, None, :]
    sine = sine[:, None, :]
    h_one = low(normed(row_x) * g_one)
    query = low(rotate(low_back(matmul(h_one, wq) + bq).reshape(LEN, Q_HEADS, HEAD), cosine, sine))
    query = query.reshape(LEN, KV_HEADS, group, HEAD)
    keys = low(rotate(low_back(matmul(h_one, wk) + bk).reshape(LEN, KV_HEADS, HEAD), cosine, sine))
    values = low(low_back(matmul(h_one, wv) + bv)).reshape(LEN, KV_HEADS, HEAD)
    block = min(512, LEN)
    starts = jnp.arange(LEN // block, dtype=jnp.int32) * block

    def one_block(begin):
        q_block = lax.dynamic_slice_in_dim(query, begin, block, 0)
        s_block = lax.dynamic_slice_in_dim(seg_row, begin, block, 0)
        q_index = begin + jnp.arange(block, dtype=jnp.int32)
        allowed = (s_block[:, None] == seg_row[None, :]) & (index[None, :] < q_index[:, None]) & (pad_row[None, :] == 1) | (index[None, :] == q_index[:, None])
        scores = low_back(jnp.einsum('qhgd,khd->hgqk', q_block, keys, precision=lax.Precision.HIGHEST)) * scale
        scores = jnp.where(allowed[None, None], scores, -1e+30)
        probs = jax.nn.softmax(scores, axis=-1)
        return jnp.einsum('hgqk,khd->qhgd', low(probs), values, precision=lax.Precision.HIGHEST)
    blocks = lax.map(jax.checkpoint(one_block), starts)
    attended = low(low_back(blocks.reshape(LEN, Q_HEADS * HEAD)))
    x_mid = row_x + low_back(matmul(attended, wo))
    h_two = low(normed(x_mid) * g_two)
    gate = low_back(matmul(h_two, wg))
    up = low_back(matmul(h_two, wu))
    hidden = low(jax.nn.silu(gate) * up)
    return x_mid + matmul(hidden, wd)

def reference(layer_in, seg_ids, pad_mask, gain_attn, w_query, b_query, w_key, b_key, w_value, b_value, w_out, gain_mlp, w_gate, w_up, w_down, grad_out):
    params = tuple((item.astype(jnp.float32) for item in (gain_attn, w_query, b_query, w_key, b_key, w_value, b_value, w_out, gain_mlp, w_gate, w_up, w_down)))

    def step(totals, items):
        row_x, seg_row, pad_row, row_grad = items

        def apply(value, weights):
            return row_layer(value, weights, seg_row, pad_row)
        result, pull = jax.vjp(apply, row_x.astype(jnp.float32), params)
        d_value, d_params = pull(row_grad.astype(jnp.float32))
        totals = tuple((total + grad for total, grad in zip(totals, d_params)))
        return (totals, (result.astype(jnp.bfloat16), d_value.astype(jnp.bfloat16)))
    zeros = tuple((jnp.zeros_like(item) for item in params))
    totals, (outputs, grads) = lax.scan(step, zeros, (layer_in, seg_ids, pad_mask, grad_out))
    return (outputs, grads, totals[0], totals[1], totals[2], totals[3], totals[4], totals[5], totals[6], totals[7], totals[8], totals[9], totals[10], totals[11])
```

```python
import math

import jax
import jax.numpy as jnp
from jax import lax
from jax.sharding import PartitionSpec as P

Q_HEADS = 12
KV_HEADS = 2
HEAD = 128
HQ = 1536
HK = 256

EPS = 1e-06
THETA = 10000.0

F32 = jnp.float32
BF16 = jnp.bfloat16


def norm_parts(value):
    factor = lax.rsqrt(jnp.mean(value * value, axis=-1, keepdims=True) + EPS)
    return (value * factor, factor)


def norm_back(grad, unit, factor, gain):
    scaled = grad * gain
    return factor * (scaled - unit * jnp.mean(scaled * unit, axis=-1, keepdims=True))


def rotate(value, cosine, sine):
    half = value.shape[-1] // 2
    first = value[..., :half]
    second = value[..., half:]
    return jnp.concatenate(
        [first * cosine - second * sine, second * cosine + first * sine], axis=-1
    )


def angles(places, head_size):
    freq = jnp.exp(
        jnp.arange(head_size // 2, dtype=jnp.float32) * (-2.0 * math.log(THETA) / head_size)
    )
    turn = places.astype(jnp.float32)[..., None] * freq
    return (jnp.cos(turn), jnp.sin(turn))


def row_probs(query, keys, allowed, scale):
    scores = jnp.einsum("qhgd,khd->hgqk", query, keys, preferred_element_type=F32) * scale
    scores = jnp.where(allowed[None, None], scores, -1e30)
    top = jnp.max(scores, axis=-1, keepdims=True)
    expo = jnp.exp(scores - top)
    return expo / jnp.sum(expo, axis=-1, keepdims=True)


def mm(left, right):
    return jnp.dot(left, right, preferred_element_type=F32)


def mm_t(left, right):
    return lax.dot_general(
        left, right, (((left.ndim - 1,), (1,)), ((), ())), preferred_element_type=F32
    )


def t_mm(left, right):
    return lax.dot_general(left, right, (((0,), (0,)), ((), ())), preferred_element_type=F32)


class Links:
    def __init__(self, wide, narrow):
        self.wide, self.narrow = wide, narrow
        bits = [1 << i for i in range(1, (narrow - 1).bit_length())]
        half = len(bits) // 2
        core = [1] if narrow > 1 else []
        self.orders = (bits + core, bits[half:] + bits[:half] + core)
        self.ring = [(i, (i + 1) % wide) for i in range(wide)]

    def hop(self, value, bit):
        return lax.ppermute(value, "narrow", [(i, i ^ bit) for i in range(self.narrow)])

    def offsets(self, which):
        found = [0]
        for bit in self.orders[which]:
            found = found + [o ^ bit for o in found]
        return found

    def gather(self, value, which):
        held = value[None]
        for bit in self.orders[which]:
            held = jnp.concatenate([held, self.hop(held, bit)], axis=0)
        return held

    def scatter(self, blocks, which, bits=None):
        for bit in reversed(self.orders[which] if bits is None else bits):
            half = blocks.shape[0] // 2
            got = self.hop(blocks[half:], bit)
            blocks = (blocks[:half].astype(F32) + got.astype(F32)).astype(blocks.dtype)
        return blocks[0]

    def ring_gather(self, value):
        slots = [value]
        for _ in range(self.wide - 1):
            slots.append(lax.ppermute(slots[-1], "wide", self.ring))
        return slots

    def ring_scatter(self, slots):
        got = None
        for k in range(1, self.wide):
            send = slots[k] if got is None else (slots[k].astype(F32) + got.astype(F32)).astype(BF16)
            got = lax.ppermute(send, "wide", self.ring)
        if got is None:
            return slots[0].astype(F32)
        return slots[0].astype(F32) + got.astype(F32)

    def direct_gather(self, value):
        return [value] + [
            lax.ppermute(value, "wide", [(i, (i + k) % self.wide) for i in range(self.wide)])
            for k in range(1, self.wide)
        ]

    def direct_scatter(self, slots):
        total = slots[0].astype(F32)
        for k in range(1, self.wide):
            total = total + lax.ppermute(
                slots[k], "wide", [(i, (i - k) % self.wide) for i in range(self.wide)]
            ).astype(F32)
        return total


def on_device(
    layer_in,
    seg_ids,
    pad_mask,
    gain_attn,
    w_query,
    b_query,
    w_key,
    b_key,
    w_value,
    b_value,
    w_out,
    gain_mlp,
    w_gate,
    w_up,
    w_down,
    grad_out,
):
    rows, seg_len, width = layer_in.shape
    wide = lax.axis_size("wide")
    parts = lax.axis_size("narrow")
    links = Links(wide, parts)
    here = lax.axis_index("wide")
    me = lax.axis_index("narrow")
    row_len = seg_len * parts
    tokens = rows * seg_len
    group = Q_HEADS // KV_HEADS
    scale = 1.0 / math.sqrt(HEAD)
    share = w_query.shape[0]
    small = b_key.shape[0]
    slot = width // wide
    which = [row % 2 for row in range(rows)]

    vectors = jnp.concatenate([gain_attn, gain_mlp, b_query, b_key, b_value])
    vectors = jnp.pad(vectors, (0, 2 * HK - vectors.shape[0]))[None]
    kv_own = jnp.concatenate([jnp.concatenate([w_key, w_value], axis=1), vectors], axis=0)

    def gather_weight(own, order):
        held = links.gather(jnp.stack(links.direct_gather(own)), order)
        if order == 0:
            return held
        at = {offset: i for i, offset in enumerate(links.offsets(order))}
        return jnp.concatenate([held[at[o]][None] for o in links.offsets(0)], axis=0)

    def scatter_weight(grad, order):
        if order != 0:
            at = {offset: i for i, offset in enumerate(links.offsets(0))}
            grad = jnp.concatenate([grad[at[o]][None] for o in links.offsets(order)], axis=0)
        held = links.scatter(grad, order)
        return links.direct_scatter([held[k] for k in range(wide)])

    kv_all = gather_weight(kv_own, 1)
    wq = gather_weight(w_query, 0).reshape(width, HQ)
    wo = gather_weight(w_out, 1).reshape(HQ, width)
    wkv = kv_all[:, :, :share].reshape(width, 2 * HK)
    packed = kv_all[:, :, share]
    g_one_rel = packed[:, :, :share].reshape(width).astype(F32)
    g_two_rel = packed[:, :, share : 2 * share].reshape(width)
    bq_rel = packed[:, :, 2 * share : 3 * share].reshape(HQ)
    bk_rel = packed[:, :, 3 * share : 3 * share + small].reshape(HK)
    bv_rel = packed[:, :, 3 * share + small : 3 * share + 2 * small].reshape(HK)

    def placing(block):
        offs = jnp.array(links.offsets(0), jnp.int32) ^ me
        from_wide = (here - jnp.arange(wide, dtype=jnp.int32)) % wide
        source = (
            (from_wide[None, :, None] * parts + offs[:, None, None]) * block
            + jnp.arange(block, dtype=jnp.int32)[None, None, :]
        ).reshape(-1)
        count = block * parts * wide
        return (jnp.arange(count, dtype=jnp.int32)[:, None] == source[None, :]).astype(BF16)

    place = placing(share)
    place_small = placing(small)

    def to_rel(value):
        return mm(value, place).astype(BF16)

    def from_rel(value):
        return mm_t(value, place).astype(BF16)

    two = mm_t(jnp.stack([g_two_rel, bq_rel]), place)
    g_two, bq = two[0], two[1]
    two = mm_t(jnp.stack([bk_rel, bv_rel]), place_small)
    bkv = two.reshape(2 * HK)

    wg_slots = links.ring_gather(w_gate)
    wu_slots = links.ring_gather(w_up)
    wd_slots = links.ring_gather(w_down)
    wg = jnp.concatenate(wg_slots, axis=0)
    wu = jnp.concatenate(wu_slots, axis=0)
    wd = jnp.concatenate(wd_slots, axis=1)

    def rolled(value):
        return jnp.concatenate(
            [
                lax.dynamic_slice_in_dim(value, ((here - k) % wide) * slot, slot, value.ndim - 1)
                for k in range(wide)
            ],
            axis=-1,
        )

    def unrolled(value):
        return jnp.concatenate(
            [
                lax.dynamic_slice_in_dim(value, ((here - k) % wide) * slot, slot, value.ndim - 1)
                for k in range(wide)
            ],
            axis=-1,
        )

    def gather_tokens(value):
        return jnp.stack([links.gather(value[r], which[r]) for r in range(rows)])

    def scatter_tokens(value):
        return jnp.stack([links.scatter(value[r], which[r]) for r in range(rows)])

    marks = gather_tokens(jnp.stack([seg_ids, pad_mask], axis=1))
    ids_all = marks[:, :, 0].reshape(rows, row_len)
    pads_all = marks[:, :, 1].reshape(rows, row_len)
    sources = jnp.array([links.offsets(which[r]) for r in range(rows)], jnp.int32) ^ me
    key_idx = (
        sources[:, :, None] * seg_len + jnp.arange(seg_len, dtype=jnp.int32)[None, None, :]
    ).reshape(rows, row_len)
    global_idx = me * seg_len + jnp.arange(seg_len, dtype=jnp.int32)
    begins = jnp.sum((ids_all[:, None, :] < seg_ids[:, :, None]).astype(jnp.int32), axis=-1)
    cosine, sine = angles(global_idx[None, :] - begins, HEAD)
    cosine = cosine[:, :, None, :]
    sine = sine[:, :, None, :]
    allowed = (ids_all[:, None, :] == seg_ids[:, :, None]) & (
        key_idx[:, None, :] < global_idx[None, :, None]
    ) & (pads_all[:, None, :] == 1) | (key_idx[:, None, :] == global_idx[None, :, None])

    x_in = layer_in.reshape(tokens, width).astype(F32)
    x_rel = mm(layer_in.reshape(tokens, width), place)
    unit_one, factor_one = norm_parts(x_rel)
    h_one = (unit_one * g_one_rel).astype(BF16)
    kv_lin = mm(h_one, wkv) + bkv
    k_rot = rotate(kv_lin[:, :HK].reshape(rows, seg_len, KV_HEADS, HEAD), cosine, sine)
    k_rot = k_rot.astype(BF16).reshape(rows, seg_len, HK)
    v_low = kv_lin[:, HK:].astype(BF16).reshape(rows, seg_len, HK)
    kv_rows = gather_tokens(jnp.concatenate([k_rot, v_low], axis=-1))
    kv_rows = kv_rows.reshape(rows, row_len, 2, KV_HEADS, HEAD)
    keys_all = kv_rows[:, :, 0]
    values_all = kv_rows[:, :, 1]
    q_lin = mm(h_one, wq) + bq
    q_rot = rotate(q_lin.reshape(rows, seg_len, Q_HEADS, HEAD), cosine, sine).astype(BF16)
    queries = q_rot.reshape(rows, seg_len, KV_HEADS, group, HEAD)
    outputs = []
    for row in range(rows):
        probs = row_probs(queries[row], keys_all[row], allowed[row], scale)
        outputs.append(
            jnp.einsum(
                "hgqk,khd->qhgd", probs.astype(BF16), values_all[row], preferred_element_type=F32
            )
        )
    attended = to_rel(jnp.stack(outputs).reshape(tokens, HQ).astype(BF16))
    x_mid = x_in + mm(attended, wo)
    unit_two, factor_two = norm_parts(x_mid)
    h_two = rolled((unit_two * g_two).astype(BF16))

    all_tokens = rows * row_len
    grad_all = gather_tokens(rolled(grad_out)).reshape(all_tokens, width)
    h_all = gather_tokens(h_two.reshape(rows, seg_len, width)).reshape(all_tokens, width)
    d_hidden = mm_t(grad_all, wd)
    gate = mm(h_all, wg)
    up = mm(h_all, wu)
    sigma = jax.nn.sigmoid(gate)
    active = gate * sigma
    hidden = (active * up).astype(BF16)
    d_gate = (d_hidden * up * sigma * (1.0 + gate * (1.0 - sigma))).astype(BF16)
    d_up = (d_hidden * active).astype(BF16)

    def by_token(value):
        return value.astype(BF16).reshape(rows, parts, seg_len, width)

    d_h_two = scatter_tokens(by_token(mm_t(d_gate, wg) + mm_t(d_up, wu)))
    mixed = scatter_tokens(by_token(mm(hidden, wd)))
    layer_out = (x_mid + unrolled(mixed.reshape(tokens, width)).astype(F32)).astype(BF16)

    def row_slots(grad):
        return [grad[k * slot : (k + 1) * slot].astype(BF16) for k in range(wide)]

    grad_w_down = links.ring_scatter(
        [
            t_mm(hidden, grad_all[:, k * slot : (k + 1) * slot]).astype(BF16)
            for k in range(wide)
        ]
    )
    grad_w_gate = links.ring_scatter(row_slots(t_mm(h_all, d_gate)))
    grad_w_up = links.ring_scatter(row_slots(t_mm(h_all, d_up)))

    d_h_two = unrolled(d_h_two.reshape(tokens, width)).astype(F32)
    d_g_two = jnp.sum(d_h_two * unit_two, axis=0)
    d_mid = grad_out.reshape(tokens, width).astype(F32) + norm_back(
        d_h_two, unit_two, factor_two, g_two
    )
    d_branch = d_mid.astype(BF16)
    d_wo = t_mm(attended, d_branch)
    grad_w_out = scatter_weight(d_wo.astype(BF16).reshape(parts, wide, share, width), 1)
    d_attended = from_rel(mm_t(d_branch, wo).astype(BF16))
    d_att_heads = d_attended.reshape(rows, seg_len, KV_HEADS, group, HEAD)
    query_grads = []
    kv_grads = []
    for row in range(rows):
        probs = row_probs(queries[row], keys_all[row], allowed[row], scale)
        d_prob = jnp.einsum(
            "qhgd,khd->hgqk", d_att_heads[row], values_all[row], preferred_element_type=F32
        )
        delta = jnp.sum(probs * d_prob, axis=-1, keepdims=True)
        d_score = (scale * probs * (d_prob - delta)).astype(BF16)
        query_grads.append(
            jnp.einsum("hgqk,khd->qhgd", d_score, keys_all[row], preferred_element_type=F32)
        )
        d_key = jnp.einsum("hgqk,qhgd->khd", d_score, queries[row], preferred_element_type=F32)
        d_value = jnp.einsum(
            "hgqk,qhgd->khd", probs.astype(BF16), d_att_heads[row], preferred_element_type=F32
        )
        kv_grads.append(
            jnp.concatenate(
                [d_key.reshape(row_len, HK), d_value.reshape(row_len, HK)], axis=-1
            ).astype(BF16)
        )
    d_kv = jnp.stack(kv_grads).reshape(rows, parts, seg_len, 2 * HK)
    d_kv = scatter_tokens(d_kv).reshape(rows, seg_len, 2 * HK).astype(F32)
    d_query = jnp.stack(query_grads).reshape(rows, seg_len, Q_HEADS, HEAD)
    dq_lin = rotate(d_query, cosine, -sine).reshape(tokens, HQ).astype(BF16)
    d_wq = t_mm(h_one, dq_lin)
    grad_w_query = scatter_weight(d_wq.astype(BF16).reshape(parts, wide, share, HQ), 0)
    dk_lin = rotate(d_kv[..., :HK].reshape(rows, seg_len, KV_HEADS, HEAD), cosine, -sine)
    dk_lin = dk_lin.reshape(tokens, HK).astype(BF16)
    dv_lin = d_kv[..., HK:].reshape(tokens, HK).astype(BF16)
    dkv_lin = jnp.concatenate([dk_lin, dv_lin], axis=-1)
    d_wkv = t_mm(h_one, dkv_lin)
    d_bq = jnp.sum(dq_lin.astype(F32), axis=0)
    d_bkv = jnp.sum(dkv_lin.astype(F32), axis=0).reshape(2, HK)
    d_h_one = mm_t(dq_lin, wq) + mm_t(dkv_lin, wkv)
    d_g_one = jnp.sum(d_h_one * unit_one, axis=0)
    back = norm_back(d_h_one, unit_one, factor_one, g_one_rel).astype(BF16)
    grad_in = (d_mid + mm_t(back, place)).astype(BF16)

    two = mm(jnp.stack([d_g_two, d_bq]).astype(BF16), place)
    two = two.reshape(2, parts, wide, share)
    small_two = mm(d_bkv.astype(BF16), place_small).reshape(2, parts, wide, small)
    vec = jnp.concatenate(
        [
            d_g_one.reshape(parts, wide, share),
            two[0],
            two[1],
            small_two[0],
            small_two[1],
        ],
        axis=-1,
    )
    vec = jnp.pad(vec, ((0, 0), (0, 0), (0, 2 * HK - vec.shape[-1])))[:, :, None]
    kv_block = jnp.concatenate([d_wkv.reshape(parts, wide, share, 2 * HK), vec], axis=2)
    kv_sum = scatter_weight(kv_block.astype(BF16), 1)
    grad_w_key = kv_sum[:share, :HK]
    grad_w_value = kv_sum[:share, HK:]
    last = kv_sum[share]
    grad_gain_attn = last[:share]
    grad_gain_mlp = last[share : 2 * share]
    grad_b_query = last[2 * share : 3 * share]
    grad_b_key = last[3 * share : 3 * share + small]
    grad_b_value = last[3 * share + small : 3 * share + 2 * small]
    return (
        layer_out.reshape(rows, seg_len, width),
        grad_in.reshape(rows, seg_len, width),
        grad_gain_attn,
        grad_w_query,
        grad_b_query,
        grad_w_key,
        grad_b_key,
        grad_w_value,
        grad_b_value,
        grad_w_out,
        grad_gain_mlp,
        grad_w_gate,
        grad_w_up,
        grad_w_down,
    )


def solution(mesh):
    return jax.shard_map(
        on_device,
        mesh=mesh,
        in_specs=(
            P("wide", "narrow", None),
            P("wide", "narrow"),
            P("wide", "narrow"),
            P(("wide", "narrow")),
            P(("wide", "narrow"), None),
            P(("wide", "narrow")),
            P(("wide", "narrow"), None),
            P(("wide", "narrow")),
            P(("wide", "narrow"), None),
            P(("wide", "narrow")),
            P(("wide", "narrow"), None),
            P(("wide", "narrow")),
            P("wide", "narrow"),
            P("wide", "narrow"),
            P("narrow", "wide"),
            P("wide", "narrow", None),
        ),
        out_specs=(
            P("wide", "narrow", None),
            P("wide", "narrow", None),
            P(("wide", "narrow")),
            P(("wide", "narrow"), None),
            P(("wide", "narrow")),
            P(("wide", "narrow"), None),
            P(("wide", "narrow")),
            P(("wide", "narrow"), None),
            P(("wide", "narrow")),
            P(("wide", "narrow"), None),
            P(("wide", "narrow")),
            P("wide", "narrow"),
            P("wide", "narrow"),
            P("narrow", "wide"),
        ),
        check_vma=False,
    )
```

```python
import functools
import math

import jax
import jax.numpy as jnp
import numpy as np
from jax import lax
from jax.experimental import pallas as pl
from jax.experimental.pallas import tpu as pltpu
from jax.sharding import PartitionSpec as P

Q_HEADS = 12
KV_HEADS = 2
HEAD = 128
HQ = 1536
HK = 256


EPS = 1e-06
THETA = 10000.0


def norm_parts(value):
    factor = lax.rsqrt(jnp.mean(value * value, axis=-1, keepdims=True) + EPS)
    return (value * factor, factor)


def norm_back(grad, unit, factor, gain):
    scaled = grad * gain
    return factor * (scaled - unit * jnp.mean(scaled * unit, axis=-1, keepdims=True))


def rotate(value, cosine, sine):
    half = value.shape[-1] // 2
    first = value[..., :half]
    second = value[..., half:]
    return jnp.concatenate(
        [first * cosine - second * sine, second * cosine + first * sine], axis=-1
    )


def angles(places, head_size):
    freq = jnp.exp(
        jnp.arange(head_size // 2, dtype=jnp.float32) * (-2.0 * math.log(THETA) / head_size)
    )
    turn = places.astype(jnp.float32)[..., None] * freq
    return (jnp.cos(turn), jnp.sin(turn))


def row_probs(query, keys, allowed, scale):
    scores = jnp.einsum("qhgd,khd->hgqk", query, keys, preferred_element_type=jnp.float32) * scale
    scores = jnp.where(allowed[None, None], scores, -1e30)
    top = jnp.max(scores, axis=-1, keepdims=True)
    expo = jnp.exp(scores - top)
    return expo / jnp.sum(expo, axis=-1, keepdims=True)


def swiglu_back(d_hidden, gate, up):
    sigma = jax.nn.sigmoid(gate)
    active = gate * sigma
    d_gate = (d_hidden * up * sigma * (1.0 + gate * (1.0 - sigma))).astype(jnp.bfloat16)
    d_up = (d_hidden * active).astype(jnp.bfloat16)
    return (d_gate, d_up)


def plain_device(
    layer_in,
    seg_ids,
    pad_mask,
    gain_attn,
    w_query,
    b_query,
    w_key,
    b_key,
    w_value,
    b_value,
    w_out,
    gain_mlp,
    w_gate,
    w_up,
    w_down,
    grad_out,
):
    rows, seg_len, width = layer_in.shape
    parts = lax.axis_size("narrow")
    row_len = seg_len * parts
    me = lax.axis_index("narrow")
    group = Q_HEADS // KV_HEADS
    scale = 1.0 / math.sqrt(HEAD)
    f32 = jnp.float32
    bf16 = jnp.bfloat16
    ids_all, pads_all = (
        lax.all_gather(seg_ids, "narrow", axis=1, tiled=True),
        lax.all_gather(pad_mask, "narrow", axis=1, tiled=True),
    )
    wq, wk, wv, wo, g_one, g_two, bq, bk, bv = (
        lax.all_gather(w_query, ("wide", "narrow"), axis=0, tiled=True),
        lax.all_gather(w_key, ("wide", "narrow"), axis=0, tiled=True),
        lax.all_gather(w_value, ("wide", "narrow"), axis=0, tiled=True),
        lax.all_gather(w_out, ("wide", "narrow"), axis=0, tiled=True),
        lax.all_gather(gain_attn, ("wide", "narrow"), axis=0, tiled=True),
        lax.all_gather(gain_mlp, ("wide", "narrow"), axis=0, tiled=True),
        lax.all_gather(b_query, ("wide", "narrow"), axis=0, tiled=True),
        lax.all_gather(b_key, ("wide", "narrow"), axis=0, tiled=True),
        lax.all_gather(b_value, ("wide", "narrow"), axis=0, tiled=True),
    )
    wg, wu, wd = (
        lax.all_gather(w_gate, "wide", axis=0, tiled=True),
        lax.all_gather(w_up, "wide", axis=0, tiled=True),
        lax.all_gather(w_down, "wide", axis=1, tiled=True),
    )
    g_one = g_one.astype(f32)
    g_two = g_two.astype(f32)
    global_idx = me * seg_len + jnp.arange(seg_len, dtype=jnp.int32)
    begins = jnp.sum((ids_all[:, None, :] < seg_ids[:, :, None]).astype(jnp.int32), axis=-1)
    cosine, sine = angles(global_idx[None, :] - begins, HEAD)
    cosine = cosine[:, :, None, :]
    sine = sine[:, :, None, :]
    key_idx = jnp.arange(row_len, dtype=jnp.int32)
    allowed = (ids_all[:, None, :] == seg_ids[:, :, None]) & (
        key_idx[None, None, :] < global_idx[None, :, None]
    ) & (pads_all[:, None, :] == 1) | (key_idx[None, None, :] == global_idx[None, :, None])
    x_in = layer_in.astype(f32)
    unit_one, factor_one = norm_parts(x_in)
    h_one = (unit_one * g_one).astype(bf16)
    q_lin = jnp.dot(h_one, wq, preferred_element_type=f32) + bq.astype(f32)
    k_lin = jnp.dot(h_one, wk, preferred_element_type=f32) + bk.astype(f32)
    v_lin = jnp.dot(h_one, wv, preferred_element_type=f32) + bv.astype(f32)
    q_rot = rotate(q_lin.reshape(rows, seg_len, Q_HEADS, HEAD), cosine, sine).astype(bf16)
    k_rot = rotate(k_lin.reshape(rows, seg_len, KV_HEADS, HEAD), cosine, sine).astype(bf16)
    v_low = v_lin.astype(bf16)
    keys_all, values_all = (
        lax.all_gather(k_rot.reshape(rows, seg_len, HK), "narrow", axis=1, tiled=True),
        lax.all_gather(v_low, "narrow", axis=1, tiled=True),
    )
    keys_all = keys_all.reshape(rows, row_len, KV_HEADS, HEAD)
    values_all = values_all.reshape(rows, row_len, KV_HEADS, HEAD)
    queries = q_rot.reshape(rows, seg_len, KV_HEADS, group, HEAD)
    outputs = []
    for row in range(rows):
        probs = row_probs(queries[row], keys_all[row], allowed[row], scale)
        outputs.append(
            jnp.einsum(
                "hgqk,khd->qhgd", probs.astype(bf16), values_all[row], preferred_element_type=f32
            )
        )
    attended = jnp.stack(outputs).reshape(rows, seg_len, HQ).astype(bf16)
    x_mid = x_in + jnp.dot(attended, wo, preferred_element_type=f32)
    unit_two, factor_two = norm_parts(x_mid)
    h_two = (unit_two * g_two).astype(bf16)
    h_all = lax.all_gather(h_two, "narrow", axis=1, tiled=True)
    gate = jnp.dot(h_all, wg, preferred_element_type=f32)
    up = jnp.dot(h_all, wu, preferred_element_type=f32)
    hidden = (jax.nn.silu(gate) * up).astype(bf16)
    partial_value = jnp.dot(hidden, wd, preferred_element_type=f32)
    mixed = lax.psum_scatter(partial_value, "narrow", scatter_dimension=1, tiled=True)
    layer_out = (x_mid + mixed).astype(bf16)
    grad_all = lax.all_gather(grad_out, "narrow", axis=1, tiled=True)
    d_hidden = jnp.einsum("rtd,fd->rtf", grad_all, wd, preferred_element_type=f32)
    d_wd = jnp.einsum("rtf,rtd->fd", hidden, grad_all, preferred_element_type=f32)
    d_gate, d_up = swiglu_back(d_hidden, gate, up)
    d_wg = jnp.einsum("rtd,rtf->df", h_all, d_gate, preferred_element_type=f32)
    d_wu = jnp.einsum("rtd,rtf->df", h_all, d_up, preferred_element_type=f32)
    grad_w_gate, grad_w_up, grad_w_down = (
        lax.psum_scatter(d_wg, "wide", scatter_dimension=0, tiled=True),
        lax.psum_scatter(d_wu, "wide", scatter_dimension=0, tiled=True),
        lax.psum_scatter(d_wd, "wide", scatter_dimension=1, tiled=True),
    )
    d_h_part = jnp.einsum("rtf,df->rtd", d_gate, wg, preferred_element_type=f32) + jnp.einsum(
        "rtf,df->rtd", d_up, wu, preferred_element_type=f32
    )
    d_h_two = lax.psum_scatter(d_h_part, "narrow", scatter_dimension=1, tiled=True)
    d_g_two = jnp.sum(d_h_two * unit_two, axis=(0, 1))
    d_mid = grad_out.astype(f32) + norm_back(d_h_two, unit_two, factor_two, g_two)
    d_branch = d_mid.astype(bf16)
    d_wo = jnp.einsum("rsh,rsd->hd", attended, d_branch, preferred_element_type=f32)
    d_attended = jnp.einsum("rsd,hd->rsh", d_branch, wo, preferred_element_type=f32).astype(bf16)
    d_att_heads = d_attended.reshape(rows, seg_len, KV_HEADS, group, HEAD)
    query_grads = []
    key_grads = []
    value_grads = []
    for row in range(rows):
        probs = row_probs(queries[row], keys_all[row], allowed[row], scale)
        d_prob = jnp.einsum(
            "qhgd,khd->hgqk", d_att_heads[row], values_all[row], preferred_element_type=f32
        )
        delta = jnp.sum(probs * d_prob, axis=-1, keepdims=True)
        d_score = (scale * probs * (d_prob - delta)).astype(bf16)
        query_grads.append(
            jnp.einsum("hgqk,khd->qhgd", d_score, keys_all[row], preferred_element_type=f32)
        )
        key_grads.append(
            jnp.einsum("hgqk,qhgd->khd", d_score, queries[row], preferred_element_type=f32)
        )
        value_grads.append(
            jnp.einsum(
                "hgqk,qhgd->khd", probs.astype(bf16), d_att_heads[row], preferred_element_type=f32
            )
        )
    d_query = jnp.stack(query_grads).reshape(rows, seg_len, Q_HEADS, HEAD)
    d_keys_all = jnp.stack(key_grads).reshape(rows, row_len, HK)
    d_values_all = jnp.stack(value_grads).reshape(rows, row_len, HK)
    d_keys, d_values = (
        lax.psum_scatter(d_keys_all, "narrow", scatter_dimension=1, tiled=True),
        lax.psum_scatter(d_values_all, "narrow", scatter_dimension=1, tiled=True),
    )
    dq_lin = rotate(d_query, cosine, -sine).reshape(rows, seg_len, HQ).astype(bf16)
    dk_lin = (
        rotate(d_keys.reshape(rows, seg_len, KV_HEADS, HEAD), cosine, -sine)
        .reshape(rows, seg_len, HK)
        .astype(bf16)
    )
    dv_lin = d_values.astype(bf16)
    d_wq = jnp.einsum("rsd,rsh->dh", h_one, dq_lin, preferred_element_type=f32)
    d_wk = jnp.einsum("rsd,rsh->dh", h_one, dk_lin, preferred_element_type=f32)
    d_wv = jnp.einsum("rsd,rsh->dh", h_one, dv_lin, preferred_element_type=f32)
    d_bq = jnp.sum(dq_lin.astype(f32), axis=(0, 1))
    d_bk = jnp.sum(dk_lin.astype(f32), axis=(0, 1))
    d_bv = jnp.sum(dv_lin.astype(f32), axis=(0, 1))
    d_h_one = jnp.einsum("rsh,dh->rsd", dq_lin, wq, preferred_element_type=f32)
    d_h_one = d_h_one + jnp.einsum("rsh,dh->rsd", dk_lin, wk, preferred_element_type=f32)
    d_h_one = d_h_one + jnp.einsum("rsh,dh->rsd", dv_lin, wv, preferred_element_type=f32)
    d_g_one = jnp.sum(d_h_one * unit_one, axis=(0, 1))
    grad_in = (d_mid + norm_back(d_h_one, unit_one, factor_one, g_one)).astype(bf16)
    (
        grad_w_query,
        grad_w_key,
        grad_w_value,
        grad_w_out,
        grad_gain_attn,
        grad_gain_mlp,
        grad_b_query,
        grad_b_key,
        grad_b_value,
    ) = (
        lax.psum_scatter(d_wq, ("wide", "narrow"), scatter_dimension=0, tiled=True),
        lax.psum_scatter(d_wk, ("wide", "narrow"), scatter_dimension=0, tiled=True),
        lax.psum_scatter(d_wv, ("wide", "narrow"), scatter_dimension=0, tiled=True),
        lax.psum_scatter(d_wo, ("wide", "narrow"), scatter_dimension=0, tiled=True),
        lax.psum_scatter(d_g_one, ("wide", "narrow"), scatter_dimension=0, tiled=True),
        lax.psum_scatter(d_g_two, ("wide", "narrow"), scatter_dimension=0, tiled=True),
        lax.psum_scatter(d_bq, ("wide", "narrow"), scatter_dimension=0, tiled=True),
        lax.psum_scatter(d_bk, ("wide", "narrow"), scatter_dimension=0, tiled=True),
        lax.psum_scatter(d_bv, ("wide", "narrow"), scatter_dimension=0, tiled=True),
    )
    return (
        layer_out,
        grad_in,
        grad_gain_attn,
        grad_w_query,
        grad_b_query,
        grad_w_key,
        grad_b_key,
        grad_w_value,
        grad_b_value,
        grad_w_out,
        grad_gain_mlp,
        grad_w_gate,
        grad_w_up,
        grad_w_down,
    )


F32 = jnp.float32
BF16 = jnp.bfloat16
VMEM_BYTES = 58 * 1024 * 1024
ROWS = 2
PARTS = 8
WIDE = 4
SEG = 128
SHARE = 48
GROUP = Q_HEADS // KV_HEADS
SCALE = 1.0 / math.sqrt(HEAD)
TOKENS = ROWS * SEG
ROW_LEN = SEG * PARTS
KV_BLOCK = SHARE + 16
TILE = 512


def dot_nn(left, right):
    return lax.dot_general(left, right, (((1,), (0,)), ((), ())), preferred_element_type=F32)


def dot_nt(left, right):
    return lax.dot_general(left, right, (((1,), (1,)), ((), ())), preferred_element_type=F32)


def flipped(value):
    return value.astype(F32).T.astype(BF16)


class Links:
    def __init__(self):
        self.orders = ((2, 4, 1), (4, 2, 1))

    def hop(self, value, bit):
        return lax.ppermute(value, "narrow", [(i, i ^ bit) for i in range(PARTS)])

    def offsets(self, which):
        found = [0]
        for bit in self.orders[which]:
            found = found + [o ^ bit for o in found]
        return found

    def near(self, value, which):
        return jnp.concatenate([value, self.hop(value, self.orders[which][0])], axis=0)

    def rest(self, near, which):
        _, second, core = self.orders[which]
        far = self.hop(near, second)
        return [near, far, self.hop(near, core), self.hop(far, core)]

    def gather(self, value, which):
        return self.rest(self.near(value, which), which)

    def scatter_core(self, own, other):
        return own + self.hop(other, 1)

    def scatter_second(self, held, which):
        half = held.shape[0] // 2
        return held[:half] + self.hop(held[half:], self.orders[which][1])

    def scatter_first(self, held, which):
        half = held.shape[0] // 2
        return held[:half], self.hop(held[half:], self.orders[which][0])

    def scatter(self, own, other, which):
        held = self.scatter_second(self.scatter_core(own, other), which)
        return self.scatter_first(held, which)

    def over_wide(self, value, step):
        return lax.ppermute(value, "wide", [(i, (i + step) % WIDE) for i in range(WIDE)])

    def direct_gather(self, value):
        return [value] + [self.over_wide(value, k) for k in range(1, WIDE)]

    def direct_scatter(self, near, far):
        slots = (near + far).reshape((WIDE, near.shape[0] // WIDE) + near.shape[1:])
        total = slots[0].astype(F32)
        for k in range(1, WIDE):
            total = total + self.over_wide(slots[k], -k).astype(F32)
        return total


def after(values, *earlier):
    return lax.optimization_barrier((values, earlier))[0]


def in_vmem(count):
    return [pl.BlockSpec(memory_space=pltpu.VMEM)] * count


def in_smem(count):
    return [pl.BlockSpec(memory_space=pltpu.SMEM)] * count


def anywhere(count):
    return [pl.BlockSpec(memory_space=pl.ANY)] * count


def call(body, outs, scratch, in_specs, out_specs, flops, nbytes, grid=None, name=None):
    return pl.pallas_call(
        body,
        out_shape=outs,
        grid=grid if grid is not None else (),
        in_specs=in_specs,
        out_specs=out_specs,
        scratch_shapes=scratch,
        name=name,
        compiler_params=pltpu.CompilerParams(vmem_limit_bytes=VMEM_BYTES),
        cost_estimate=pl.CostEstimate(flops=int(flops) // 10, bytes_accessed=int(nbytes) // 10, transcendentals=0),
    )


def shaped(*dims, dtype=BF16):
    return jax.ShapeDtypeStruct(dims, dtype)


def weight_copies(pieces, held, starts, sems, stride, columns):
    copies = []
    for i in range(PARTS * WIDE):
        piece = pieces[i // 8]
        copies.append(
            pltpu.make_async_copy(
                piece.at[pl.ds((i % 8) * stride, SHARE), :],
                held.at[pl.ds(pl.multiple_of(starts[i], 16), SHARE), columns],
                sems.at[i],
            )
        )
    return copies


def grad_copies(held, own, other, starts, sems, stride, columns):
    copies = []
    for i in range(PARTS * WIDE):
        target = own if i < 16 else other
        copies.append(
            pltpu.make_async_copy(
                held.at[pl.ds(pl.multiple_of(starts[i], 16), SHARE), columns],
                target.at[pl.ds((i % 16) * stride, SHARE), :],
                sems.at[i],
            )
        )
    return copies


def half_copies(pieces, held, starts_a, starts_b, sems):
    half = held.shape[1] // 2
    return weight_copies(
        pieces[:4], held, starts_a, sems.at[0], SHARE, slice(0, half)
    ) + weight_copies(pieces[4:], held, starts_b, sems.at[1], SHARE, slice(half, 2 * half))


def half_grad_copies(held, outs, starts_a, starts_b, sems):
    half = held.shape[1] // 2
    return grad_copies(
        held, outs[0], outs[1], starts_a, sems.at[0], SHARE, slice(0, half)
    ) + grad_copies(held, outs[2], outs[3], starts_b, sems.at[1], SHARE, slice(half, 2 * half))


def vector_masks(start_column, lanes, block):
    at = lax.broadcasted_iota(jnp.int32, (PARTS * WIDE, lanes), 1)
    return (at >= start_column) & (at < start_column + block)


def turn(value, cosine, sine):
    return value * cosine + pltpu.roll(value, HEAD // 2, 1) * sine


def project_kv(starts, x, cosine, sine, begin, begin_small, pick, pick_k, pick_v, *refs):
    pieces, (kv_out, h_out, vec_out, held, vecs, sems, vec_sems) = refs[:4], refs[4:]
    copies = weight_copies(pieces, held, starts, sems, KV_BLOCK, slice(None))
    for i in range(PARTS * WIDE):
        copies.append(
            pltpu.make_async_copy(
                pieces[i // 8].at[pl.ds((i % 8) * KV_BLOCK + SHARE, 16), :],
                vecs.at[pl.ds(16 * i, 16), :],
                vec_sems.at[i],
            )
        )
    for copy in copies:
        copy.start()
    value = x[...].astype(F32)
    unit = value * lax.rsqrt(jnp.mean(value * value, axis=-1, keepdims=True) + EPS)
    for copy in copies:
        copy.wait()
    row = lax.broadcasted_iota(jnp.int32, (32, 512), 0) * 16
    col = lax.broadcasted_iota(jnp.int32, (32, 512), 1)
    packed = dot_nn((row == col).astype(BF16), vecs[...]).astype(BF16)
    mask = vector_masks(begin[...], HQ, SHARE)
    mask_small = vector_masks(begin_small[...], HK, 8)

    def spread(lane, chosen, where):
        found = dot_nn(packed[:, lane : lane + 128], chosen[...])
        return jnp.sum(jnp.where(where, found, 0.0), axis=0, keepdims=True)

    g_one = spread(0, pick, mask)
    vec_out[...] = jnp.concatenate(
        [g_one, spread(128, pick, mask), spread(256, pick, mask), jnp.zeros((5, HQ), F32)], axis=0
    )
    b_key = spread(384, pick_k, mask_small)
    b_value = spread(384, pick_v, mask_small)
    h_one = (unit * g_one).astype(BF16)
    h_out[...] = h_one
    lin = dot_nn(h_one, held[...])
    for head in range(KV_HEADS):
        cut = slice(head * HEAD, (head + 1) * HEAD)
        key = turn(lin[:, cut] + b_key[:, cut], cosine[...], sine[...])
        kv_out[:, cut] = key.astype(BF16)
    kv_out[:, HK:] = (lin[:, HK:] + b_value).astype(BF16)


def project_q(starts_a, starts_b, h_one, vec, cosine, sine, *refs):
    pieces, (q_out, held, sems) = refs[:8], refs[8:]
    copies = half_copies(pieces, held, starts_a, starts_b, sems)
    for copy in copies:
        copy.start()
    for copy in copies:
        copy.wait()
    lin = dot_nn(h_one[...], held[...]) + vec[2:3, :]
    for head in range(Q_HEADS):
        cut = slice(head * HEAD, (head + 1) * HEAD)
        q_out[:, cut] = turn(lin[:, cut], cosine[...], sine[...]).astype(BF16)


def stacked(ref, row, kv_head):
    first = kv_head * GROUP
    return jnp.concatenate(
        [
            ref[row * SEG : (row + 1) * SEG, (first + g) * HEAD : (first + g + 1) * HEAD]
            for g in range(GROUP)
        ],
        axis=0,
    )


def row_keys(pieces, row, column):
    return jnp.concatenate(
        [piece[:, column : column + HEAD] for piece in pieces[4 * row : 4 * row + 4]], axis=0
    )


def attend(starts_a, starts_b, q, x, vec, barred, *refs):
    kv, pieces = refs[:8], refs[8:16]
    att_out, lse_out, mid_out, h_out, held, sems = refs[16:]
    copies = half_copies(pieces, held, starts_a, starts_b, sems)
    for copy in copies:
        copy.start()
    for row in range(ROWS):
        bar = barred[row]
        bar = jnp.concatenate([bar] * GROUP, axis=1)
        for kv_head in range(KV_HEADS):
            keys = row_keys(kv, row, kv_head * HEAD)
            values = row_keys(kv, row, HK + kv_head * HEAD)
            scores = dot_nt(keys, stacked(q, row, kv_head)) * SCALE + bar
            top = jnp.max(scores, axis=0, keepdims=True)
            expo = jnp.exp(scores - top)
            total = jnp.sum(expo, axis=0, keepdims=True)
            lse_out[row * KV_HEADS + kv_head] = top + jnp.log(total)
            probs = (expo / total).astype(BF16)
            out = dot_nn(flipped(values), probs)
            for g in range(GROUP):
                head = kv_head * GROUP + g
                att_out[row * SEG : (row + 1) * SEG, head * HEAD : (head + 1) * HEAD] = (
                    out[:, g * SEG : (g + 1) * SEG].T.astype(BF16)
                )
    for copy in copies:
        copy.wait()
    mid = x[...].astype(F32) + dot_nn(att_out[...], held[...])
    mid_out[...] = mid
    factor = lax.rsqrt(jnp.mean(mid * mid, axis=-1, keepdims=True) + EPS)
    h_out[...] = (mid * factor * vec[1:2, :]).astype(BF16)


def mlp_front(*refs):
    h_pieces, wg, wu = refs[:8], refs[8], refs[9]
    hid_out, hid_t_out, gate_out, up_out, h_all = refs[10:15]
    h_v, w_v, sems, w_sems, out_sems = refs[15:]
    step = pl.program_id(0)
    rows = h_pieces[0].shape[0]
    units = hid_out.shape[1]
    second = w_v.shape[0] // 2

    def pieces_in():
        return [
            pltpu.make_async_copy(h_pieces[i], h_v.at[pl.ds(i * rows, rows), :], sems.at[i])
            for i in range(8)
        ]

    def weights_in():
        return [
            pltpu.make_async_copy(wg, w_v.at[pl.ds(0, units), :], w_sems.at[0]),
            pltpu.make_async_copy(wu, w_v.at[pl.ds(second, units), :], w_sems.at[1]),
        ]

    def h_over(tile):
        at = pl.ds(pl.multiple_of(tile * TILE, TILE), TILE)
        return pltpu.make_async_copy(h_v.at[at, :], h_all.at[at, :], out_sems.at[tile])

    @pl.when(step == 0)
    def _():
        held = pieces_in()
        for copy in held[:2] + weights_in() + held[2:]:
            copy.start()
        gap = jnp.zeros((second - units, w_v.shape[1]), BF16)
        w_v[units:second, :] = gap
        w_v[second + units :, :] = gap

    for tile in range(4):

        @pl.when(step == tile)
        def _(tile=tile):
            for copy in pieces_in()[2 * tile : 2 * tile + 2]:
                copy.wait()
            h_over(tile).start()

    @pl.when(step == 0)
    def _():
        for copy in weights_in():
            copy.wait()

    h = h_v[pl.ds(pl.multiple_of(step * TILE, TILE), TILE), :]
    both = dot_nt(h, w_v[...])
    gate = both[:, :units]
    up = both[:, second : second + units]
    gate_out[...] = gate.astype(BF16)
    up_out[...] = up.astype(BF16)
    hidden = (gate * jax.nn.sigmoid(gate) * up).astype(BF16)
    hid_out[...] = hidden
    hid_t_out[...] = hidden.T

    @pl.when(step == 3)
    def _():
        for tile in range(4):
            h_over(tile).wait()


def mlp_back(grad, gate_in, up_in, wd, wg, wu, *refs):
    dg_out, du_out, own_h, other_h, wd_v, w_v, d_v, sems = refs
    step = pl.program_id(0)
    units = gate_in.shape[1]
    second = w_v.shape[0] // 2

    def down_in():
        return [pltpu.make_async_copy(wd, wd_v, sems.at[0])]

    def weights_in():
        return [
            pltpu.make_async_copy(wg, w_v.at[pl.ds(0, units), :], sems.at[1]),
            pltpu.make_async_copy(wu, w_v.at[pl.ds(second, units), :], sems.at[2]),
        ]

    @pl.when(step == 0)
    def _():
        for copy in down_in() + weights_in():
            copy.start()
        gap = jnp.zeros((second - units, w_v.shape[1]), BF16)
        w_v[units:second, :] = gap
        w_v[second + units :, :] = gap
        gap = jnp.zeros((TILE, second - units), BF16)
        d_v[:, units:second] = gap
        d_v[:, second + units :] = gap
        for copy in down_in():
            copy.wait()

    d_hidden = dot_nt(grad[...], wd_v[...])
    gate = gate_in[...].astype(F32)
    up = up_in[...].astype(F32)
    sigma = jax.nn.sigmoid(gate)
    d_gate = (d_hidden * up * sigma * (1.0 + gate * (1.0 - sigma))).astype(BF16)
    d_up = (d_hidden * (gate * sigma)).astype(BF16)
    dg_out[...] = d_gate.T
    du_out[...] = d_up.T
    d_v[:, :units] = d_gate
    d_v[:, second : second + units] = d_up

    @pl.when(step == 0)
    def _():
        for copy in weights_in():
            copy.wait()

    d_h = dot_nn(d_v[...], w_v[...]).astype(BF16)

    @pl.when(step % 2 == 0)
    def _():
        own_h[...] = d_h

    @pl.when(step % 2 == 1)
    def _():
        other_h[...] = d_h


def mlp_down(hid, wd, own_m, other_m):
    step = pl.program_id(0)
    mixed = dot_nn(hid[...], wd[...]).astype(BF16)

    @pl.when(step % 2 == 0)
    def _():
        own_m[...] = mixed

    @pl.when(step % 2 == 1)
    def _():
        other_m[...] = mixed


def weight_grad(left, right, out):
    found = dot_nn(left[...], right[...]).astype(BF16)
    cut = out.shape[2]
    out[0] = found[:, :cut]
    out[1] = found[:, cut:]


def branch_back(starts_a, starts_b, keep_a, got_a, keep_b, got_b, mid, grad, vec, att, *refs):
    pieces, (d_mid_out, d_att_out, d_gain_out), outs = refs[:8], refs[8:11], refs[11:15]
    held, held_d, sems, out_sems = refs[15:]
    copies = half_copies(pieces, held, starts_a, starts_b, sems)
    for copy in copies:
        copy.start()
    d_h = jnp.concatenate(
        [
            keep_a[...].astype(F32) + got_a[...].astype(F32),
            keep_b[...].astype(F32) + got_b[...].astype(F32),
        ],
        axis=0,
    )
    x_mid = mid[...]
    factor = lax.rsqrt(jnp.mean(x_mid * x_mid, axis=-1, keepdims=True) + EPS)
    unit = x_mid * factor
    d_gain_out[...] = jnp.sum(d_h * unit, axis=0, keepdims=True)
    d_mid = grad[...].astype(F32) + norm_back(d_h, unit, factor, vec[1:2, :])
    d_mid_out[...] = d_mid
    d_branch = d_mid.astype(BF16)
    held_d[...] = dot_nn(flipped(att[...]), d_branch).astype(BF16)
    out_copies = half_grad_copies(held_d, outs, starts_a, starts_b, out_sems)
    for copy in out_copies:
        copy.start()
    for copy in copies:
        copy.wait()
    d_att_out[...] = dot_nt(d_branch, held[...]).astype(BF16)
    for copy in out_copies:
        copy.wait()


def attend_back(q, d_att, cosine, sine, barred, lse, *refs):
    kv, (dq_out, own, other) = refs[:8], refs[8:]
    for row in range(ROWS):
        bar = barred[row]
        bar = jnp.concatenate([bar] * GROUP, axis=1)
        for kv_head in range(KV_HEADS):
            keys = row_keys(kv, row, kv_head * HEAD)
            values = row_keys(kv, row, HK + kv_head * HEAD)
            queries = stacked(q, row, kv_head)
            d_out = stacked(d_att, row, kv_head)
            scores = dot_nt(keys, queries) * SCALE + bar
            probs = jnp.exp(scores - lse[row * KV_HEADS + kv_head])
            d_prob = dot_nt(values, d_out)
            delta = jnp.sum(probs * d_prob, axis=0, keepdims=True)
            d_score = (SCALE * probs * (d_prob - delta)).astype(BF16)
            d_value = dot_nn(probs.astype(BF16), d_out).astype(BF16)
            d_key = dot_nn(d_score, queries).astype(BF16)
            half = ROW_LEN // 2
            cut = slice(kv_head * HEAD, (kv_head + 1) * HEAD)
            cut_v = slice(HK + kv_head * HEAD, HK + (kv_head + 1) * HEAD)
            own[row, :, cut] = d_key[:half]
            other[row, :, cut] = d_key[half:]
            own[row, :, cut_v] = d_value[:half]
            other[row, :, cut_v] = d_value[half:]
            d_query = dot_nn(flipped(keys), d_score)
            at = slice(row * SEG, (row + 1) * SEG)
            for g in range(GROUP):
                head = kv_head * GROUP + g
                back = turn(d_query[:, g * SEG : (g + 1) * SEG].T, cosine[at, :], -sine[at, :])
                dq_out[at, head * HEAD : (head + 1) * HEAD] = back.astype(BF16)


def query_back(starts_a, starts_b, dq, h_one, *refs):
    pieces, (d_h_out, d_bias_out), outs = refs[:8], refs[8:10], refs[10:14]
    held, held_d, sems, out_sems = refs[14:]
    copies = half_copies(pieces, held, starts_a, starts_b, sems)
    for copy in copies:
        copy.start()
    held_d[...] = dot_nn(flipped(h_one[...]), dq[...]).astype(BF16)
    out_copies = half_grad_copies(held_d, outs, starts_a, starts_b, out_sems)
    for copy in out_copies:
        copy.start()
    d_bias_out[...] = jnp.sum(dq[...].astype(F32), axis=0, keepdims=True)
    for copy in copies:
        copy.wait()
    d_h_out[...] = dot_nt(dq[...], held[...])
    for copy in out_copies:
        copy.wait()


def kv_back(
    starts, keep_a, got_a, keep_b, got_b, x, h_one, vec, cosine, sine, d_h_q, d_mid, d_gain, d_bias,
    begin, begin_small, pick, pick_k, pick_v, *refs,
):
    pieces, (grad_out, own, other, held, held_d, vecs, sems, out_sems, vec_sems) = refs[:4], refs[4:]
    copies = weight_copies(pieces, held, starts, sems, KV_BLOCK, slice(None))
    for copy in copies:
        copy.start()
    d_kv = jnp.concatenate(
        [
            keep_a[...].astype(F32) + got_a[...].astype(F32),
            keep_b[...].astype(F32) + got_b[...].astype(F32),
        ],
        axis=0,
    )
    parts = [
        turn(d_kv[:, head * HEAD : (head + 1) * HEAD], cosine[...], -sine[...])
        for head in range(KV_HEADS)
    ]
    d_lin = jnp.concatenate(parts + [d_kv[:, HK:]], axis=1).astype(BF16)
    held_d[...] = dot_nn(flipped(h_one[...]), d_lin).astype(BF16)
    out_copies = grad_copies(held_d, own, other, starts, out_sems, KV_BLOCK, slice(None))
    for copy in out_copies:
        copy.start()
    for copy in copies:
        copy.wait()
    d_h = d_h_q[...] + dot_nt(d_lin, held[...])
    value = x[...].astype(F32)
    factor = lax.rsqrt(jnp.mean(value * value, axis=-1, keepdims=True) + EPS)
    unit = value * factor
    d_small = jnp.sum(d_lin.astype(F32), axis=0, keepdims=True)
    mask = vector_masks(begin[...], HQ, SHARE)
    mask_small = vector_masks(begin_small[...], HK, 8)

    def collect(row, chosen, where):
        return dot_nt(jnp.where(where, row, 0.0).astype(BF16), chosen[...])

    packed = jnp.concatenate(
        [
            collect(jnp.sum(d_h * unit, axis=0, keepdims=True), pick, mask),
            collect(d_gain[...], pick, mask),
            collect(d_bias[...], pick, mask),
            collect(d_small[:, :HK], pick_k, mask_small) + collect(d_small[:, HK:], pick_v, mask_small),
        ],
        axis=1,
    ).astype(BF16)
    row = lax.broadcasted_iota(jnp.int32, (512, 32), 0)
    col = lax.broadcasted_iota(jnp.int32, (512, 32), 1) * 16
    vecs[...] = dot_nn((row == col).astype(BF16), packed).astype(BF16)
    vec_copies = [
        pltpu.make_async_copy(
            vecs.at[pl.ds(16 * i, 16), :],
            (own if i < 16 else other).at[pl.ds((i % 16) * KV_BLOCK + SHARE, 16), :],
            vec_sems.at[i],
        )
        for i in range(PARTS * WIDE)
    ]
    for copy in vec_copies:
        copy.start()
    grad_out[...] = (d_mid[...] + norm_back(d_h, unit, factor, vec[0:1, :])).astype(BF16)
    for copy in out_copies + vec_copies:
        copy.wait()


def fast_device(
    layer_in,
    seg_ids,
    pad_mask,
    gain_attn,
    w_query,
    b_query,
    w_key,
    b_key,
    w_value,
    b_value,
    w_out,
    gain_mlp,
    w_gate,
    w_up,
    w_down,
    grad_out,
):
    width = layer_in.shape[2]
    units = w_gate.shape[1]
    links = Links()
    here = lax.axis_index("wide")
    me = lax.axis_index("narrow")
    dma = pltpu.SemaphoreType.DMA
    order = [0, 1]
    x = layer_in.reshape(TOKENS, width)
    grad = grad_out.reshape(TOKENS, width)

    slots = (here - jnp.arange(WIDE, dtype=jnp.int32)) % WIDE * PARTS
    blocks = [
        ((me ^ jnp.array(links.offsets(o), jnp.int32))[:, None] + slots[None, :]).reshape(-1)
        for o in order
    ]
    starts = [b * SHARE for b in blocks]
    begin = starts[0][:, None]
    begin_small = (blocks[0] * 8)[:, None]
    lanes = np.arange(HQ)
    pick = jnp.asarray((np.arange(128)[:, None] == lanes % SHARE).astype(np.float32), BF16)
    pick_k = jnp.asarray((np.arange(128)[:, None] == lanes[:HK] % 8).astype(np.float32), BF16)
    pick_v = jnp.asarray((np.arange(128)[:, None] == lanes[:HK] % 8 + 8).astype(np.float32), BF16)

    def lane_pad(value, size):
        return jnp.pad(value, (0, size - value.shape[0]))

    packed = jnp.concatenate(
        [
            lane_pad(gain_attn, 128),
            lane_pad(gain_mlp, 128),
            lane_pad(b_query, 128),
            lane_pad(jnp.concatenate([b_key, b_value]), 128),
        ]
    )[None]
    kv_own = jnp.concatenate(
        [jnp.concatenate([w_key, w_value], axis=1), jnp.pad(packed, ((0, 15), (0, 0)))], axis=0
    )
    half = HQ // 2

    def two_halves(found):
        return [
            jnp.concatenate([s[:, :half] for s in found], axis=0),
            jnp.concatenate([s[:, half:] for s in found], axis=0),
        ]

    kv_slots = jnp.concatenate(links.direct_gather(kv_own), axis=0)
    q_slots = two_halves(links.direct_gather(w_query))
    w_out, w_gate, w_up, w_down = after((w_out, w_gate, w_up, w_down), *q_slots)
    o_slots = two_halves(links.direct_gather(w_out))
    wg = lax.all_gather(w_gate.T, "wide", axis=1, tiled=True)
    wu = lax.all_gather(w_up.T, "wide", axis=1, tiled=True)
    wd = lax.all_gather(w_down, "wide", axis=1, tiled=True)
    kv_weight = links.gather(kv_slots, 0)
    q_weight = links.gather(q_slots[0], 0) + links.gather(q_slots[1], 1)
    o_slots = after(o_slots, q_weight[1], q_weight[5])
    o_weight = links.gather(o_slots[0], 0) + links.gather(o_slots[1], 1)

    marks = jnp.stack(after((seg_ids, pad_mask), kv_slots), axis=1)
    marks = jnp.stack([jnp.concatenate(links.gather(marks[r][None], order[r]), axis=0) for r in range(ROWS)])
    ids_all = marks[:, :, 0].reshape(ROWS, ROW_LEN)
    pads_all = marks[:, :, 1].reshape(ROWS, ROW_LEN)
    sources = jnp.array([links.offsets(o) for o in order], jnp.int32) ^ me
    key_idx = (
        sources[:, :, None] * SEG + jnp.arange(SEG, dtype=jnp.int32)[None, None, :]
    ).reshape(ROWS, ROW_LEN)
    own_idx = me * SEG + jnp.arange(SEG, dtype=jnp.int32)
    begins = jnp.sum((ids_all[:, None, :] < seg_ids[:, :, None]).astype(jnp.int32), axis=-1)
    cosine, sine = angles((own_idx[None, :] - begins).reshape(TOKENS), HEAD)
    cosine = jnp.concatenate([cosine, cosine], axis=-1)
    sine = jnp.concatenate([-sine, sine], axis=-1)
    allowed = (ids_all[:, :, None] == seg_ids[:, None, :]) & (
        key_idx[:, :, None] < own_idx[None, None, :]
    ) & (pads_all[:, :, None] == 1) | (key_idx[:, :, None] == own_idx[None, None, :])
    barred = jnp.where(allowed, 0.0, -1e30).astype(F32)

    kv, h_one, vec = call(
        project_kv,
        [shaped(TOKENS, 2 * HK), shaped(TOKENS, width), shaped(8, width, dtype=F32)],
        [
            pltpu.VMEM((width, 2 * HK), BF16),
            pltpu.VMEM((512, 2 * HK), BF16),
            dma((32,)),
            dma((32,)),
        ],
        in_smem(1) + in_vmem(8) + anywhere(4),
        in_vmem(3),
        2 * TOKENS * width * 2 * HK,
        4e6,
        name="project_kv",
    )(starts[0], x, cosine, sine, begin, begin_small, pick, pick_k, pick_v, *kv_weight)
    kv_rows = []
    for r in range(ROWS):
        kv_rows += links.gather(kv[r * SEG : (r + 1) * SEG], order[r])
    q = call(
        project_q,
        shaped(TOKENS, HQ),
        [pltpu.VMEM((width, HQ), BF16), dma((2, 32))],
        in_smem(2) + in_vmem(4) + anywhere(8),
        pl.BlockSpec(memory_space=pltpu.VMEM),
        2 * TOKENS * width * HQ,
        7e6,
        name="project_q",
    )(starts[0], starts[1], h_one, vec, cosine, sine, *q_weight)
    attended, lse, x_mid, h_two = call(
        attend,
        [
            shaped(TOKENS, HQ),
            shaped(ROWS * KV_HEADS, 1, GROUP * SEG, dtype=F32),
            shaped(TOKENS, width, dtype=F32),
            shaped(TOKENS, width),
        ],
        [pltpu.VMEM((HQ, width), BF16), dma((2, 32))],
        in_smem(2) + in_vmem(4) + in_vmem(8) + anywhere(8),
        in_vmem(4),
        2 * TOKENS * width * HQ + 4 * TOKENS * ROW_LEN * HQ,
        1e7,
        name="attend",
    )(*starts, q, x, vec, barred, *kv_rows, *o_weight)

    at_row = [slice(r * SEG, (r + 1) * SEG) for r in range(ROWS)]
    grad_near = [links.near(after(grad[at_row[r]], *kv_rows), order[r]) for r in range(ROWS)]
    h_near = [links.near(h_two[at_row[r]], order[r]) for r in range(ROWS)]
    grad_near = after(grad_near, *h_near)
    h_pieces, grad_pieces = [], []
    for r in range(ROWS):
        h_pieces += links.rest(h_near[r], order[r])
        grad_pieces += links.rest(grad_near[r], order[r])
    many = ROWS * ROW_LEN
    cut = width // WIDE
    paired = 2 * -(-units // 128) * 128
    tile_f = pl.BlockSpec((TILE, units), lambda t: (t, 0))
    tile_t = pl.BlockSpec((units, TILE), lambda t: (0, t))
    hidden, hidden_t, gate, up, h_all = call(
        mlp_front,
        [shaped(many, units), shaped(units, many), shaped(many, units), shaped(many, units)]
        + [shaped(many, width)],
        [
            pltpu.VMEM((many, width), BF16),
            pltpu.VMEM((paired, width), BF16),
            dma((8,)),
            dma((2,)),
            dma((4,)),
        ],
        anywhere(10),
        [tile_f, tile_t, tile_f, tile_f] + anywhere(1),
        4 * many * width * units,
        4e7,
        grid=(many // TILE,),
        name="mlp_front",
    )(*h_pieces, wg, wu)
    grad_all = jnp.concatenate(grad_pieces, axis=0)

    def grad_of(left, right):
        out = call(
            weight_grad,
            shaped(WIDE, units, cut),
            [],
            [
                pl.BlockSpec((units, many), lambda k: (0, 0)),
                pl.BlockSpec((many, 2 * cut), lambda k: (0, k)),
            ],
            pl.BlockSpec((2, units, cut), lambda k: (k, 0, 0)),
            2 * many * width * units,
            1.4e7,
            grid=(WIDE // 2,),
            name="weight_grad",
        )(left, right)
        return out

    def sum_wide(slots):
        return lax.psum_scatter(slots, "wide", scatter_dimension=0, tiled=False).astype(F32)

    slots_d = grad_of(hidden_t, grad_all)
    grad_w_down = sum_wide(slots_d)
    tile_d = pl.BlockSpec((TILE, width), lambda t: (t, 0))
    half_d = pl.BlockSpec((TILE, width), lambda t: (t // 2, 0))
    d_gate, d_up, own_h, other_h = call(
        mlp_back,
        [shaped(units, many)] * 2 + [shaped(many // 2, width)] * 2,
        [
            pltpu.VMEM((units, width), BF16),
            pltpu.VMEM((paired, width), BF16),
            pltpu.VMEM((TILE, paired), BF16),
            dma((3,)),
        ],
        [tile_d, tile_f, tile_f] + anywhere(3),
        [tile_t, tile_t] + [half_d] * 2,
        6 * many * width * units,
        6e7,
        grid=(many // TILE,),
        name="mlp_back",
    )(after(grad_all, slots_d), gate, up, wd, wg, wu)

    def by_row(value):
        size = value.shape[0] // ROWS
        return [value[r * size : (r + 1) * size] for r in range(ROWS)]

    def core_rows(own, other):
        return by_row(links.scatter_core(own, other))

    def second_rows(held):
        return [links.scatter_second(held[r], order[r]) for r in range(ROWS)]

    def first_rows(held):
        found = []
        for r in range(ROWS):
            found += links.scatter_first(held[r], order[r])
        return found

    slots_g = grad_of(d_gate, h_all)
    grad_w_gate = sum_wide(slots_g).T
    held_h = core_rows(after(own_h, slots_g), other_h)
    slots_u = grad_of(after(d_up, *held_h), h_all)
    grad_w_up = sum_wide(slots_u).T
    held_h = second_rows(held_h)
    d_h = first_rows(held_h)
    own_m, other_m = call(
        mlp_down,
        [shaped(many // 2, width)] * 2,
        [],
        [tile_f, pl.BlockSpec((units, width), lambda t: (0, 0))],
        [half_d] * 2,
        2 * many * width * units,
        2e7,
        grid=(many // TILE,),
        name="mlp_down",
    )(after(hidden, slots_u, *held_h), wd)
    d_h = after(d_h, own_m)

    def finish_weight(held):
        near_a, far_a = links.scatter_first(held[0], 0)
        near_b, far_b = links.scatter_first(held[1], 1)
        return links.direct_scatter(
            jnp.concatenate([near_a, near_b], axis=1), jnp.concatenate([far_a, far_b], axis=1)
        )

    blocks_half = 16 * SHARE
    d_mid, d_att, d_gain, *halves_o = call(
        branch_back,
        [
            shaped(TOKENS, width, dtype=F32),
            shaped(TOKENS, HQ),
            shaped(1, width, dtype=F32),
        ]
        + [shaped(blocks_half, half)] * 4,
        [pltpu.VMEM((HQ, width), BF16), pltpu.VMEM((HQ, width), BF16), dma((2, 32)), dma((2, 32))],
        in_smem(2) + in_vmem(8) + anywhere(8),
        in_vmem(3) + anywhere(4),
        4 * TOKENS * width * HQ,
        1.5e7,
        name="branch_back",
    )(*starts, *d_h, x_mid, grad, vec, attended, *o_weight)
    dq, own_kv, other_kv = call(
        attend_back,
        [shaped(TOKENS, HQ)] + [shaped(ROWS, ROW_LEN // 2, 2 * HK)] * 2,
        [],
        in_vmem(6) + in_vmem(8),
        in_vmem(3),
        10 * TOKENS * ROW_LEN * HQ,
        1e7,
        name="attend_back",
    )(q, d_att, cosine, sine, barred, lse, *kv_rows)
    held_kv = core_rows(own_kv.reshape(ROW_LEN, 2 * HK), other_kv.reshape(ROW_LEN, 2 * HK))
    held_kv = second_rows(held_kv)
    d_kv = first_rows(held_kv)
    held_o = [
        links.scatter_core(after(halves_o[0], dq), halves_o[1]),
        links.scatter_core(after(halves_o[2], dq), halves_o[3]),
    ]
    d_h_q, d_bias, *halves_q = call(
        query_back,
        [shaped(TOKENS, width, dtype=F32), shaped(1, HQ, dtype=F32)] + [shaped(blocks_half, half)] * 4,
        [pltpu.VMEM((width, HQ), BF16), pltpu.VMEM((width, HQ), BF16), dma((2, 32)), dma((2, 32))],
        in_smem(2) + in_vmem(2) + anywhere(8),
        in_vmem(2) + anywhere(4),
        4 * TOKENS * width * HQ,
        1.2e7,
        name="query_back",
    )(starts[0], starts[1], dq, h_one, *q_weight)
    held_o = after(held_o, d_h_q)
    grad_w_out = finish_weight([links.scatter_second(held_o[i], i) for i in range(2)])
    held_q = [
        links.scatter_core(halves_q[0], halves_q[1]),
        links.scatter_core(halves_q[2], halves_q[3]),
    ]
    grad_w_query = finish_weight([links.scatter_second(held_q[i], i) for i in range(2)])
    grad_in, own_w, other_w = call(
        kv_back,
        [shaped(TOKENS, width)] + [shaped(16 * KV_BLOCK, 2 * HK)] * 2,
        [
            pltpu.VMEM((width, 2 * HK), BF16),
            pltpu.VMEM((width, 2 * HK), BF16),
            pltpu.VMEM((512, 2 * HK), BF16),
            dma((32,)),
            dma((32,)),
            dma((32,)),
        ],
        in_smem(1) + in_vmem(18) + anywhere(4),
        in_vmem(1) + anywhere(2),
        4 * TOKENS * width * 2 * HK,
        1e7,
        name="kv_back",
    )(
        starts[0], *d_kv, x, h_one, vec, cosine, sine, d_h_q, d_mid, d_gain, d_bias,
        begin, begin_small, pick, pick_k, pick_v, *kv_weight,
    )
    kv_sum = links.direct_scatter(*links.scatter(own_w, other_w, 0))
    mixed = first_rows(second_rows(core_rows(after(own_m, own_w), other_m)))
    layer_out = (
        x_mid
        + jnp.concatenate([mixed[0], mixed[2]], axis=0).astype(F32)
        + jnp.concatenate([mixed[1], mixed[3]], axis=0).astype(F32)
    ).astype(BF16)
    last = kv_sum[SHARE]
    small = b_key.shape[0]
    return (
        layer_out.reshape(layer_in.shape),
        grad_in.reshape(layer_in.shape),
        last[:SHARE],
        grad_w_query,
        last[256 : 256 + SHARE],
        kv_sum[:SHARE, :HK],
        last[384 : 384 + small],
        kv_sum[:SHARE, HK:],
        last[384 + small : 384 + 2 * small],
        grad_w_out,
        last[128 : 128 + SHARE],
        grad_w_gate,
        grad_w_up,
        grad_w_down,
    )


def choose(*args):
    rows, seg_len, _ = args[0].shape
    fits = (rows, seg_len, lax.axis_size("narrow"), lax.axis_size("wide"), args[4].shape[0]) == (
        ROWS,
        SEG,
        PARTS,
        WIDE,
        SHARE,
    )
    return (fast_device if fits else plain_device)(*args)


def solution(mesh):
    return jax.shard_map(
        choose,
        mesh=mesh,
        in_specs=(
            P("wide", "narrow", None),
            P("wide", "narrow"),
            P("wide", "narrow"),
            P(("wide", "narrow")),
            P(("wide", "narrow"), None),
            P(("wide", "narrow")),
            P(("wide", "narrow"), None),
            P(("wide", "narrow")),
            P(("wide", "narrow"), None),
            P(("wide", "narrow")),
            P(("wide", "narrow"), None),
            P(("wide", "narrow")),
            P("wide", "narrow"),
            P("wide", "narrow"),
            P("narrow", "wide"),
            P("wide", "narrow", None),
        ),
        out_specs=(
            P("wide", "narrow", None),
            P("wide", "narrow", None),
            P(("wide", "narrow")),
            P(("wide", "narrow"), None),
            P(("wide", "narrow")),
            P(("wide", "narrow"), None),
            P(("wide", "narrow")),
            P(("wide", "narrow"), None),
            P(("wide", "narrow")),
            P(("wide", "narrow"), None),
            P(("wide", "narrow")),
            P("wide", "narrow"),
            P("wide", "narrow"),
            P("narrow", "wide"),
        ),
        check_vma=False,
    )
```

```python
import functools
import math

import jax
import jax.numpy as jnp
import numpy as np
from jax import lax
from jax.experimental import pallas as pl
from jax.experimental.pallas import tpu as pltpu
from jax.sharding import PartitionSpec as P

Q_HEADS = 12
KV_HEADS = 2
HEAD = 128
HQ = 1536
HK = 256


EPS = 1e-06
THETA = 10000.0


def norm_parts(value):
    factor = lax.rsqrt(jnp.mean(value * value, axis=-1, keepdims=True) + EPS)
    return (value * factor, factor)


def norm_back(grad, unit, factor, gain):
    scaled = grad * gain
    return factor * (scaled - unit * jnp.mean(scaled * unit, axis=-1, keepdims=True))


def rotate(value, cosine, sine):
    half = value.shape[-1] // 2
    first = value[..., :half]
    second = value[..., half:]
    return jnp.concatenate(
        [first * cosine - second * sine, second * cosine + first * sine], axis=-1
    )


def angles(places, head_size):
    freq = jnp.exp(
        jnp.arange(head_size // 2, dtype=jnp.float32) * (-2.0 * math.log(THETA) / head_size)
    )
    turn = places.astype(jnp.float32)[..., None] * freq
    return (jnp.cos(turn), jnp.sin(turn))


def row_probs(query, keys, allowed, scale):
    scores = jnp.einsum("qhgd,khd->hgqk", query, keys, preferred_element_type=jnp.float32) * scale
    scores = jnp.where(allowed[None, None], scores, -1e30)
    top = jnp.max(scores, axis=-1, keepdims=True)
    expo = jnp.exp(scores - top)
    return expo / jnp.sum(expo, axis=-1, keepdims=True)


def swiglu_back(d_hidden, gate, up):
    sigma = jax.nn.sigmoid(gate)
    active = gate * sigma
    d_gate = (d_hidden * up * sigma * (1.0 + gate * (1.0 - sigma))).astype(jnp.bfloat16)
    d_up = (d_hidden * active).astype(jnp.bfloat16)
    return (d_gate, d_up)


def plain_device(
    layer_in,
    seg_ids,
    pad_mask,
    gain_attn,
    w_query,
    b_query,
    w_key,
    b_key,
    w_value,
    b_value,
    w_out,
    gain_mlp,
    w_gate,
    w_up,
    w_down,
    grad_out,
):
    rows, seg_len, width = layer_in.shape
    parts = lax.axis_size("narrow")
    row_len = seg_len * parts
    me = lax.axis_index("narrow")
    group = Q_HEADS // KV_HEADS
    scale = 1.0 / math.sqrt(HEAD)
    f32 = jnp.float32
    bf16 = jnp.bfloat16
    ids_all, pads_all = (
        lax.all_gather(seg_ids, "narrow", axis=1, tiled=True),
        lax.all_gather(pad_mask, "narrow", axis=1, tiled=True),
    )
    wq, wk, wv, wo, g_one, g_two, bq, bk, bv = (
        lax.all_gather(w_query, ("wide", "narrow"), axis=0, tiled=True),
        lax.all_gather(w_key, ("wide", "narrow"), axis=0, tiled=True),
        lax.all_gather(w_value, ("wide", "narrow"), axis=0, tiled=True),
        lax.all_gather(w_out, ("wide", "narrow"), axis=0, tiled=True),
        lax.all_gather(gain_attn, ("wide", "narrow"), axis=0, tiled=True),
        lax.all_gather(gain_mlp, ("wide", "narrow"), axis=0, tiled=True),
        lax.all_gather(b_query, ("wide", "narrow"), axis=0, tiled=True),
        lax.all_gather(b_key, ("wide", "narrow"), axis=0, tiled=True),
        lax.all_gather(b_value, ("wide", "narrow"), axis=0, tiled=True),
    )
    wg, wu, wd = (
        lax.all_gather(w_gate, "wide", axis=0, tiled=True),
        lax.all_gather(w_up, "wide", axis=0, tiled=True),
        lax.all_gather(w_down, "wide", axis=1, tiled=True),
    )
    g_one = g_one.astype(f32)
    g_two = g_two.astype(f32)
    global_idx = me * seg_len + jnp.arange(seg_len, dtype=jnp.int32)
    begins = jnp.sum((ids_all[:, None, :] < seg_ids[:, :, None]).astype(jnp.int32), axis=-1)
    cosine, sine = angles(global_idx[None, :] - begins, HEAD)
    cosine = cosine[:, :, None, :]
    sine = sine[:, :, None, :]
    key_idx = jnp.arange(row_len, dtype=jnp.int32)
    allowed = (ids_all[:, None, :] == seg_ids[:, :, None]) & (
        key_idx[None, None, :] < global_idx[None, :, None]
    ) & (pads_all[:, None, :] == 1) | (key_idx[None, None, :] == global_idx[None, :, None])
    x_in = layer_in.astype(f32)
    unit_one, factor_one = norm_parts(x_in)
    h_one = (unit_one * g_one).astype(bf16)
    q_lin = jnp.dot(h_one, wq, preferred_element_type=f32) + bq.astype(f32)
    k_lin = jnp.dot(h_one, wk, preferred_element_type=f32) + bk.astype(f32)
    v_lin = jnp.dot(h_one, wv, preferred_element_type=f32) + bv.astype(f32)
    q_rot = rotate(q_lin.reshape(rows, seg_len, Q_HEADS, HEAD), cosine, sine).astype(bf16)
    k_rot = rotate(k_lin.reshape(rows, seg_len, KV_HEADS, HEAD), cosine, sine).astype(bf16)
    v_low = v_lin.astype(bf16)
    keys_all, values_all = (
        lax.all_gather(k_rot.reshape(rows, seg_len, HK), "narrow", axis=1, tiled=True),
        lax.all_gather(v_low, "narrow", axis=1, tiled=True),
    )
    keys_all = keys_all.reshape(rows, row_len, KV_HEADS, HEAD)
    values_all = values_all.reshape(rows, row_len, KV_HEADS, HEAD)
    queries = q_rot.reshape(rows, seg_len, KV_HEADS, group, HEAD)
    outputs = []
    for row in range(rows):
        probs = row_probs(queries[row], keys_all[row], allowed[row], scale)
        outputs.append(
            jnp.einsum(
                "hgqk,khd->qhgd", probs.astype(bf16), values_all[row], preferred_element_type=f32
            )
        )
    attended = jnp.stack(outputs).reshape(rows, seg_len, HQ).astype(bf16)
    x_mid = x_in + jnp.dot(attended, wo, preferred_element_type=f32)
    unit_two, factor_two = norm_parts(x_mid)
    h_two = (unit_two * g_two).astype(bf16)
    h_all = lax.all_gather(h_two, "narrow", axis=1, tiled=True)
    gate = jnp.dot(h_all, wg, preferred_element_type=f32)
    up = jnp.dot(h_all, wu, preferred_element_type=f32)
    hidden = (jax.nn.silu(gate) * up).astype(bf16)
    partial_value = jnp.dot(hidden, wd, preferred_element_type=f32)
    mixed = lax.psum_scatter(partial_value, "narrow", scatter_dimension=1, tiled=True)
    layer_out = (x_mid + mixed).astype(bf16)
    grad_all = lax.all_gather(grad_out, "narrow", axis=1, tiled=True)
    d_hidden = jnp.einsum("rtd,fd->rtf", grad_all, wd, preferred_element_type=f32)
    d_wd = jnp.einsum("rtf,rtd->fd", hidden, grad_all, preferred_element_type=f32)
    d_gate, d_up = swiglu_back(d_hidden, gate, up)
    d_wg = jnp.einsum("rtd,rtf->df", h_all, d_gate, preferred_element_type=f32)
    d_wu = jnp.einsum("rtd,rtf->df", h_all, d_up, preferred_element_type=f32)
    grad_w_gate, grad_w_up, grad_w_down = (
        lax.psum_scatter(d_wg, "wide", scatter_dimension=0, tiled=True),
        lax.psum_scatter(d_wu, "wide", scatter_dimension=0, tiled=True),
        lax.psum_scatter(d_wd, "wide", scatter_dimension=1, tiled=True),
    )
    d_h_part = jnp.einsum("rtf,df->rtd", d_gate, wg, preferred_element_type=f32) + jnp.einsum(
        "rtf,df->rtd", d_up, wu, preferred_element_type=f32
    )
    d_h_two = lax.psum_scatter(d_h_part, "narrow", scatter_dimension=1, tiled=True)
    d_g_two = jnp.sum(d_h_two * unit_two, axis=(0, 1))
    d_mid = grad_out.astype(f32) + norm_back(d_h_two, unit_two, factor_two, g_two)
    d_branch = d_mid.astype(bf16)
    d_wo = jnp.einsum("rsh,rsd->hd", attended, d_branch, preferred_element_type=f32)
    d_attended = jnp.einsum("rsd,hd->rsh", d_branch, wo, preferred_element_type=f32).astype(bf16)
    d_att_heads = d_attended.reshape(rows, seg_len, KV_HEADS, group, HEAD)
    query_grads = []
    key_grads = []
    value_grads = []
    for row in range(rows):
        probs = row_probs(queries[row], keys_all[row], allowed[row], scale)
        d_prob = jnp.einsum(
            "qhgd,khd->hgqk", d_att_heads[row], values_all[row], preferred_element_type=f32
        )
        delta = jnp.sum(probs * d_prob, axis=-1, keepdims=True)
        d_score = (scale * probs * (d_prob - delta)).astype(bf16)
        query_grads.append(
            jnp.einsum("hgqk,khd->qhgd", d_score, keys_all[row], preferred_element_type=f32)
        )
        key_grads.append(
            jnp.einsum("hgqk,qhgd->khd", d_score, queries[row], preferred_element_type=f32)
        )
        value_grads.append(
            jnp.einsum(
                "hgqk,qhgd->khd", probs.astype(bf16), d_att_heads[row], preferred_element_type=f32
            )
        )
    d_query = jnp.stack(query_grads).reshape(rows, seg_len, Q_HEADS, HEAD)
    d_keys_all = jnp.stack(key_grads).reshape(rows, row_len, HK)
    d_values_all = jnp.stack(value_grads).reshape(rows, row_len, HK)
    d_keys, d_values = (
        lax.psum_scatter(d_keys_all, "narrow", scatter_dimension=1, tiled=True),
        lax.psum_scatter(d_values_all, "narrow", scatter_dimension=1, tiled=True),
    )
    dq_lin = rotate(d_query, cosine, -sine).reshape(rows, seg_len, HQ).astype(bf16)
    dk_lin = (
        rotate(d_keys.reshape(rows, seg_len, KV_HEADS, HEAD), cosine, -sine)
        .reshape(rows, seg_len, HK)
        .astype(bf16)
    )
    dv_lin = d_values.astype(bf16)
    d_wq = jnp.einsum("rsd,rsh->dh", h_one, dq_lin, preferred_element_type=f32)
    d_wk = jnp.einsum("rsd,rsh->dh", h_one, dk_lin, preferred_element_type=f32)
    d_wv = jnp.einsum("rsd,rsh->dh", h_one, dv_lin, preferred_element_type=f32)
    d_bq = jnp.sum(dq_lin.astype(f32), axis=(0, 1))
    d_bk = jnp.sum(dk_lin.astype(f32), axis=(0, 1))
    d_bv = jnp.sum(dv_lin.astype(f32), axis=(0, 1))
    d_h_one = jnp.einsum("rsh,dh->rsd", dq_lin, wq, preferred_element_type=f32)
    d_h_one = d_h_one + jnp.einsum("rsh,dh->rsd", dk_lin, wk, preferred_element_type=f32)
    d_h_one = d_h_one + jnp.einsum("rsh,dh->rsd", dv_lin, wv, preferred_element_type=f32)
    d_g_one = jnp.sum(d_h_one * unit_one, axis=(0, 1))
    grad_in = (d_mid + norm_back(d_h_one, unit_one, factor_one, g_one)).astype(bf16)
    (
        grad_w_query,
        grad_w_key,
        grad_w_value,
        grad_w_out,
        grad_gain_attn,
        grad_gain_mlp,
        grad_b_query,
        grad_b_key,
        grad_b_value,
    ) = (
        lax.psum_scatter(d_wq, ("wide", "narrow"), scatter_dimension=0, tiled=True),
        lax.psum_scatter(d_wk, ("wide", "narrow"), scatter_dimension=0, tiled=True),
        lax.psum_scatter(d_wv, ("wide", "narrow"), scatter_dimension=0, tiled=True),
        lax.psum_scatter(d_wo, ("wide", "narrow"), scatter_dimension=0, tiled=True),
        lax.psum_scatter(d_g_one, ("wide", "narrow"), scatter_dimension=0, tiled=True),
        lax.psum_scatter(d_g_two, ("wide", "narrow"), scatter_dimension=0, tiled=True),
        lax.psum_scatter(d_bq, ("wide", "narrow"), scatter_dimension=0, tiled=True),
        lax.psum_scatter(d_bk, ("wide", "narrow"), scatter_dimension=0, tiled=True),
        lax.psum_scatter(d_bv, ("wide", "narrow"), scatter_dimension=0, tiled=True),
    )
    return (
        layer_out,
        grad_in,
        grad_gain_attn,
        grad_w_query,
        grad_b_query,
        grad_w_key,
        grad_b_key,
        grad_w_value,
        grad_b_value,
        grad_w_out,
        grad_gain_mlp,
        grad_w_gate,
        grad_w_up,
        grad_w_down,
    )


F32 = jnp.float32
BF16 = jnp.bfloat16
ROWS = 2
PARTS = 8
WIDE = 4
SEG = 128
SHARE = 48
GROUP = Q_HEADS // KV_HEADS
SCALE = 1.0 / math.sqrt(HEAD)
TOKENS = ROWS * SEG
ROW_LEN = SEG * PARTS
KV_COLUMNS = 2 * HK + 128
FIRST = KV_COLUMNS + 512
TILE = 512


def dot_nn(left, right):
    return lax.dot_general(left, right, (((1,), (0,)), ((), ())), preferred_element_type=F32)


def dot_nt(left, right):
    return lax.dot_general(left, right, (((1,), (1,)), ((), ())), preferred_element_type=F32)


def flipped(value):
    return value.astype(F32).T.astype(BF16)


class Links:
    def __init__(self):
        self.orders = ((2, 4, 1), (4, 2, 1))

    def hop(self, value, bit):
        return lax.ppermute(value, "narrow", [(i, i ^ bit) for i in range(PARTS)])

    def offsets(self, which):
        found = [0]
        for bit in self.orders[which]:
            found = found + [o ^ bit for o in found]
        return found

    def first(self, value, which):
        return self.hop(value, self.orders[which][0])

    def second(self, value, which):
        return self.hop(value, self.orders[which][1])

    def core(self, value):
        return self.hop(value, 1)

    def gather(self, value, which):
        near = jnp.concatenate([value, self.first(value, which)], axis=0)
        far = self.second(near, which)
        return [near, far, self.core(near), self.core(far)]

    def scatter_second(self, held, which):
        half = held.shape[0] // 2
        return held[:half], self.second(held[half:], which)

    def scatter_first(self, held, which):
        half = held.shape[0] // 2
        return held[:half], self.first(held[half:], which)

    def over_wide(self, value, step):
        return lax.ppermute(value, "wide", [(i, (i + step) % WIDE) for i in range(WIDE)])

    def direct_gather(self, value):
        return [value] + [self.over_wide(value, k) for k in range(1, WIDE)]

    def direct_scatter(self, held):
        slots = held.reshape((WIDE, held.shape[0] // WIDE) + held.shape[1:])
        total = slots[0].astype(F32)
        for k in range(1, WIDE):
            total = total + self.over_wide(slots[k], -k).astype(F32)
        return total


def tie(one, other):
    return lax.optimization_barrier((one, other))


def together(values):
    return list(lax.optimization_barrier(tuple(values)))


def in_vmem(count):
    return [pl.BlockSpec(memory_space=pltpu.VMEM)] * count


def in_smem(count):
    return [pl.BlockSpec(memory_space=pltpu.SMEM)] * count


def in_hbm(count):
    return [pl.BlockSpec(memory_space=pltpu.HBM)] * count


def call(body, outs, scratch, in_specs, out_specs, flops, nbytes, vmem, grid=None, name=None):
    return pl.pallas_call(
        body,
        out_shape=outs,
        grid=grid if grid is not None else (),
        in_specs=in_specs,
        out_specs=out_specs,
        scratch_shapes=scratch,
        name=name,
        compiler_params=pltpu.CompilerParams(vmem_limit_bytes=vmem * 1024 * 1024),
        cost_estimate=pl.CostEstimate(
            flops=10 * int(flops), bytes_accessed=10 * int(nbytes), transcendentals=0
        ),
    )


def shaped(*dims, dtype=BF16):
    return jax.ShapeDtypeStruct(dims, dtype)


def weight_copies(pieces, held, starts, sems, source, target):
    copies = []
    for i in range(PARTS * WIDE):
        copies.append(
            pltpu.make_async_copy(
                pieces[i // 8].at[pl.ds((i % 8) * SHARE, SHARE), source],
                held.at[pl.ds(pl.multiple_of(starts[i], 16), SHARE), target],
                sems.at[i],
            )
        )
    return copies


def grad_copies(held, own, other, starts, sems, columns):
    copies = []
    for i in range(PARTS * WIDE):
        target = own if i < 16 else other
        copies.append(
            pltpu.make_async_copy(
                held.at[pl.ds(pl.multiple_of(starts[i], 16), SHARE), columns],
                target.at[pl.ds((i % 16) * SHARE, SHARE), :],
                sems.at[i],
            )
        )
    return copies


def half_copies(pieces, held, starts_a, starts_b, sems):
    half = held.shape[1] // 2
    every = slice(None)
    return weight_copies(
        pieces[:4], held, starts_a, sems.at[0], every, slice(0, half)
    ) + weight_copies(pieces[4:], held, starts_b, sems.at[1], every, slice(half, 2 * half))


def query_copies(pieces, held, starts_a, starts_b, sems):
    cut = FIRST - KV_COLUMNS
    return weight_copies(
        pieces[:4], held, starts_a, sems.at[0], slice(KV_COLUMNS, FIRST), slice(0, cut)
    ) + weight_copies(pieces[4:], held, starts_b, sems.at[1], slice(None), slice(cut, HQ))


def half_grad_copies(held, outs, starts_a, starts_b, sems):
    half = held.shape[1] // 2
    return grad_copies(
        held, outs[0], outs[1], starts_a, sems.at[0], slice(0, half)
    ) + grad_copies(held, outs[2], outs[3], starts_b, sems.at[1], slice(half, 2 * half))


def turn(value, cosine, sine):
    return value * cosine + pltpu.roll(value, HEAD // 2, 1) * sine


def project_kv(starts, x, cosine, sine, pick_k, pick_v, *refs):
    pieces, (kv_out, h_out, vec_out, whole, held, sems, out_sem) = refs[:4], refs[4:]
    copies = weight_copies(pieces, held, starts, sems, slice(0, KV_COLUMNS), slice(None))
    for copy in copies:
        copy.start()
    value = x[...].astype(F32)
    unit = value * lax.rsqrt(jnp.mean(value * value, axis=-1, keepdims=True) + EPS)
    for copy in copies:
        copy.wait()
    over = pltpu.make_async_copy(held, whole, out_sem)
    over.start()
    vec = held[:, 2 * HK :].astype(F32).T[:8, :]
    vec_out[...] = vec
    low = vec.astype(BF16)
    b_key = dot_nn(low, pick_k[...])[3:4, :]
    b_value = dot_nn(low, pick_v[...])[3:4, :]
    h_one = (unit * vec[0:1, :]).astype(BF16)
    h_out[...] = h_one
    lin = dot_nn(h_one, held[:, : 2 * HK])
    for head in range(KV_HEADS):
        cut = slice(head * HEAD, (head + 1) * HEAD)
        key = turn(lin[:, cut] + b_key[:, cut], cosine[...], sine[...])
        kv_out[:, cut] = key.astype(BF16)
    kv_out[:, HK:] = (lin[:, HK:] + b_value).astype(BF16)
    over.wait()


def project_q(starts_a, starts_b, h_one, vec, cosine, sine, *refs):
    pieces, (q_out, whole, held, sems, out_sem) = refs[:8], refs[8:]
    copies = query_copies(pieces, held, starts_a, starts_b, sems)
    for copy in copies:
        copy.start()
    for copy in copies:
        copy.wait()
    over = pltpu.make_async_copy(held, whole, out_sem)
    over.start()
    lin = dot_nn(h_one[...], held[...]) + vec[2:3, :]
    for head in range(Q_HEADS):
        cut = slice(head * HEAD, (head + 1) * HEAD)
        q_out[:, cut] = turn(lin[:, cut], cosine[...], sine[...]).astype(BF16)
    over.wait()


def stacked(ref, row, kv_head):
    first = kv_head * GROUP
    return jnp.concatenate(
        [
            ref[row * SEG : (row + 1) * SEG, (first + g) * HEAD : (first + g + 1) * HEAD]
            for g in range(GROUP)
        ],
        axis=0,
    )


def row_keys(pieces, row, column):
    return jnp.concatenate(
        [piece[:, column : column + HEAD] for piece in pieces[4 * row : 4 * row + 4]], axis=0
    )


def attend(q, barred, *refs):
    kv, (att_out, lse_out) = refs[:8], refs[8:]
    for row in range(ROWS):
        bar = barred[row]
        bar = jnp.concatenate([bar] * GROUP, axis=1)
        for kv_head in range(KV_HEADS):
            keys = row_keys(kv, row, kv_head * HEAD)
            values = row_keys(kv, row, HK + kv_head * HEAD)
            scores = dot_nt(keys, stacked(q, row, kv_head)) * SCALE + bar
            top = jnp.max(scores, axis=0, keepdims=True)
            expo = jnp.exp(scores - top)
            total = jnp.sum(expo, axis=0, keepdims=True)
            lse_out[row * KV_HEADS + kv_head] = top + jnp.log(total)
            probs = (expo / total).astype(BF16)
            out = dot_nn(flipped(values), probs)
            for g in range(GROUP):
                head = kv_head * GROUP + g
                att_out[row * SEG : (row + 1) * SEG, head * HEAD : (head + 1) * HEAD] = (
                    out[:, g * SEG : (g + 1) * SEG].T.astype(BF16)
                )


def branch(starts_a, starts_b, att, x, vec, *refs):
    pieces, (mid_out, h_out, whole, held, sems, out_sem) = refs[:8], refs[8:]
    copies = half_copies(pieces, held, starts_a, starts_b, sems)
    for copy in copies:
        copy.start()
    for copy in copies:
        copy.wait()
    over = pltpu.make_async_copy(held, whole, out_sem)
    over.start()
    mid = x[...].astype(F32) + dot_nn(att[...], held[...])
    mid_out[...] = mid
    factor = lax.rsqrt(jnp.mean(mid * mid, axis=-1, keepdims=True) + EPS)
    h_out[...] = (mid * factor * vec[1:2, :]).astype(BF16)
    over.wait()


def swiglu_parts(h, grad, weights):
    units = weights.shape[0] // 3
    d_hidden = dot_nt(grad, weights[:units, :])
    both = dot_nt(h, weights[units:, :])
    gate, up = both[:, :units], both[:, units:]
    sigma = jax.nn.sigmoid(gate)
    active = gate * sigma
    hidden = (active * up).astype(BF16)
    d_gate = (d_hidden * up * sigma * (1.0 + gate * (1.0 - sigma))).astype(BF16)
    d_up = (d_hidden * active).astype(BF16)
    return hidden, d_gate, d_up


def mlp_first(grad, *refs):
    h_pieces, weights, refs = refs[:8], refs[8], refs[9:]
    d_t_out, d_h_out, mixed_out, h_all, h_v, w_v, sems, w_sem, out_sems = refs
    step = pl.program_id(0)
    rows = h_pieces[0].shape[0]
    units = w_v.shape[0] // 3

    def pieces_in():
        return [
            pltpu.make_async_copy(h_pieces[i], h_v.at[pl.ds(i * rows, rows), :], sems.at[i])
            for i in range(8)
        ]

    def weights_in():
        return pltpu.make_async_copy(weights, w_v, w_sem.at[0])

    def h_over(tile):
        at = pl.ds(pl.multiple_of(tile * TILE, TILE), TILE)
        return pltpu.make_async_copy(h_v.at[at, :], h_all.at[at, :], out_sems.at[tile])

    @pl.when(step == 0)
    def _():
        held = pieces_in()
        for copy in held[:2] + [weights_in()] + held[2:]:
            copy.start()

    for tile in range(4):

        @pl.when(step == tile)
        def _(tile=tile):
            for copy in pieces_in()[2 * tile : 2 * tile + 2]:
                copy.wait()
            h_over(tile).start()

    @pl.when(step == 0)
    def _():
        weights_in().wait()

    h = h_v[pl.ds(pl.multiple_of(step * TILE, TILE), TILE), :]
    hidden, d_gate, d_up = swiglu_parts(h, grad[...], w_v)
    d_t_out[:units, :] = hidden.T
    d_t_out[units : 2 * units, :] = d_gate.T
    d_t_out[2 * units :, :] = d_up.T
    d_pair = jnp.concatenate([d_gate, d_up], axis=1)
    d_h_out[...] = dot_nn(d_pair, w_v[units:, :]).astype(BF16)
    mixed_out[...] = dot_nn(hidden, w_v[:units, :]).astype(BF16)

    @pl.when(step == 3)
    def _():
        for tile in range(4):
            h_over(tile).wait()


def put_halves(value, outs, step):
    if len(outs) == 1:
        outs[0][...] = value
        return
    half = value.shape[0] // 2
    outs[0][...] = value[:half, :]
    for row in range(ROWS):

        @pl.when(step == row)
        def _(row=row):
            outs[1 + row][...] = value[half:, :]


def mlp_second(grad, h, weights, *refs):
    count = 3 if len(refs) == 10 else 1
    added, d_t_out, hid_out = refs[: -5 - count], refs[-5 - count], refs[-4 - count]
    h_outs, (d_v, w_v, sems) = refs[-3 - count : -3], refs[-3:]
    step = pl.program_id(0)
    units = w_v.shape[0] // 3

    def weights_in():
        return [
            pltpu.make_async_copy(
                weights.at[pl.ds(i * units, (1 + i) * units), :],
                w_v.at[pl.ds(i * units, (1 + i) * units), :],
                sems.at[i],
            )
            for i in range(2)
        ]

    @pl.when(step == 0)
    def _():
        for copy in weights_in():
            copy.start()
        for copy in weights_in():
            copy.wait()

    hidden, d_gate, d_up = swiglu_parts(h[...], grad[...], w_v)
    hid_out[...] = hidden
    d_t_out[:units, :] = hidden.T
    d_t_out[units : 2 * units, :] = d_gate.T
    d_t_out[2 * units :, :] = d_up.T
    d_v[:, :units] = d_gate
    d_v[:, units:] = d_up
    d_h = dot_nn(d_v[...], w_v[units:, :])
    for ref in added:
        d_h = d_h + ref[...].astype(F32)
    put_halves(d_h.astype(BF16), h_outs, step)


def mlp_down(hid, weights, *refs):
    count = 3 if len(refs) == 5 else 1
    added, outs = refs[:-count], refs[-count:]
    mixed = dot_nn(hid[...], weights[...])
    for ref in added:
        mixed = mixed + ref[...].astype(F32)
    put_halves(mixed.astype(BF16), outs, pl.program_id(0))


def weight_grad(left_own, left_other, right_grad, right_h, out):
    half = left_own.shape[1]
    cut = out.shape[2]

    def put(right):
        found = dot_nn(left_own[...], right[:half, :]) + dot_nn(left_other[...], right[half:, :])
        found = found.astype(BF16)
        out[0] = found[:, :cut]
        out[1] = found[:, cut:]

    @pl.when(pl.program_id(1) == 0)
    def _():
        put(right_grad)

    @pl.when(pl.program_id(1) > 0)
    def _():
        put(right_h)


def branch_back(starts_a, starts_b, keep_a, got_a, keep_b, got_b, mid, grad, vec, att, weight, *refs):
    (d_mid_out, d_att_out, d_gain_out), outs = refs[:3], refs[3:7]
    held, held_d, sem, out_sems = refs[7:]
    copy = pltpu.make_async_copy(weight, held, sem)
    copy.start()
    d_h = jnp.concatenate(
        [
            keep_a[...].astype(F32) + got_a[...].astype(F32),
            keep_b[...].astype(F32) + got_b[...].astype(F32),
        ],
        axis=0,
    )
    x_mid = mid[...]
    factor = lax.rsqrt(jnp.mean(x_mid * x_mid, axis=-1, keepdims=True) + EPS)
    unit = x_mid * factor
    d_gain_out[...] = jnp.sum(d_h * unit, axis=0, keepdims=True)
    d_mid = grad[...].astype(F32) + norm_back(d_h, unit, factor, vec[1:2, :])
    d_mid_out[...] = d_mid
    d_branch = d_mid.astype(BF16)
    held_d[...] = dot_nn(flipped(att[...]), d_branch).astype(BF16)
    out_copies = half_grad_copies(held_d, outs, starts_a, starts_b, out_sems)
    for out_copy in out_copies:
        out_copy.start()
    copy.wait()
    d_att_out[...] = dot_nt(d_branch, held[...]).astype(BF16)
    for out_copy in out_copies:
        out_copy.wait()


def attend_back(row, q, d_att, cosine, sine, barred, lse, *refs):
    kv, (dq_out, own, other) = refs[:4], refs[4:]
    bar = jnp.concatenate([barred[row]] * GROUP, axis=1)
    at = slice(row * SEG, (row + 1) * SEG)
    for kv_head in range(KV_HEADS):
        keys = row_keys(kv, 0, kv_head * HEAD)
        values = row_keys(kv, 0, HK + kv_head * HEAD)
        queries = stacked(q, row, kv_head)
        d_out = stacked(d_att, row, kv_head)
        scores = dot_nt(keys, queries) * SCALE + bar
        probs = jnp.exp(scores - lse[row * KV_HEADS + kv_head])
        d_prob = dot_nt(values, d_out)
        delta = jnp.sum(probs * d_prob, axis=0, keepdims=True)
        d_score = (SCALE * probs * (d_prob - delta)).astype(BF16)
        d_value = dot_nn(probs.astype(BF16), d_out).astype(BF16)
        d_key = dot_nn(d_score, queries).astype(BF16)
        half = ROW_LEN // 2
        cut = slice(kv_head * HEAD, (kv_head + 1) * HEAD)
        cut_v = slice(HK + kv_head * HEAD, HK + (kv_head + 1) * HEAD)
        own[:, cut] = d_key[:half]
        other[:, cut] = d_key[half:]
        own[:, cut_v] = d_value[:half]
        other[:, cut_v] = d_value[half:]
        d_query = dot_nn(flipped(keys), d_score)
        for g in range(GROUP):
            head = kv_head * GROUP + g
            back = turn(d_query[:, g * SEG : (g + 1) * SEG].T, cosine[at, :], -sine[at, :])
            dq_out[:, head * HEAD : (head + 1) * HEAD] = back.astype(BF16)


def query_back(starts_a, starts_b, dq_a, dq_b, h_one, weight, *refs):
    (d_h_out, d_bias_out), outs = refs[:2], refs[2:6]
    held, held_d, sem, out_sems = refs[6:]
    copy = pltpu.make_async_copy(weight, held, sem)
    copy.start()
    dq = jnp.concatenate([dq_a[...], dq_b[...]], axis=0)
    held_d[...] = dot_nn(flipped(h_one[...]), dq).astype(BF16)
    out_copies = half_grad_copies(held_d, outs, starts_a, starts_b, out_sems)
    for out_copy in out_copies:
        out_copy.start()
    d_bias_out[...] = jnp.sum(dq.astype(F32), axis=0, keepdims=True)
    copy.wait()
    d_h_out[...] = dot_nt(dq, held[...])
    for out_copy in out_copies:
        out_copy.wait()


def kv_back(
    starts, keep_a, got_a, keep_b, got_b, x, h_one, vec, cosine, sine, d_h_q, d_mid, d_gain, d_bias,
    pick_k, pick_v, weight, *refs,
):
    grad_out, own, other, held_d, out_sems = refs
    d_kv = jnp.concatenate(
        [
            keep_a[...].astype(F32) + got_a[...].astype(F32),
            keep_b[...].astype(F32) + got_b[...].astype(F32),
        ],
        axis=0,
    )
    parts = [
        turn(d_kv[:, head * HEAD : (head + 1) * HEAD], cosine[...], -sine[...])
        for head in range(KV_HEADS)
    ]
    d_lin = jnp.concatenate(parts + [d_kv[:, HK:]], axis=1).astype(BF16)
    held_d[:, : 2 * HK] = dot_nn(flipped(h_one[...]), d_lin).astype(BF16)
    d_small = jnp.sum(d_lin.astype(F32), axis=0, keepdims=True).astype(BF16)
    value = x[...].astype(F32)
    factor = lax.rsqrt(jnp.mean(value * value, axis=-1, keepdims=True) + EPS)
    unit = value * factor
    d_h = d_h_q[...] + dot_nt(d_lin, weight[:, : 2 * HK])
    packed = jnp.concatenate(
        [
            jnp.sum(d_h * unit, axis=0, keepdims=True),
            d_gain[...],
            d_bias[...],
            dot_nt(d_small[:, :HK], pick_k[...]) + dot_nt(d_small[:, HK:], pick_v[...]),
            jnp.zeros((124, HQ), F32),
        ],
        axis=0,
    )
    held_d[:, 2 * HK :] = packed.T.astype(BF16)
    out_copies = grad_copies(held_d, own, other, starts, out_sems, slice(None))
    for copy in out_copies:
        copy.start()
    grad_out[...] = (d_mid[...] + norm_back(d_h, unit, factor, vec[0:1, :])).astype(BF16)
    for copy in out_copies:
        copy.wait()


def fast_device(
    layer_in,
    seg_ids,
    pad_mask,
    gain_attn,
    w_query,
    b_query,
    w_key,
    b_key,
    w_value,
    b_value,
    w_out,
    gain_mlp,
    w_gate,
    w_up,
    w_down,
    grad_out,
):
    width = layer_in.shape[2]
    units = w_gate.shape[1]
    split = units * 4 // 7
    links = Links()
    here = lax.axis_index("wide")
    me = lax.axis_index("narrow")
    dma = pltpu.SemaphoreType.DMA
    order = [0, 1]
    x = layer_in.reshape(TOKENS, width)
    grad = grad_out.reshape(TOKENS, width)

    slots = jnp.arange(WIDE, dtype=jnp.int32)
    partners = [me ^ jnp.array(links.offsets(o), jnp.int32) for o in order]
    starts = [
        (p[:, None] + (slots * PARTS)[None, :]).reshape(-1) * SHARE for p in partners
    ]
    ends = [
        (p[:, None] + ((here - slots) % WIDE * PARTS)[None, :]).reshape(-1) * SHARE for p in partners
    ]
    cut = width // WIDE
    lanes = np.arange(HQ)
    small = b_key.shape[0]
    in_block = lanes % SHARE
    head_lane = lanes // SHARE * small + in_block
    pick_k = (in_block < small)[:, None] & (head_lane[:, None] == np.arange(HK))
    pick_v = ((in_block >= small) & (in_block < 2 * small))[:, None] & (
        (head_lane - small)[:, None] == np.arange(HK)
    )
    pick_k, pick_v = jnp.asarray(pick_k, BF16), jnp.asarray(pick_v, BF16)

    half = HQ // 2
    rows = range(ROWS)
    both = range(2)
    at_row = [slice(r * SEG, (r + 1) * SEG) for r in rows]

    vectors = jnp.stack(
        [gain_attn, gain_mlp, b_query, jnp.pad(jnp.concatenate([b_key, b_value]), (0, SHARE - 2 * small))],
        axis=1,
    )
    vectors = jnp.pad(vectors, ((0, 0), (0, 124)))
    own = jnp.concatenate([w_key, w_value, vectors, w_query, w_out], axis=1)
    w_rows = lax.all_gather(own, "wide", axis=0, tiled=True)
    parts = [(0, split), (split, units)]
    own_parts = [
        jnp.concatenate([w_down[p:q], w_gate.T[p:q], w_up.T[p:q]], axis=0) for p, q in parts
    ]

    grad_own = [grad[at_row[r]] for r in rows]
    grad_one = [links.first(grad_own[r], order[r]) for r in rows]
    grad_one = together(grad_one)
    marks = jnp.stack([seg_ids, pad_mask])[None]
    marks = jnp.concatenate([marks, links.first(marks, 0)], axis=0)
    marks = jnp.concatenate([marks, links.second(marks, 0)], axis=0)
    marks = jnp.concatenate([marks, links.core(marks)], axis=0)
    grad_near = [jnp.concatenate([grad_own[r], grad_one[r]], axis=0) for r in rows]
    grad_far = [links.second(grad_near[r], order[r]) for r in rows]

    at = {o: i for i, o in enumerate(links.offsets(0))}
    marks = [jnp.stack([marks[at[o], :, r] for o in links.offsets(order[r])]) for r in rows]
    ids_all = jnp.stack([m[:, 0].reshape(ROW_LEN) for m in marks])
    pads_all = jnp.stack([m[:, 1].reshape(ROW_LEN) for m in marks])
    sources = jnp.array([links.offsets(o) for o in order], jnp.int32) ^ me
    key_idx = (
        sources[:, :, None] * SEG + jnp.arange(SEG, dtype=jnp.int32)[None, None, :]
    ).reshape(ROWS, ROW_LEN)
    own_idx = me * SEG + jnp.arange(SEG, dtype=jnp.int32)
    begins = jnp.sum((ids_all[:, None, :] < seg_ids[:, :, None]).astype(jnp.int32), axis=-1)
    cosine, sine = angles((own_idx[None, :] - begins).reshape(TOKENS), HEAD)
    cosine = jnp.concatenate([cosine, cosine], axis=-1)
    sine = jnp.concatenate([-sine, sine], axis=-1)
    allowed = (ids_all[:, :, None] == seg_ids[:, None, :]) & (
        key_idx[:, :, None] < own_idx[None, None, :]
    ) & (pads_all[:, :, None] == 1) | (key_idx[:, :, None] == own_idx[None, None, :])
    barred = jnp.where(allowed, 0.0, -1e30).astype(F32)

    w_rows, (cosine, sine, barred, grad_far) = tie(w_rows, (cosine, sine, barred, grad_far))
    w_rows, own_parts[0] = tie(w_rows, own_parts[0])
    weights = [lax.all_gather(own_parts[0], "wide", axis=1, tiled=True)]
    bounds = (0, FIRST, KV_COLUMNS + HQ, KV_COLUMNS + HQ + half, KV_COLUMNS + HQ + width)
    w_slots = [w_rows[:, bounds[i] : bounds[i + 1]] for i in both]
    w_one = [links.first(w_slots[i], i) for i in both]
    w_one = together(w_one)
    w_near = [jnp.concatenate([w_slots[i], w_one[i]], axis=0) for i in both]
    w_far = [links.second(w_near[i], i) for i in both]
    w_far = together(w_far)
    grad_pieces = [p for r in rows for p in (grad_near[r], grad_far[r])]
    grad_pieces += [links.core(p) for p in grad_pieces]
    grad_all = jnp.concatenate(grad_pieces, axis=0)
    w_far, grad_all = tie(w_far, grad_all)
    w_pieces = [
        [w_near[i], w_far[i], links.core(w_near[i]), links.core(w_far[i])] for i in both
    ]
    o_slots = [w_rows[:, bounds[i + 2] : bounds[i + 3]] for i in both]
    o_slots, w_far = tie(o_slots, w_far)
    o_one = [links.first(o_slots[i], i) for i in both]
    o_one = together(o_one)
    kv, h_one, vec, w_kv = call(
        project_kv,
        [
            shaped(TOKENS, 2 * HK),
            shaped(TOKENS, width),
            shaped(8, width, dtype=F32),
            shaped(width, KV_COLUMNS),
        ],
        [pltpu.VMEM((width, KV_COLUMNS), BF16), dma((32,)), dma],
        in_smem(1) + in_vmem(5) + in_hbm(4),
        in_vmem(3) + in_hbm(1),
        2 * TOKENS * width * 2 * HK,
        4e6,
        20,
        name="project_kv",
    )(starts[0], x, cosine, sine, pick_k, pick_v, *w_pieces[0])
    kv_own = [kv[at_row[r]] for r in rows]
    kv_one = [links.first(kv_own[r], order[r]) for r in rows]
    kv_one = together(kv_one)
    q, w_q = call(
        project_q,
        [shaped(TOKENS, HQ), shaped(width, HQ)],
        [pltpu.VMEM((width, HQ), BF16), dma((2, 32)), dma],
        in_smem(2) + in_vmem(4) + in_hbm(8),
        in_vmem(1) + in_hbm(1),
        2 * TOKENS * width * HQ,
        7e6,
        20,
        name="project_q",
    )(*starts, h_one, vec, cosine, sine, *w_pieces[0], *w_pieces[1])
    kv_near = [jnp.concatenate([kv_own[r], kv_one[r]], axis=0) for r in rows]
    kv_far = [links.second(kv_near[r], order[r]) for r in rows]
    kv_far = together(kv_far)
    kv_far, q = tie(kv_far, q)
    kv_far, o_one = tie(kv_far, o_one)
    kv_rows = []
    for r in rows:
        kv_rows += [kv_near[r], kv_far[r], links.core(kv_near[r]), links.core(kv_far[r])]
    o_near = [jnp.concatenate([o_slots[i], o_one[i]], axis=0) for i in both]
    o_far = [links.second(o_near[i], i) for i in both]
    o_far = together(o_far)
    attended, lse = call(
        attend,
        [shaped(TOKENS, HQ), shaped(ROWS * KV_HEADS, 1, GROUP * SEG, dtype=F32)],
        [],
        in_vmem(2) + in_vmem(8),
        in_vmem(2),
        4 * TOKENS * ROW_LEN * HQ,
        4e6,
        40,
        name="attend",
    )(q, barred, *kv_rows)
    o_weight = []
    for i in both:
        o_weight += [o_near[i], o_far[i], links.core(o_near[i]), links.core(o_far[i])]
    x_mid, h_two, w_o = call(
        branch,
        [shaped(TOKENS, width, dtype=F32), shaped(TOKENS, width), shaped(HQ, width)],
        [pltpu.VMEM((HQ, width), BF16), dma((2, 32)), dma],
        in_smem(2) + in_vmem(3) + in_hbm(8),
        in_vmem(2) + in_hbm(1),
        2 * TOKENS * width * HQ,
        8e6,
        24,
        name="branch",
    )(*starts, attended, x, vec, *o_weight)

    h_own = [h_two[at_row[r]] for r in rows]
    h_one_hop = [links.first(h_own[r], order[r]) for r in rows]
    h_one_hop = together(h_one_hop)
    h_one_hop, own_parts[1] = tie(h_one_hop, own_parts[1])
    weights.append(lax.all_gather(own_parts[1], "wide", axis=1, tiled=True))
    h_near = [jnp.concatenate([h_own[r], h_one_hop[r]], axis=0) for r in rows]
    h_far = [links.second(h_near[r], order[r]) for r in rows]
    h_far = together(h_far)
    h_pieces = [p for r in rows for p in (h_near[r], h_far[r])]
    h_pieces += [links.core(p) for p in h_pieces]
    many = ROWS * ROW_LEN
    tile_d = pl.BlockSpec((TILE, width), lambda t: (t, 0))
    size = 3 * split
    d_t, d_h, mixed, h_all = call(
        mlp_first,
        [shaped(size, many), shaped(many, width), shaped(many, width), shaped(many, width)],
        [
            pltpu.VMEM((many, width), BF16),
            pltpu.VMEM((size, width), BF16),
            dma((8,)),
            dma((1,)),
            dma((4,)),
        ],
        [tile_d] + in_hbm(9),
        [pl.BlockSpec((size, TILE), lambda t: (0, t)), tile_d, tile_d] + in_hbm(1),
        many * width * split,
        4e6,
        56,
        grid=(many // TILE,),
        name="mlp_first",
    )(grad_all, *h_pieces, weights[0])

    def grad_of(left_own, left_other, place):
        size = left_own.shape[0]
        block = size // 3
        half_t = [
            pl.BlockSpec((block, many // 2), lambda k, m, at=at: (m, at)) for at in (0, place)
        ]
        right = pl.BlockSpec((many, 2 * cut), lambda k, m: (0, k))
        return call(
            weight_grad,
            shaped(WIDE, size, cut),
            [],
            half_t + [right, right],
            pl.BlockSpec((2, block, cut), lambda k, m: (k, m, 0)),
            (2.0 if place == 0 else 0.2) * many * width * size,
            2e7 if place == 0 else 2e6,
            48,
            grid=(WIDE // 2, 3),
            name="weight_grad",
        )(left_own, left_other, grad_all, h_all)

    def sum_wide(slots):
        return lax.psum_scatter(slots, "wide", scatter_dimension=0, tiled=False)

    slots_a = grad_of(d_t, d_t, 1)
    sum_a = sum_wide(slots_a)
    grad_all, slots_a = tie(grad_all, slots_a)
    rest = units - split

    def sums(last):
        if not last:
            return [shaped(many // 2, width)], [pl.BlockSpec((TILE, width), lambda t: (t, 0))]
        size = TILE // 2
        return (
            [shaped(2 * size, width), shaped(size, width), shaped(size, width)],
            [pl.BlockSpec((size, width), lambda t: (t, 0))]
            + [pl.BlockSpec((size, width), lambda t: (0, 0))] * 2,
        )

    def half_of(place, got):
        tiles = many // TILE // 2
        tile_d = pl.BlockSpec((TILE, width), lambda t: (t + place * tiles, 0))
        tile_o = pl.BlockSpec((TILE, width), lambda t: (t, 0))
        shapes, specs = sums(bool(got))
        return call(
            mlp_second,
            [shaped(3 * rest, many // 2), shaped(many // 2, rest)] + shapes,
            [
                pltpu.VMEM((TILE, 2 * rest), BF16),
                pltpu.VMEM((3 * rest, width), BF16),
                dma((2,)),
            ],
            [tile_d, tile_d] + in_hbm(1) + [tile_d] + [tile_o] * len(got),
            [
                pl.BlockSpec((3 * rest, TILE), lambda t: (0, t)),
                pl.BlockSpec((TILE, rest), lambda t: (t, 0)),
            ]
            + specs,
            5 * many * width * rest,
            3e7,
            50,
            grid=(tiles,),
            name="mlp_second",
        )(grad_all, h_all, weights[1], d_h, *got)

    def down_of(hidden, place, got):
        tiles = many // TILE // 2
        tile_o = pl.BlockSpec((TILE, width), lambda t: (t, 0))
        shapes, specs = sums(bool(got))
        return call(
            mlp_down,
            shapes,
            [],
            [
                pl.BlockSpec((TILE, rest), lambda t: (t, 0)),
                pl.BlockSpec((rest, width), lambda t: (0, 0)),
                pl.BlockSpec((TILE, width), lambda t: (t + place * tiles, 0)),
            ]
            + [tile_o] * len(got),
            specs,
            many * width * rest,
            1e7,
            36,
            grid=(tiles,),
            name="mlp_down",
        )(hidden, weights[1], mixed, *got)

    def by_row(value):
        size = value.shape[0] // ROWS
        return [value[r * size : (r + 1) * size] for r in rows]

    def second_rows(held):
        found = [links.scatter_second(held[r], order[r]) for r in rows]
        return [f[0] for f in found], [f[1] for f in found]

    def first_rows(held):
        return [part for r in rows for part in links.scatter_first(held[r], order[r])]

    def added(keep, got):
        return [k + g for k, g in zip(keep, got)]

    d_other, hid_other, other_h = half_of(1, [])
    got_h = links.core(other_h)
    (other_m,) = down_of(hid_other, 1, [])
    got_m = links.core(other_m)
    got_h, other_m = tie(got_h, other_m)
    d_own, hid_own, keep_h, *send_h = half_of(0, [got_h])
    got_h = [links.second(send_h[r], order[r]) for r in rows]
    got_h = together(got_h)
    slots_b = grad_of(d_own, d_other, 0)
    sum_b = sum_wide(slots_b)
    keep_h, slots_b = tie(keep_h, slots_b)
    d_h = together(first_rows(added(by_row(keep_h), got_h)))
    d_h[0], hid_own = tie(d_h[0], hid_own)
    keep_m, *send_m = down_of(hid_own, 0, [got_m])
    d_h[0], keep_m = tie(d_h[0], keep_m)
    send_m, d_h = tie(send_m, d_h)
    got_m = [links.second(send_m[r], order[r]) for r in rows]
    got_m = together(got_m)

    def last_sums(held):
        found = [links.scatter_first(held[i], i) for i in both]
        return [near + far for near, far in found]

    blocks_half = 16 * SHARE
    d_mid, d_att, d_gain, *halves_o = call(
        branch_back,
        [
            shaped(TOKENS, width, dtype=F32),
            shaped(TOKENS, HQ),
            shaped(1, width, dtype=F32),
        ]
        + [shaped(blocks_half, half)] * 4,
        [pltpu.VMEM((HQ, width), BF16), pltpu.VMEM((HQ, width), BF16), dma, dma((2, 32))],
        in_smem(2) + in_vmem(8) + in_hbm(1),
        in_vmem(3) + in_hbm(4),
        4 * TOKENS * width * HQ,
        1.5e7,
        36,
        name="branch_back",
    )(*ends, *d_h, x_mid, grad, vec, attended, w_o)
    own_o, other_o = halves_o[0::2], halves_o[1::2]
    got_o = [links.core(o) for o in other_o]
    def back_of(row, d_att):
        return call(
            functools.partial(attend_back, row),
            [shaped(SEG, HQ)] + [shaped(ROW_LEN // 2, 2 * HK)] * 2,
            [],
            in_vmem(6) + in_vmem(4),
            in_vmem(3),
            5 * TOKENS * ROW_LEN * HQ,
            5e6,
            48,
            name="attend_back",
        )(q, d_att, cosine, sine, barred, lse, *kv_rows[4 * row : 4 * row + 4])

    dq_a, own_a, other_a = back_of(0, d_att)
    got_a = links.core(other_a)
    own_o, dq_a = tie(own_o, dq_a)
    held_o = added(own_o, got_o)
    keep_o = [links.scatter_second(held_o[i], i) for i in both]
    d_att, held_o = tie(d_att, held_o)
    got_m, d_att = tie(got_m, d_att)
    keep_m = added(by_row(keep_m), got_m)
    mixed = first_rows(keep_m)
    mixed[0], d_att = tie(mixed[0], d_att)
    dq_b, own_b, other_b = back_of(1, d_att)
    got_b = links.core(other_b)
    own_a, dq_b = tie(own_a, dq_b)
    keep_a, got_a = links.scatter_second(own_a + got_a, order[0])
    keep_a, dq_b = tie(keep_a, dq_b)
    d_h_q, d_bias, *halves_q = call(
        query_back,
        [shaped(TOKENS, width, dtype=F32), shaped(1, HQ, dtype=F32)] + [shaped(blocks_half, half)] * 4,
        [pltpu.VMEM((width, HQ), BF16), pltpu.VMEM((width, HQ), BF16), dma, dma((2, 32))],
        in_smem(2) + in_vmem(3) + in_hbm(1),
        in_vmem(2) + in_hbm(4),
        4 * TOKENS * width * HQ,
        1.2e7,
        32,
        name="query_back",
    )(*ends, dq_a, dq_b, h_one, w_q)
    own_q, other_q = halves_q[0::2], halves_q[1::2]
    got_q = [links.core(o) for o in other_q]
    own_b, d_h_q = tie(own_b, d_h_q)
    keep_b, got_b = links.scatter_second(own_b + got_b, order[1])
    keep_a, keep_b = tie(keep_a, keep_b)
    d_kv = list(links.scatter_first(keep_a + got_a, order[0]))
    own_q, d_kv = tie(own_q, d_kv)
    own_q, sum_a = tie(own_q, sum_a)
    held_q = added(own_q, got_q)
    keep_b, held_q = tie(keep_b, held_q)
    d_kv += links.scatter_first(keep_b + got_b, order[1])
    keep_q = [links.scatter_second(held_q[i], i) for i in both]
    grad_in, own_w, other_w = call(
        kv_back,
        [shaped(TOKENS, width)] + [shaped(16 * SHARE, KV_COLUMNS)] * 2,
        [pltpu.VMEM((width, KV_COLUMNS), BF16), dma((32,))],
        in_smem(1) + in_vmem(16),
        in_vmem(1) + in_hbm(2),
        4 * TOKENS * width * 2 * HK,
        1e7,
        24,
        name="kv_back",
    )(
        ends[0], *d_kv, x, h_one, vec, cosine, sine, d_h_q, d_mid, d_gain, d_bias,
        pick_k, pick_v, w_kv,
    )
    got_w = links.core(other_w)
    keep_o, d_h_q = tie(keep_o, d_h_q)
    sum_o = last_sums([k + g for k, g in keep_o])
    got_w, sum_o = tie(got_w, sum_o)
    keep_w, got_w = links.scatter_second(own_w + got_w, 0)
    grad_w_out = links.direct_scatter(jnp.concatenate(sum_o, axis=1))
    keep_w, keep_q = tie(keep_w, keep_q)
    near, far = links.scatter_first(keep_w + got_w, 0)
    sums_q = last_sums([k + g for k, g in keep_q])
    last = links.direct_scatter(jnp.concatenate([near + far] + sums_q, axis=1))
    kv_sum, grad_w_query = last[:, :KV_COLUMNS], last[:, KV_COLUMNS:]
    layer_out = (
        x_mid
        + jnp.concatenate([mixed[0], mixed[2]], axis=0).astype(F32)
        + jnp.concatenate([mixed[1], mixed[3]], axis=0).astype(F32)
    ).astype(BF16)
    grad_w_down, grad_w_gate, grad_w_up = [
        jnp.concatenate(
            [sum_a[i * split : (i + 1) * split], sum_b[i * rest : (i + 1) * rest]], axis=0
        ).astype(F32)
        for i in range(3)
    ]
    last = kv_sum[:, 2 * HK : 2 * HK + 4]
    return (
        layer_out.reshape(layer_in.shape),
        grad_in.reshape(layer_in.shape),
        last[:, 0],
        grad_w_query,
        last[:, 2],
        kv_sum[:, :HK],
        last[:small, 3],
        kv_sum[:, HK : 2 * HK],
        last[small : 2 * small, 3],
        grad_w_out,
        last[:, 1],
        grad_w_gate.T,
        grad_w_up.T,
        grad_w_down,
    )


def choose(*args):
    rows, seg_len, _ = args[0].shape
    fits = (rows, seg_len, lax.axis_size("narrow"), lax.axis_size("wide"), args[4].shape[0]) == (
        ROWS,
        SEG,
        PARTS,
        WIDE,
        SHARE,
    )
    return (fast_device if fits else plain_device)(*args)


def solution(mesh):
    return jax.shard_map(
        choose,
        mesh=mesh,
        in_specs=(
            P("wide", "narrow", None),
            P("wide", "narrow"),
            P("wide", "narrow"),
            P(("wide", "narrow")),
            P(("wide", "narrow"), None),
            P(("wide", "narrow")),
            P(("wide", "narrow"), None),
            P(("wide", "narrow")),
            P(("wide", "narrow"), None),
            P(("wide", "narrow")),
            P(("wide", "narrow"), None),
            P(("wide", "narrow")),
            P("wide", "narrow"),
            P("wide", "narrow"),
            P("narrow", "wide"),
            P("wide", "narrow", None),
        ),
        out_specs=(
            P("wide", "narrow", None),
            P("wide", "narrow", None),
            P(("wide", "narrow")),
            P(("wide", "narrow"), None),
            P(("wide", "narrow")),
            P(("wide", "narrow"), None),
            P(("wide", "narrow")),
            P(("wide", "narrow"), None),
            P(("wide", "narrow")),
            P(("wide", "narrow"), None),
            P(("wide", "narrow")),
            P("wide", "narrow"),
            P("wide", "narrow"),
            P("narrow", "wide"),
        ),
        check_vma=False,
    )
```

```python
import functools
import math

import jax
import jax.numpy as jnp
import numpy as np
from jax import lax
from jax.experimental import pallas as pl
from jax.experimental.pallas import tpu as pltpu
from jax.sharding import PartitionSpec as P

Q_HEADS = 12
KV_HEADS = 2
HEAD = 128
HQ = 1536
HK = 256


EPS = 1e-06
THETA = 10000.0


def norm_parts(value):
    factor = lax.rsqrt(jnp.mean(value * value, axis=-1, keepdims=True) + EPS)
    return (value * factor, factor)


def norm_back(grad, unit, factor, gain):
    scaled = grad * gain
    return factor * (scaled - unit * jnp.mean(scaled * unit, axis=-1, keepdims=True))


def rotate(value, cosine, sine):
    half = value.shape[-1] // 2
    first = value[..., :half]
    second = value[..., half:]
    return jnp.concatenate(
        [first * cosine - second * sine, second * cosine + first * sine], axis=-1
    )


def angles(places, head_size):
    freq = jnp.exp(
        jnp.arange(head_size // 2, dtype=jnp.float32) * (-2.0 * math.log(THETA) / head_size)
    )
    turn = places.astype(jnp.float32)[..., None] * freq
    return (jnp.cos(turn), jnp.sin(turn))


def row_probs(query, keys, allowed, scale):
    scores = jnp.einsum("qhgd,khd->hgqk", query, keys, preferred_element_type=jnp.float32) * scale
    scores = jnp.where(allowed[None, None], scores, -1e30)
    top = jnp.max(scores, axis=-1, keepdims=True)
    expo = jnp.exp(scores - top)
    return expo / jnp.sum(expo, axis=-1, keepdims=True)


def swiglu_back(d_hidden, gate, up):
    sigma = jax.nn.sigmoid(gate)
    active = gate * sigma
    d_gate = (d_hidden * up * sigma * (1.0 + gate * (1.0 - sigma))).astype(jnp.bfloat16)
    d_up = (d_hidden * active).astype(jnp.bfloat16)
    return (d_gate, d_up)


def plain_device(
    layer_in,
    seg_ids,
    pad_mask,
    gain_attn,
    w_query,
    b_query,
    w_key,
    b_key,
    w_value,
    b_value,
    w_out,
    gain_mlp,
    w_gate,
    w_up,
    w_down,
    grad_out,
):
    rows, seg_len, width = layer_in.shape
    parts = lax.axis_size("narrow")
    row_len = seg_len * parts
    me = lax.axis_index("narrow")
    group = Q_HEADS // KV_HEADS
    scale = 1.0 / math.sqrt(HEAD)
    f32 = jnp.float32
    bf16 = jnp.bfloat16
    ids_all, pads_all = (
        lax.all_gather(seg_ids, "narrow", axis=1, tiled=True),
        lax.all_gather(pad_mask, "narrow", axis=1, tiled=True),
    )
    wq, wk, wv, wo, g_one, g_two, bq, bk, bv = (
        lax.all_gather(w_query, ("wide", "narrow"), axis=0, tiled=True),
        lax.all_gather(w_key, ("wide", "narrow"), axis=0, tiled=True),
        lax.all_gather(w_value, ("wide", "narrow"), axis=0, tiled=True),
        lax.all_gather(w_out, ("wide", "narrow"), axis=0, tiled=True),
        lax.all_gather(gain_attn, ("wide", "narrow"), axis=0, tiled=True),
        lax.all_gather(gain_mlp, ("wide", "narrow"), axis=0, tiled=True),
        lax.all_gather(b_query, ("wide", "narrow"), axis=0, tiled=True),
        lax.all_gather(b_key, ("wide", "narrow"), axis=0, tiled=True),
        lax.all_gather(b_value, ("wide", "narrow"), axis=0, tiled=True),
    )
    wg, wu, wd = (
        lax.all_gather(w_gate, "wide", axis=0, tiled=True),
        lax.all_gather(w_up, "wide", axis=0, tiled=True),
        lax.all_gather(w_down, "wide", axis=1, tiled=True),
    )
    g_one = g_one.astype(f32)
    g_two = g_two.astype(f32)
    global_idx = me * seg_len + jnp.arange(seg_len, dtype=jnp.int32)
    begins = jnp.sum((ids_all[:, None, :] < seg_ids[:, :, None]).astype(jnp.int32), axis=-1)
    cosine, sine = angles(global_idx[None, :] - begins, HEAD)
    cosine = cosine[:, :, None, :]
    sine = sine[:, :, None, :]
    key_idx = jnp.arange(row_len, dtype=jnp.int32)
    allowed = (ids_all[:, None, :] == seg_ids[:, :, None]) & (
        key_idx[None, None, :] < global_idx[None, :, None]
    ) & (pads_all[:, None, :] == 1) | (key_idx[None, None, :] == global_idx[None, :, None])
    x_in = layer_in.astype(f32)
    unit_one, factor_one = norm_parts(x_in)
    h_one = (unit_one * g_one).astype(bf16)
    q_lin = jnp.dot(h_one, wq, preferred_element_type=f32) + bq.astype(f32)
    k_lin = jnp.dot(h_one, wk, preferred_element_type=f32) + bk.astype(f32)
    v_lin = jnp.dot(h_one, wv, preferred_element_type=f32) + bv.astype(f32)
    q_rot = rotate(q_lin.reshape(rows, seg_len, Q_HEADS, HEAD), cosine, sine).astype(bf16)
    k_rot = rotate(k_lin.reshape(rows, seg_len, KV_HEADS, HEAD), cosine, sine).astype(bf16)
    v_low = v_lin.astype(bf16)
    keys_all, values_all = (
        lax.all_gather(k_rot.reshape(rows, seg_len, HK), "narrow", axis=1, tiled=True),
        lax.all_gather(v_low, "narrow", axis=1, tiled=True),
    )
    keys_all = keys_all.reshape(rows, row_len, KV_HEADS, HEAD)
    values_all = values_all.reshape(rows, row_len, KV_HEADS, HEAD)
    queries = q_rot.reshape(rows, seg_len, KV_HEADS, group, HEAD)
    outputs = []
    for row in range(rows):
        probs = row_probs(queries[row], keys_all[row], allowed[row], scale)
        outputs.append(
            jnp.einsum(
                "hgqk,khd->qhgd", probs.astype(bf16), values_all[row], preferred_element_type=f32
            )
        )
    attended = jnp.stack(outputs).reshape(rows, seg_len, HQ).astype(bf16)
    x_mid = x_in + jnp.dot(attended, wo, preferred_element_type=f32)
    unit_two, factor_two = norm_parts(x_mid)
    h_two = (unit_two * g_two).astype(bf16)
    h_all = lax.all_gather(h_two, "narrow", axis=1, tiled=True)
    gate = jnp.dot(h_all, wg, preferred_element_type=f32)
    up = jnp.dot(h_all, wu, preferred_element_type=f32)
    hidden = (jax.nn.silu(gate) * up).astype(bf16)
    partial_value = jnp.dot(hidden, wd, preferred_element_type=f32)
    mixed = lax.psum_scatter(partial_value, "narrow", scatter_dimension=1, tiled=True)
    layer_out = (x_mid + mixed).astype(bf16)
    grad_all = lax.all_gather(grad_out, "narrow", axis=1, tiled=True)
    d_hidden = jnp.einsum("rtd,fd->rtf", grad_all, wd, preferred_element_type=f32)
    d_wd = jnp.einsum("rtf,rtd->fd", hidden, grad_all, preferred_element_type=f32)
    d_gate, d_up = swiglu_back(d_hidden, gate, up)
    d_wg = jnp.einsum("rtd,rtf->df", h_all, d_gate, preferred_element_type=f32)
    d_wu = jnp.einsum("rtd,rtf->df", h_all, d_up, preferred_element_type=f32)
    grad_w_gate, grad_w_up, grad_w_down = (
        lax.psum_scatter(d_wg, "wide", scatter_dimension=0, tiled=True),
        lax.psum_scatter(d_wu, "wide", scatter_dimension=0, tiled=True),
        lax.psum_scatter(d_wd, "wide", scatter_dimension=1, tiled=True),
    )
    d_h_part = jnp.einsum("rtf,df->rtd", d_gate, wg, preferred_element_type=f32) + jnp.einsum(
        "rtf,df->rtd", d_up, wu, preferred_element_type=f32
    )
    d_h_two = lax.psum_scatter(d_h_part, "narrow", scatter_dimension=1, tiled=True)
    d_g_two = jnp.sum(d_h_two * unit_two, axis=(0, 1))
    d_mid = grad_out.astype(f32) + norm_back(d_h_two, unit_two, factor_two, g_two)
    d_branch = d_mid.astype(bf16)
    d_wo = jnp.einsum("rsh,rsd->hd", attended, d_branch, preferred_element_type=f32)
    d_attended = jnp.einsum("rsd,hd->rsh", d_branch, wo, preferred_element_type=f32).astype(bf16)
    d_att_heads = d_attended.reshape(rows, seg_len, KV_HEADS, group, HEAD)
    query_grads = []
    key_grads = []
    value_grads = []
    for row in range(rows):
        probs = row_probs(queries[row], keys_all[row], allowed[row], scale)
        d_prob = jnp.einsum(
            "qhgd,khd->hgqk", d_att_heads[row], values_all[row], preferred_element_type=f32
        )
        delta = jnp.sum(probs * d_prob, axis=-1, keepdims=True)
        d_score = (scale * probs * (d_prob - delta)).astype(bf16)
        query_grads.append(
            jnp.einsum("hgqk,khd->qhgd", d_score, keys_all[row], preferred_element_type=f32)
        )
        key_grads.append(
            jnp.einsum("hgqk,qhgd->khd", d_score, queries[row], preferred_element_type=f32)
        )
        value_grads.append(
            jnp.einsum(
                "hgqk,qhgd->khd", probs.astype(bf16), d_att_heads[row], preferred_element_type=f32
            )
        )
    d_query = jnp.stack(query_grads).reshape(rows, seg_len, Q_HEADS, HEAD)
    d_keys_all = jnp.stack(key_grads).reshape(rows, row_len, HK)
    d_values_all = jnp.stack(value_grads).reshape(rows, row_len, HK)
    d_keys, d_values = (
        lax.psum_scatter(d_keys_all, "narrow", scatter_dimension=1, tiled=True),
        lax.psum_scatter(d_values_all, "narrow", scatter_dimension=1, tiled=True),
    )
    dq_lin = rotate(d_query, cosine, -sine).reshape(rows, seg_len, HQ).astype(bf16)
    dk_lin = (
        rotate(d_keys.reshape(rows, seg_len, KV_HEADS, HEAD), cosine, -sine)
        .reshape(rows, seg_len, HK)
        .astype(bf16)
    )
    dv_lin = d_values.astype(bf16)
    d_wq = jnp.einsum("rsd,rsh->dh", h_one, dq_lin, preferred_element_type=f32)
    d_wk = jnp.einsum("rsd,rsh->dh", h_one, dk_lin, preferred_element_type=f32)
    d_wv = jnp.einsum("rsd,rsh->dh", h_one, dv_lin, preferred_element_type=f32)
    d_bq = jnp.sum(dq_lin.astype(f32), axis=(0, 1))
    d_bk = jnp.sum(dk_lin.astype(f32), axis=(0, 1))
    d_bv = jnp.sum(dv_lin.astype(f32), axis=(0, 1))
    d_h_one = jnp.einsum("rsh,dh->rsd", dq_lin, wq, preferred_element_type=f32)
    d_h_one = d_h_one + jnp.einsum("rsh,dh->rsd", dk_lin, wk, preferred_element_type=f32)
    d_h_one = d_h_one + jnp.einsum("rsh,dh->rsd", dv_lin, wv, preferred_element_type=f32)
    d_g_one = jnp.sum(d_h_one * unit_one, axis=(0, 1))
    grad_in = (d_mid + norm_back(d_h_one, unit_one, factor_one, g_one)).astype(bf16)
    (
        grad_w_query,
        grad_w_key,
        grad_w_value,
        grad_w_out,
        grad_gain_attn,
        grad_gain_mlp,
        grad_b_query,
        grad_b_key,
        grad_b_value,
    ) = (
        lax.psum_scatter(d_wq, ("wide", "narrow"), scatter_dimension=0, tiled=True),
        lax.psum_scatter(d_wk, ("wide", "narrow"), scatter_dimension=0, tiled=True),
        lax.psum_scatter(d_wv, ("wide", "narrow"), scatter_dimension=0, tiled=True),
        lax.psum_scatter(d_wo, ("wide", "narrow"), scatter_dimension=0, tiled=True),
        lax.psum_scatter(d_g_one, ("wide", "narrow"), scatter_dimension=0, tiled=True),
        lax.psum_scatter(d_g_two, ("wide", "narrow"), scatter_dimension=0, tiled=True),
        lax.psum_scatter(d_bq, ("wide", "narrow"), scatter_dimension=0, tiled=True),
        lax.psum_scatter(d_bk, ("wide", "narrow"), scatter_dimension=0, tiled=True),
        lax.psum_scatter(d_bv, ("wide", "narrow"), scatter_dimension=0, tiled=True),
    )
    return (
        layer_out,
        grad_in,
        grad_gain_attn,
        grad_w_query,
        grad_b_query,
        grad_w_key,
        grad_b_key,
        grad_w_value,
        grad_b_value,
        grad_w_out,
        grad_gain_mlp,
        grad_w_gate,
        grad_w_up,
        grad_w_down,
    )


F32 = jnp.float32
BF16 = jnp.bfloat16
ROWS = 2
PARTS = 8
WIDE = 4
SEG = 128
SHARE = 48
GROUP = Q_HEADS // KV_HEADS
SCALE = 1.0 / math.sqrt(HEAD)
TOKENS = ROWS * SEG
ROW_LEN = SEG * PARTS
KV_COLUMNS = 2 * HK + 128
FIRST = KV_COLUMNS + 512
TILE = 512


def dot_nn(left, right):
    return lax.dot_general(left, right, (((1,), (0,)), ((), ())), preferred_element_type=F32)


def dot_nt(left, right):
    return lax.dot_general(left, right, (((1,), (1,)), ((), ())), preferred_element_type=F32)


def flipped(value):
    return value.astype(F32).T.astype(BF16)


class Links:
    def __init__(self):
        self.orders = ((2, 4, 1), (4, 2, 1))

    def hop(self, value, bit):
        return lax.ppermute(value, "narrow", [(i, i ^ bit) for i in range(PARTS)])

    def offsets(self, which):
        found = [0]
        for bit in self.orders[which]:
            found = found + [o ^ bit for o in found]
        return found

    def first(self, value, which):
        return self.hop(value, self.orders[which][0])

    def second(self, value, which):
        return self.hop(value, self.orders[which][1])

    def core(self, value):
        return self.hop(value, 1)

    def gather(self, value, which):
        near = jnp.concatenate([value, self.first(value, which)], axis=0)
        far = self.second(near, which)
        return [near, far, self.core(near), self.core(far)]

    def scatter_second(self, held, which):
        half = held.shape[0] // 2
        return held[:half], self.second(held[half:], which)

    def scatter_first(self, held, which):
        half = held.shape[0] // 2
        return held[:half], self.first(held[half:], which)

    def over_wide(self, value, step):
        return lax.ppermute(value, "wide", [(i, (i + step) % WIDE) for i in range(WIDE)])

    def direct_gather(self, value):
        return [value] + [self.over_wide(value, k) for k in range(1, WIDE)]

    def direct_scatter(self, held):
        slots = held.reshape((WIDE, held.shape[0] // WIDE) + held.shape[1:])
        total = slots[0].astype(F32)
        for k in range(1, WIDE):
            total = total + self.over_wide(slots[k], -k).astype(F32)
        return total


def tie(one, other):
    return lax.optimization_barrier((one, other))


def together(values):
    return list(lax.optimization_barrier(tuple(values)))


def in_vmem(count):
    return [pl.BlockSpec(memory_space=pltpu.VMEM)] * count


def in_smem(count):
    return [pl.BlockSpec(memory_space=pltpu.SMEM)] * count


def in_hbm(count):
    return [pl.BlockSpec(memory_space=pltpu.HBM)] * count


def call(body, outs, scratch, in_specs, out_specs, flops, nbytes, vmem, grid=None, name=None):
    return pl.pallas_call(
        body,
        out_shape=outs,
        grid=grid if grid is not None else (),
        in_specs=in_specs,
        out_specs=out_specs,
        scratch_shapes=scratch,
        name=name,
        compiler_params=pltpu.CompilerParams(vmem_limit_bytes=vmem * 1024 * 1024),
        cost_estimate=pl.CostEstimate(
            flops=int(flops), bytes_accessed=int(nbytes), transcendentals=0
        ),
    )


def shaped(*dims, dtype=BF16):
    return jax.ShapeDtypeStruct(dims, dtype)


def weight_copies(pieces, held, starts, sems, source, target):
    copies = []
    for i in range(PARTS * WIDE):
        copies.append(
            pltpu.make_async_copy(
                pieces[i // 8].at[pl.ds((i % 8) * SHARE, SHARE), source],
                held.at[pl.ds(pl.multiple_of(starts[i], 16), SHARE), target],
                sems.at[i],
            )
        )
    return copies


def grad_copies(held, own, other, starts, sems, columns):
    copies = []
    for i in range(PARTS * WIDE):
        target = own if i < 16 else other
        copies.append(
            pltpu.make_async_copy(
                held.at[pl.ds(pl.multiple_of(starts[i], 16), SHARE), columns],
                target.at[pl.ds((i % 16) * SHARE, SHARE), :],
                sems.at[i],
            )
        )
    return copies


def half_copies(pieces, held, starts_a, starts_b, sems):
    half = held.shape[1] // 2
    every = slice(None)
    return weight_copies(
        pieces[:4], held, starts_a, sems.at[0], every, slice(0, half)
    ) + weight_copies(pieces[4:], held, starts_b, sems.at[1], every, slice(half, 2 * half))


def query_copies(pieces, held, starts_a, starts_b, sems):
    cut = FIRST - KV_COLUMNS
    return weight_copies(
        pieces[:4], held, starts_a, sems.at[0], slice(KV_COLUMNS, FIRST), slice(0, cut)
    ) + weight_copies(pieces[4:], held, starts_b, sems.at[1], slice(None), slice(cut, HQ))


def half_grad_copies(held, outs, starts_a, starts_b, sems):
    half = held.shape[1] // 2
    return grad_copies(
        held, outs[0], outs[1], starts_a, sems.at[0], slice(0, half)
    ) + grad_copies(held, outs[2], outs[3], starts_b, sems.at[1], slice(half, 2 * half))


def turn(value, cosine, sine):
    return value * cosine + pltpu.roll(value, HEAD // 2, 1) * sine


def project_kv(starts, x, cosine, sine, pick_k, pick_v, *refs):
    pieces, (kv_out, h_out, vec_out, whole, held, sems, out_sem) = refs[:4], refs[4:]
    copies = weight_copies(pieces, held, starts, sems, slice(0, KV_COLUMNS), slice(None))
    for copy in copies:
        copy.start()
    value = x[...].astype(F32)
    unit = value * lax.rsqrt(jnp.mean(value * value, axis=-1, keepdims=True) + EPS)
    for copy in copies:
        copy.wait()
    over = pltpu.make_async_copy(held, whole, out_sem)
    over.start()
    vec = held[:, 2 * HK :].astype(F32).T[:8, :]
    vec_out[...] = vec
    low = vec.astype(BF16)
    b_key = dot_nn(low, pick_k[...])[3:4, :]
    b_value = dot_nn(low, pick_v[...])[3:4, :]
    h_one = (unit * vec[0:1, :]).astype(BF16)
    h_out[...] = h_one
    lin = dot_nn(h_one, held[:, : 2 * HK])
    for head in range(KV_HEADS):
        cut = slice(head * HEAD, (head + 1) * HEAD)
        key = turn(lin[:, cut] + b_key[:, cut], cosine[...], sine[...])
        kv_out[:, cut] = key.astype(BF16)
    kv_out[:, HK:] = (lin[:, HK:] + b_value).astype(BF16)
    over.wait()


def project_q(starts_a, starts_b, h_one, vec, cosine, sine, *refs):
    pieces, (q_out, whole, held, sems, out_sem) = refs[:8], refs[8:]
    copies = query_copies(pieces, held, starts_a, starts_b, sems)
    for copy in copies:
        copy.start()
    for copy in copies:
        copy.wait()
    over = pltpu.make_async_copy(held, whole, out_sem)
    over.start()
    lin = dot_nn(h_one[...], held[...]) + vec[2:3, :]
    for head in range(Q_HEADS):
        cut = slice(head * HEAD, (head + 1) * HEAD)
        q_out[:, cut] = turn(lin[:, cut], cosine[...], sine[...]).astype(BF16)
    over.wait()


def stacked(ref, row, kv_head):
    first = kv_head * GROUP
    return jnp.concatenate(
        [
            ref[row * SEG : (row + 1) * SEG, (first + g) * HEAD : (first + g + 1) * HEAD]
            for g in range(GROUP)
        ],
        axis=0,
    )


def row_keys(pieces, row, column):
    return jnp.concatenate(
        [piece[:, column : column + HEAD] for piece in pieces[4 * row : 4 * row + 4]], axis=0
    )


def attend(q, barred, *refs):
    kv, (att_out, lse_out) = refs[:8], refs[8:]
    for row in range(ROWS):
        bar = barred[row]
        bar = jnp.concatenate([bar] * GROUP, axis=1)
        for kv_head in range(KV_HEADS):
            keys = row_keys(kv, row, kv_head * HEAD)
            values = row_keys(kv, row, HK + kv_head * HEAD)
            scores = dot_nt(keys, stacked(q, row, kv_head)) * SCALE + bar
            top = jnp.max(scores, axis=0, keepdims=True)
            expo = jnp.exp(scores - top)
            total = jnp.sum(expo, axis=0, keepdims=True)
            lse_out[row * KV_HEADS + kv_head] = top + jnp.log(total)
            probs = (expo / total).astype(BF16)
            out = dot_nn(flipped(values), probs)
            for g in range(GROUP):
                head = kv_head * GROUP + g
                att_out[row * SEG : (row + 1) * SEG, head * HEAD : (head + 1) * HEAD] = (
                    out[:, g * SEG : (g + 1) * SEG].T.astype(BF16)
                )


def branch(starts_a, starts_b, att, x, vec, *refs):
    pieces, (mid_out, h_out, whole, held, sems, out_sem) = refs[:8], refs[8:]
    copies = half_copies(pieces, held, starts_a, starts_b, sems)
    for copy in copies:
        copy.start()
    for copy in copies:
        copy.wait()
    over = pltpu.make_async_copy(held, whole, out_sem)
    over.start()
    mid = x[...].astype(F32) + dot_nn(att[...], held[...])
    mid_out[...] = mid
    factor = lax.rsqrt(jnp.mean(mid * mid, axis=-1, keepdims=True) + EPS)
    h_out[...] = (mid * factor * vec[1:2, :]).astype(BF16)
    over.wait()


def swiglu_parts(h, grad, weights):
    units = weights.shape[0] // 3
    d_hidden = dot_nt(grad, weights[:units, :])
    both = dot_nt(h, weights[units:, :])
    gate, up = both[:, :units], both[:, units:]
    sigma = jax.nn.sigmoid(gate)
    active = gate * sigma
    hidden = (active * up).astype(BF16)
    d_gate = (d_hidden * up * sigma * (1.0 + gate * (1.0 - sigma))).astype(BF16)
    d_up = (d_hidden * active).astype(BF16)
    return hidden, d_gate, d_up


def mlp_first(grad, *refs):
    h_pieces, weights, refs = refs[:8], refs[8], refs[9:]
    d_t_out, d_h_out, mixed_out, h_all, h_v, w_v, sems, w_sem, out_sems = refs
    step = pl.program_id(0)
    rows = h_pieces[0].shape[0]
    units = w_v.shape[0] // 3

    def pieces_in():
        return [
            pltpu.make_async_copy(h_pieces[i], h_v.at[pl.ds(i * rows, rows), :], sems.at[i])
            for i in range(8)
        ]

    def weights_in():
        return pltpu.make_async_copy(weights, w_v, w_sem.at[0])

    def h_over(tile):
        at = pl.ds(pl.multiple_of(tile * TILE, TILE), TILE)
        return pltpu.make_async_copy(h_v.at[at, :], h_all.at[at, :], out_sems.at[tile])

    @pl.when(step == 0)
    def _():
        held = pieces_in()
        for copy in held[:2] + [weights_in()] + held[2:]:
            copy.start()

    for tile in range(4):

        @pl.when(step == tile)
        def _(tile=tile):
            for copy in pieces_in()[2 * tile : 2 * tile + 2]:
                copy.wait()
            h_over(tile).start()

    @pl.when(step == 0)
    def _():
        weights_in().wait()

    h = h_v[pl.ds(pl.multiple_of(step * TILE, TILE), TILE), :]
    hidden, d_gate, d_up = swiglu_parts(h, grad[...], w_v)
    d_t_out[:units, :] = hidden.T
    d_t_out[units : 2 * units, :] = d_gate.T
    d_t_out[2 * units :, :] = d_up.T
    d_pair = jnp.concatenate([d_gate, d_up], axis=1)
    d_h_out[...] = dot_nn(d_pair, w_v[units:, :]).astype(BF16)
    mixed_out[...] = dot_nn(hidden, w_v[:units, :]).astype(BF16)

    @pl.when(step == 3)
    def _():
        for tile in range(4):
            h_over(tile).wait()


def put_halves(value, outs, step):
    if len(outs) == 1:
        outs[0][...] = value
        return
    half = value.shape[0] // 2
    outs[0][...] = value[:half, :]
    for row in range(ROWS):

        @pl.when(step == row)
        def _(row=row):
            outs[1 + row][...] = value[half:, :]


def mlp_second(grad, h, weights, *refs):
    count = 3 if len(refs) == 10 else 1
    added, d_t_out, hid_out = refs[: -5 - count], refs[-5 - count], refs[-4 - count]
    h_outs, (d_v, w_v, sems) = refs[-3 - count : -3], refs[-3:]
    step = pl.program_id(0)
    units = w_v.shape[0] // 3

    def weights_in():
        return [
            pltpu.make_async_copy(
                weights.at[pl.ds(i * units, (1 + i) * units), :],
                w_v.at[pl.ds(i * units, (1 + i) * units), :],
                sems.at[i],
            )
            for i in range(2)
        ]

    @pl.when(step == 0)
    def _():
        for copy in weights_in():
            copy.start()
        for copy in weights_in():
            copy.wait()

    hidden, d_gate, d_up = swiglu_parts(h[...], grad[...], w_v)
    hid_out[...] = hidden
    d_t_out[:units, :] = hidden.T
    d_t_out[units : 2 * units, :] = d_gate.T
    d_t_out[2 * units :, :] = d_up.T
    d_v[:, :units] = d_gate
    d_v[:, units:] = d_up
    d_h = dot_nn(d_v[...], w_v[units:, :])
    for ref in added:
        d_h = d_h + ref[...].astype(F32)
    put_halves(d_h.astype(BF16), h_outs, step)


def mlp_down(hid, weights, *refs):
    count = 3 if len(refs) == 5 else 1
    added, outs = refs[:-count], refs[-count:]
    mixed = dot_nn(hid[...], weights[...])
    for ref in added:
        mixed = mixed + ref[...].astype(F32)
    put_halves(mixed.astype(BF16), outs, pl.program_id(0))


def weight_grad(left_own, left_other, right_grad, right_h, out):
    half = left_own.shape[1]
    cut = out.shape[2]

    def put(right):
        found = dot_nn(left_own[...], right[:half, :]) + dot_nn(left_other[...], right[half:, :])
        found = found.astype(BF16)
        out[0] = found[:, :cut]
        out[1] = found[:, cut:]

    @pl.when(pl.program_id(1) == 0)
    def _():
        put(right_grad)

    @pl.when(pl.program_id(1) > 0)
    def _():
        put(right_h)


def branch_back(starts_a, starts_b, keep_a, got_a, keep_b, got_b, mid, grad, vec, att, weight, *refs):
    (d_mid_out, d_att_out, d_gain_out), outs = refs[:3], refs[3:7]
    held, held_d, sem, out_sems = refs[7:]
    copy = pltpu.make_async_copy(weight, held, sem)
    copy.start()
    d_h = jnp.concatenate(
        [
            keep_a[...].astype(F32) + got_a[...].astype(F32),
            keep_b[...].astype(F32) + got_b[...].astype(F32),
        ],
        axis=0,
    )
    x_mid = mid[...]
    factor = lax.rsqrt(jnp.mean(x_mid * x_mid, axis=-1, keepdims=True) + EPS)
    unit = x_mid * factor
    d_gain_out[...] = jnp.sum(d_h * unit, axis=0, keepdims=True)
    d_mid = grad[...].astype(F32) + norm_back(d_h, unit, factor, vec[1:2, :])
    d_mid_out[...] = d_mid
    d_branch = d_mid.astype(BF16)
    held_d[...] = dot_nn(flipped(att[...]), d_branch).astype(BF16)
    out_copies = half_grad_copies(held_d, outs, starts_a, starts_b, out_sems)
    for out_copy in out_copies:
        out_copy.start()
    copy.wait()
    d_att_out[...] = dot_nt(d_branch, held[...]).astype(BF16)
    for out_copy in out_copies:
        out_copy.wait()


def attend_back(row, q, d_att, cosine, sine, barred, lse, *refs):
    kv, (dq_out, own, other) = refs[:4], refs[4:]
    bar = jnp.concatenate([barred[row]] * GROUP, axis=1)
    at = slice(row * SEG, (row + 1) * SEG)
    for kv_head in range(KV_HEADS):
        keys = row_keys(kv, 0, kv_head * HEAD)
        values = row_keys(kv, 0, HK + kv_head * HEAD)
        queries = stacked(q, row, kv_head)
        d_out = stacked(d_att, row, kv_head)
        scores = dot_nt(keys, queries) * SCALE + bar
        probs = jnp.exp(scores - lse[row * KV_HEADS + kv_head])
        d_prob = dot_nt(values, d_out)
        delta = jnp.sum(probs * d_prob, axis=0, keepdims=True)
        d_score = (SCALE * probs * (d_prob - delta)).astype(BF16)
        d_value = dot_nn(probs.astype(BF16), d_out).astype(BF16)
        d_key = dot_nn(d_score, queries).astype(BF16)
        half = ROW_LEN // 2
        cut = slice(kv_head * HEAD, (kv_head + 1) * HEAD)
        cut_v = slice(HK + kv_head * HEAD, HK + (kv_head + 1) * HEAD)
        own[:, cut] = d_key[:half]
        other[:, cut] = d_key[half:]
        own[:, cut_v] = d_value[:half]
        other[:, cut_v] = d_value[half:]
        d_query = dot_nn(flipped(keys), d_score)
        for g in range(GROUP):
            head = kv_head * GROUP + g
            back = turn(d_query[:, g * SEG : (g + 1) * SEG].T, cosine[at, :], -sine[at, :])
            dq_out[:, head * HEAD : (head + 1) * HEAD] = back.astype(BF16)


def query_back(starts_a, starts_b, dq_a, dq_b, h_one, weight, *refs):
    (d_h_out, d_bias_out), outs = refs[:2], refs[2:6]
    held, held_d, sem, out_sems = refs[6:]
    copy = pltpu.make_async_copy(weight, held, sem)
    copy.start()
    dq = jnp.concatenate([dq_a[...], dq_b[...]], axis=0)
    held_d[...] = dot_nn(flipped(h_one[...]), dq).astype(BF16)
    out_copies = half_grad_copies(held_d, outs, starts_a, starts_b, out_sems)
    for out_copy in out_copies:
        out_copy.start()
    d_bias_out[...] = jnp.sum(dq.astype(F32), axis=0, keepdims=True)
    copy.wait()
    d_h_out[...] = dot_nt(dq, held[...])
    for out_copy in out_copies:
        out_copy.wait()


def kv_back(
    starts, keep_a, got_a, keep_b, got_b, x, h_one, vec, cosine, sine, d_h_q, d_mid, d_gain, d_bias,
    pick_k, pick_v, weight, *refs,
):
    grad_out, own, other, held_d, out_sems = refs
    d_kv = jnp.concatenate(
        [
            keep_a[...].astype(F32) + got_a[...].astype(F32),
            keep_b[...].astype(F32) + got_b[...].astype(F32),
        ],
        axis=0,
    )
    parts = [
        turn(d_kv[:, head * HEAD : (head + 1) * HEAD], cosine[...], -sine[...])
        for head in range(KV_HEADS)
    ]
    d_lin = jnp.concatenate(parts + [d_kv[:, HK:]], axis=1).astype(BF16)
    held_d[:, : 2 * HK] = dot_nn(flipped(h_one[...]), d_lin).astype(BF16)
    d_small = jnp.sum(d_lin.astype(F32), axis=0, keepdims=True).astype(BF16)
    value = x[...].astype(F32)
    factor = lax.rsqrt(jnp.mean(value * value, axis=-1, keepdims=True) + EPS)
    unit = value * factor
    d_h = d_h_q[...] + dot_nt(d_lin, weight[:, : 2 * HK])
    packed = jnp.concatenate(
        [
            jnp.sum(d_h * unit, axis=0, keepdims=True),
            d_gain[...],
            d_bias[...],
            dot_nt(d_small[:, :HK], pick_k[...]) + dot_nt(d_small[:, HK:], pick_v[...]),
            jnp.zeros((124, HQ), F32),
        ],
        axis=0,
    )
    held_d[:, 2 * HK :] = packed.T.astype(BF16)
    out_copies = grad_copies(held_d, own, other, starts, out_sems, slice(None))
    for copy in out_copies:
        copy.start()
    grad_out[...] = (d_mid[...] + norm_back(d_h, unit, factor, vec[0:1, :])).astype(BF16)
    for copy in out_copies:
        copy.wait()


def fast_device(
    layer_in,
    seg_ids,
    pad_mask,
    gain_attn,
    w_query,
    b_query,
    w_key,
    b_key,
    w_value,
    b_value,
    w_out,
    gain_mlp,
    w_gate,
    w_up,
    w_down,
    grad_out,
):
    width = layer_in.shape[2]
    units = w_gate.shape[1]
    split = units * 4 // 7
    links = Links()
    here = lax.axis_index("wide")
    me = lax.axis_index("narrow")
    dma = pltpu.SemaphoreType.DMA
    order = [0, 1]
    x = layer_in.reshape(TOKENS, width)
    grad = grad_out.reshape(TOKENS, width)

    slots = jnp.arange(WIDE, dtype=jnp.int32)
    partners = [me ^ jnp.array(links.offsets(o), jnp.int32) for o in order]
    starts = [
        (p[:, None] + (slots * PARTS)[None, :]).reshape(-1) * SHARE for p in partners
    ]
    ends = [
        (p[:, None] + ((here - slots) % WIDE * PARTS)[None, :]).reshape(-1) * SHARE for p in partners
    ]
    cut = width // WIDE
    lanes = np.arange(HQ)
    small = b_key.shape[0]
    in_block = lanes % SHARE
    head_lane = lanes // SHARE * small + in_block
    pick_k = (in_block < small)[:, None] & (head_lane[:, None] == np.arange(HK))
    pick_v = ((in_block >= small) & (in_block < 2 * small))[:, None] & (
        (head_lane - small)[:, None] == np.arange(HK)
    )
    pick_k, pick_v = jnp.asarray(pick_k, BF16), jnp.asarray(pick_v, BF16)

    half = HQ // 2
    rows = range(ROWS)
    both = range(2)
    at_row = [slice(r * SEG, (r + 1) * SEG) for r in rows]

    vectors = jnp.stack(
        [gain_attn, gain_mlp, b_query, jnp.pad(jnp.concatenate([b_key, b_value]), (0, SHARE - 2 * small))],
        axis=1,
    )
    vectors = jnp.pad(vectors, ((0, 0), (0, 124)))
    own = jnp.concatenate([w_key, w_value, vectors, w_query, w_out], axis=1)
    w_rows = lax.all_gather(own, "wide", axis=0, tiled=True)
    parts = [(0, split), (split, units)]
    own_parts = [
        jnp.concatenate([w_down[p:q], w_gate.T[p:q], w_up.T[p:q]], axis=0) for p, q in parts
    ]

    grad_own = [grad[at_row[r]] for r in rows]
    grad_one = [links.first(grad_own[r], order[r]) for r in rows]
    grad_one = together(grad_one)
    marks = jnp.stack([seg_ids, pad_mask])[None]
    marks = jnp.concatenate([marks, links.first(marks, 0)], axis=0)
    marks = jnp.concatenate([marks, links.second(marks, 0)], axis=0)
    marks = jnp.concatenate([marks, links.core(marks)], axis=0)
    grad_near = [jnp.concatenate([grad_own[r], grad_one[r]], axis=0) for r in rows]
    grad_far = [links.second(grad_near[r], order[r]) for r in rows]

    at = {o: i for i, o in enumerate(links.offsets(0))}
    marks = [jnp.stack([marks[at[o], :, r] for o in links.offsets(order[r])]) for r in rows]
    ids_all = jnp.stack([m[:, 0].reshape(ROW_LEN) for m in marks])
    pads_all = jnp.stack([m[:, 1].reshape(ROW_LEN) for m in marks])
    sources = jnp.array([links.offsets(o) for o in order], jnp.int32) ^ me
    key_idx = (
        sources[:, :, None] * SEG + jnp.arange(SEG, dtype=jnp.int32)[None, None, :]
    ).reshape(ROWS, ROW_LEN)
    own_idx = me * SEG + jnp.arange(SEG, dtype=jnp.int32)
    begins = jnp.sum((ids_all[:, None, :] < seg_ids[:, :, None]).astype(jnp.int32), axis=-1)
    cosine, sine = angles((own_idx[None, :] - begins).reshape(TOKENS), HEAD)
    cosine = jnp.concatenate([cosine, cosine], axis=-1)
    sine = jnp.concatenate([-sine, sine], axis=-1)
    allowed = (ids_all[:, :, None] == seg_ids[:, None, :]) & (
        key_idx[:, :, None] < own_idx[None, None, :]
    ) & (pads_all[:, :, None] == 1) | (key_idx[:, :, None] == own_idx[None, None, :])
    barred = jnp.where(allowed, 0.0, -1e30).astype(F32)

    w_rows, (cosine, sine, barred, grad_far) = tie(w_rows, (cosine, sine, barred, grad_far))
    w_rows, own_parts[0] = tie(w_rows, own_parts[0])
    weights = [lax.all_gather(own_parts[0], "wide", axis=1, tiled=True)]
    bounds = (0, FIRST, KV_COLUMNS + HQ, KV_COLUMNS + HQ + half, KV_COLUMNS + HQ + width)
    w_slots = [w_rows[:, bounds[i] : bounds[i + 1]] for i in both]
    w_one = [links.first(w_slots[i], i) for i in both]
    w_one = together(w_one)
    w_near = [jnp.concatenate([w_slots[i], w_one[i]], axis=0) for i in both]
    w_far = [links.second(w_near[i], i) for i in both]
    w_far = together(w_far)
    grad_pieces = [p for r in rows for p in (grad_near[r], grad_far[r])]
    grad_pieces += [links.core(p) for p in grad_pieces]
    grad_all = jnp.concatenate(grad_pieces, axis=0)
    w_far, grad_all = tie(w_far, grad_all)
    w_pieces = [
        [w_near[i], w_far[i], links.core(w_near[i]), links.core(w_far[i])] for i in both
    ]
    o_slots = [w_rows[:, bounds[i + 2] : bounds[i + 3]] for i in both]
    o_slots, w_far = tie(o_slots, w_far)
    o_one = [links.first(o_slots[i], i) for i in both]
    o_one = together(o_one)
    kv, h_one, vec, w_kv = call(
        project_kv,
        [
            shaped(TOKENS, 2 * HK),
            shaped(TOKENS, width),
            shaped(8, width, dtype=F32),
            shaped(width, KV_COLUMNS),
        ],
        [pltpu.VMEM((width, KV_COLUMNS), BF16), dma((32,)), dma],
        in_smem(1) + in_vmem(5) + in_hbm(4),
        in_vmem(3) + in_hbm(1),
        2 * TOKENS * width * 2 * HK,
        4e6,
        60,
        name="project_kv",
    )(starts[0], x, cosine, sine, pick_k, pick_v, *w_pieces[0])
    kv_own = [kv[at_row[r]] for r in rows]
    kv_one = [links.first(kv_own[r], order[r]) for r in rows]
    kv_one = together(kv_one)
    q, w_q = call(
        project_q,
        [shaped(TOKENS, HQ), shaped(width, HQ)],
        [pltpu.VMEM((width, HQ), BF16), dma((2, 32)), dma],
        in_smem(2) + in_vmem(4) + in_hbm(8),
        in_vmem(1) + in_hbm(1),
        2 * TOKENS * width * HQ,
        7e6,
        60,
        name="project_q",
    )(*starts, h_one, vec, cosine, sine, *w_pieces[0], *w_pieces[1])
    kv_near = [jnp.concatenate([kv_own[r], kv_one[r]], axis=0) for r in rows]
    kv_far = [links.second(kv_near[r], order[r]) for r in rows]
    kv_far = together(kv_far)
    kv_far, q = tie(kv_far, q)
    kv_rows = []
    for r in rows:
        kv_rows += [kv_near[r], kv_far[r], links.core(kv_near[r]), links.core(kv_far[r])]
    o_near = [jnp.concatenate([o_slots[i], o_one[i]], axis=0) for i in both]
    o_far = [links.second(o_near[i], i) for i in both]
    attended, lse = call(
        attend,
        [shaped(TOKENS, HQ), shaped(ROWS * KV_HEADS, 1, GROUP * SEG, dtype=F32)],
        [],
        in_vmem(2) + in_vmem(8),
        in_vmem(2),
        4 * TOKENS * ROW_LEN * HQ,
        4e6,
        40,
        name="attend",
    )(q, barred, *kv_rows)
    attended, o_far = tie(attended, o_far)
    o_weight = []
    for i in both:
        o_weight += [o_near[i], o_far[i], links.core(o_near[i]), links.core(o_far[i])]
    x_mid, h_two, w_o = call(
        branch,
        [shaped(TOKENS, width, dtype=F32), shaped(TOKENS, width), shaped(HQ, width)],
        [pltpu.VMEM((HQ, width), BF16), dma((2, 32)), dma],
        in_smem(2) + in_vmem(3) + in_hbm(8),
        in_vmem(2) + in_hbm(1),
        2 * TOKENS * width * HQ,
        8e6,
        60,
        name="branch",
    )(*starts, attended, x, vec, *o_weight)

    h_own = [h_two[at_row[r]] for r in rows]
    h_one_hop = [links.first(h_own[r], order[r]) for r in rows]
    h_one_hop = together(h_one_hop)
    h_one_hop, own_parts[1] = tie(h_one_hop, own_parts[1])
    weights.append(lax.all_gather(own_parts[1], "wide", axis=1, tiled=True))
    h_near = [jnp.concatenate([h_own[r], h_one_hop[r]], axis=0) for r in rows]
    h_far = [links.second(h_near[r], order[r]) for r in rows]
    h_far = together(h_far)
    h_pieces = [p for r in rows for p in (h_near[r], h_far[r])]
    h_pieces += [links.core(p) for p in h_pieces]
    many = ROWS * ROW_LEN
    tile_d = pl.BlockSpec((TILE, width), lambda t: (t, 0))
    size = 3 * split
    d_t, d_h, mixed, h_all = call(
        mlp_first,
        [shaped(size, many), shaped(many, width), shaped(many, width), shaped(many, width)],
        [
            pltpu.VMEM((many, width), BF16),
            pltpu.VMEM((size, width), BF16),
            dma((8,)),
            dma((1,)),
            dma((4,)),
        ],
        [tile_d] + in_hbm(9),
        [pl.BlockSpec((size, TILE), lambda t: (0, t)), tile_d, tile_d] + in_hbm(1),
        many * width * split,
        4e6,
        56,
        grid=(many // TILE,),
        name="mlp_first",
    )(grad_all, *h_pieces, weights[0])

    def grad_of(left_own, left_other, place):
        size = left_own.shape[0]
        block = size // 3
        half_t = [
            pl.BlockSpec((block, many // 2), lambda k, m, at=at: (m, at)) for at in (0, place)
        ]
        right = pl.BlockSpec((many, 2 * cut), lambda k, m: (0, k))
        return call(
            weight_grad,
            shaped(WIDE, size, cut),
            [],
            half_t + [right, right],
            pl.BlockSpec((2, block, cut), lambda k, m: (k, m, 0)),
            (2.0 if place == 0 else 0.2) * many * width * size,
            2e7 if place == 0 else 2e6,
            48,
            grid=(WIDE // 2, 3),
            name="weight_grad",
        )(left_own, left_other, grad_all, h_all)

    def sum_wide(slots):
        return lax.psum_scatter(slots, "wide", scatter_dimension=0, tiled=False)

    slots_a = grad_of(d_t, d_t, 1)
    sum_a = sum_wide(slots_a)
    grad_all, slots_a = tie(grad_all, slots_a)
    rest = units - split

    def sums(last):
        if not last:
            return [shaped(many // 2, width)], [pl.BlockSpec((TILE, width), lambda t: (t, 0))]
        size = TILE // 2
        return (
            [shaped(2 * size, width), shaped(size, width), shaped(size, width)],
            [pl.BlockSpec((size, width), lambda t: (t, 0))]
            + [pl.BlockSpec((size, width), lambda t: (0, 0))] * 2,
        )

    def half_of(place, got):
        tiles = many // TILE // 2
        tile_d = pl.BlockSpec((TILE, width), lambda t: (t + place * tiles, 0))
        tile_o = pl.BlockSpec((TILE, width), lambda t: (t, 0))
        shapes, specs = sums(bool(got))
        return call(
            mlp_second,
            [shaped(3 * rest, many // 2), shaped(many // 2, rest)] + shapes,
            [
                pltpu.VMEM((TILE, 2 * rest), BF16),
                pltpu.VMEM((3 * rest, width), BF16),
                dma((2,)),
            ],
            [tile_d, tile_d] + in_hbm(1) + [tile_d] + [tile_o] * len(got),
            [
                pl.BlockSpec((3 * rest, TILE), lambda t: (0, t)),
                pl.BlockSpec((TILE, rest), lambda t: (t, 0)),
            ]
            + specs,
            5 * many * width * rest,
            3e7,
            50,
            grid=(tiles,),
            name="mlp_second",
        )(grad_all, h_all, weights[1], d_h, *got)

    def down_of(hidden, place, got):
        tiles = many // TILE // 2
        tile_o = pl.BlockSpec((TILE, width), lambda t: (t, 0))
        shapes, specs = sums(bool(got))
        return call(
            mlp_down,
            shapes,
            [],
            [
                pl.BlockSpec((TILE, rest), lambda t: (t, 0)),
                pl.BlockSpec((rest, width), lambda t: (0, 0)),
                pl.BlockSpec((TILE, width), lambda t: (t + place * tiles, 0)),
            ]
            + [tile_o] * len(got),
            specs,
            many * width * rest,
            1e7,
            60,
            grid=(tiles,),
            name="mlp_down",
        )(hidden, weights[1], mixed, *got)

    def by_row(value):
        size = value.shape[0] // ROWS
        return [value[r * size : (r + 1) * size] for r in rows]

    def second_rows(held):
        found = [links.scatter_second(held[r], order[r]) for r in rows]
        return [f[0] for f in found], [f[1] for f in found]

    def first_rows(held):
        return [part for r in rows for part in links.scatter_first(held[r], order[r])]

    def added(keep, got):
        return [k + g for k, g in zip(keep, got)]

    d_other, hid_other, other_h = half_of(1, [])
    got_h = links.core(other_h)
    (other_m,) = down_of(hid_other, 1, [])
    got_m = links.core(other_m)
    got_h, other_m = tie(got_h, other_m)
    d_own, hid_own, keep_h, *send_h = half_of(0, [got_h])
    got_h = [links.second(send_h[r], order[r]) for r in rows]
    got_h = together(got_h)
    slots_b = grad_of(d_own, d_other, 0)
    sum_b = sum_wide(slots_b)
    keep_h, slots_b = tie(keep_h, slots_b)
    d_h = first_rows(added(by_row(keep_h), got_h))
    d_h[0], hid_own = tie(d_h[0], hid_own)
    keep_m, *send_m = down_of(hid_own, 0, [got_m])
    d_h[0], keep_m = tie(d_h[0], keep_m)
    send_m, d_h = tie(send_m, d_h)
    got_m = [links.second(send_m[r], order[r]) for r in rows]
    got_m = together(got_m)

    def last_sums(held):
        found = [links.scatter_first(held[i], i) for i in both]
        return [near + far for near, far in found]

    blocks_half = 16 * SHARE
    d_mid, d_att, d_gain, *halves_o = call(
        branch_back,
        [
            shaped(TOKENS, width, dtype=F32),
            shaped(TOKENS, HQ),
            shaped(1, width, dtype=F32),
        ]
        + [shaped(blocks_half, half)] * 4,
        [pltpu.VMEM((HQ, width), BF16), pltpu.VMEM((HQ, width), BF16), dma, dma((2, 32))],
        in_smem(2) + in_vmem(8) + in_hbm(1),
        in_vmem(3) + in_hbm(4),
        4 * TOKENS * width * HQ,
        1.5e7,
        60,
        name="branch_back",
    )(*ends, *d_h, x_mid, grad, vec, attended, w_o)
    own_o, other_o = halves_o[0::2], halves_o[1::2]
    got_o = [links.core(o) for o in other_o]
    def back_of(row, d_att):
        return call(
            functools.partial(attend_back, row),
            [shaped(SEG, HQ)] + [shaped(ROW_LEN // 2, 2 * HK)] * 2,
            [],
            in_vmem(6) + in_vmem(4),
            in_vmem(3),
            5 * TOKENS * ROW_LEN * HQ,
            5e6,
            48,
            name="attend_back",
        )(q, d_att, cosine, sine, barred, lse, *kv_rows[4 * row : 4 * row + 4])

    dq_a, own_a, other_a = back_of(0, d_att)
    got_a = links.core(other_a)
    own_o, dq_a = tie(own_o, dq_a)
    held_o = added(own_o, got_o)
    keep_o = [links.scatter_second(held_o[i], i) for i in both]
    d_att, held_o = tie(d_att, held_o)
    dq_b, own_b, other_b = back_of(1, d_att)
    dq_b, sum_a = tie(dq_b, sum_a)
    got_b = links.core(other_b)
    own_a, dq_b = tie(own_a, dq_b)
    keep_a, got_a = links.scatter_second(own_a + got_a, order[0])
    keep_a, dq_b = tie(keep_a, dq_b)
    d_h_q, d_bias, *halves_q = call(
        query_back,
        [shaped(TOKENS, width, dtype=F32), shaped(1, HQ, dtype=F32)] + [shaped(blocks_half, half)] * 4,
        [pltpu.VMEM((width, HQ), BF16), pltpu.VMEM((width, HQ), BF16), dma, dma((2, 32))],
        in_smem(2) + in_vmem(3) + in_hbm(1),
        in_vmem(2) + in_hbm(4),
        4 * TOKENS * width * HQ,
        1.2e7,
        60,
        name="query_back",
    )(*ends, dq_a, dq_b, h_one, w_q)
    own_q, other_q = halves_q[0::2], halves_q[1::2]
    got_q = [links.core(o) for o in other_q]
    own_b, d_h_q = tie(own_b, d_h_q)
    keep_b, got_b = links.scatter_second(own_b + got_b, order[1])
    keep_a, keep_b = tie(keep_a, keep_b)
    d_kv = list(links.scatter_first(keep_a + got_a, order[0]))
    own_q, d_kv = tie(own_q, d_kv)
    held_q = added(own_q, got_q)
    keep_b, held_q = tie(keep_b, held_q)
    d_kv += links.scatter_first(keep_b + got_b, order[1])
    keep_q = [links.scatter_second(held_q[i], i) for i in both]
    grad_in, own_w, other_w = call(
        kv_back,
        [shaped(TOKENS, width)] + [shaped(16 * SHARE, KV_COLUMNS)] * 2,
        [pltpu.VMEM((width, KV_COLUMNS), BF16), dma((32,))],
        in_smem(1) + in_vmem(16),
        in_vmem(1) + in_hbm(2),
        4 * TOKENS * width * 2 * HK,
        1e7,
        24,
        name="kv_back",
    )(
        ends[0], *d_kv, x, h_one, vec, cosine, sine, d_h_q, d_mid, d_gain, d_bias,
        pick_k, pick_v, w_kv,
    )
    got_w = links.core(other_w)
    keep_o, d_h_q = tie(keep_o, d_h_q)
    sum_o = last_sums([k + g for k, g in keep_o])
    got_w, sum_o = tie(got_w, sum_o)
    got_m, own_w = tie(got_m, own_w)
    mixed = first_rows(added(by_row(keep_m), got_m))
    keep_w, got_w = links.scatter_second(own_w + got_w, 0)
    grad_w_out = links.direct_scatter(jnp.concatenate(sum_o, axis=1))
    keep_w, keep_q = tie(keep_w, keep_q)
    near, far = links.scatter_first(keep_w + got_w, 0)
    sums_q = last_sums([k + g for k, g in keep_q])
    held_last = jnp.concatenate([near + far] + sums_q, axis=1)
    held_last, sum_b = tie(held_last, sum_b)
    last = links.direct_scatter(held_last)
    kv_sum, grad_w_query = last[:, :KV_COLUMNS], last[:, KV_COLUMNS:]
    layer_out = (
        x_mid
        + jnp.concatenate([mixed[0], mixed[2]], axis=0).astype(F32)
        + jnp.concatenate([mixed[1], mixed[3]], axis=0).astype(F32)
    ).astype(BF16)
    grad_w_down, grad_w_gate, grad_w_up = [
        jnp.concatenate(
            [sum_a[i * split : (i + 1) * split], sum_b[i * rest : (i + 1) * rest]], axis=0
        ).astype(F32)
        for i in range(3)
    ]
    last = kv_sum[:, 2 * HK : 2 * HK + 4]
    return (
        layer_out.reshape(layer_in.shape),
        grad_in.reshape(layer_in.shape),
        last[:, 0],
        grad_w_query,
        last[:, 2],
        kv_sum[:, :HK],
        last[:small, 3],
        kv_sum[:, HK : 2 * HK],
        last[small : 2 * small, 3],
        grad_w_out,
        last[:, 1],
        grad_w_gate.T,
        grad_w_up.T,
        grad_w_down,
    )


def choose(*args):
    rows, seg_len, _ = args[0].shape
    fits = (rows, seg_len, lax.axis_size("narrow"), lax.axis_size("wide"), args[4].shape[0]) == (
        ROWS,
        SEG,
        PARTS,
        WIDE,
        SHARE,
    )
    return (fast_device if fits else plain_device)(*args)


def solution(mesh):
    return jax.shard_map(
        choose,
        mesh=mesh,
        in_specs=(
            P("wide", "narrow", None),
            P("wide", "narrow"),
            P("wide", "narrow"),
            P(("wide", "narrow")),
            P(("wide", "narrow"), None),
            P(("wide", "narrow")),
            P(("wide", "narrow"), None),
            P(("wide", "narrow")),
            P(("wide", "narrow"), None),
            P(("wide", "narrow")),
            P(("wide", "narrow"), None),
            P(("wide", "narrow")),
            P("wide", "narrow"),
            P("wide", "narrow"),
            P("narrow", "wide"),
            P("wide", "narrow", None),
        ),
        out_specs=(
            P("wide", "narrow", None),
            P("wide", "narrow", None),
            P(("wide", "narrow")),
            P(("wide", "narrow"), None),
            P(("wide", "narrow")),
            P(("wide", "narrow"), None),
            P(("wide", "narrow")),
            P(("wide", "narrow"), None),
            P(("wide", "narrow")),
            P(("wide", "narrow"), None),
            P(("wide", "narrow")),
            P("wide", "narrow"),
            P("wide", "narrow"),
            P("narrow", "wide"),
        ),
        check_vma=False,
    )
```

```python
import functools
import math

import jax
import jax.numpy as jnp
import numpy as np
from jax import lax
from jax.experimental import pallas as pl
from jax.experimental.pallas import tpu as pltpu
from jax.sharding import PartitionSpec as P

Q_HEADS = 12
KV_HEADS = 2
HEAD = 128
HQ = 1536
HK = 256


EPS = 1e-06
THETA = 10000.0


def norm_parts(value):
    factor = lax.rsqrt(jnp.mean(value * value, axis=-1, keepdims=True) + EPS)
    return (value * factor, factor)


def norm_back(grad, unit, factor, gain):
    scaled = grad * gain
    return factor * (scaled - unit * jnp.mean(scaled * unit, axis=-1, keepdims=True))


def rotate(value, cosine, sine):
    half = value.shape[-1] // 2
    first = value[..., :half]
    second = value[..., half:]
    return jnp.concatenate(
        [first * cosine - second * sine, second * cosine + first * sine], axis=-1
    )


def angles(places, head_size):
    freq = jnp.exp(
        jnp.arange(head_size // 2, dtype=jnp.float32) * (-2.0 * math.log(THETA) / head_size)
    )
    turn = places.astype(jnp.float32)[..., None] * freq
    return (jnp.cos(turn), jnp.sin(turn))


def row_probs(query, keys, allowed, scale):
    scores = jnp.einsum("qhgd,khd->hgqk", query, keys, preferred_element_type=jnp.float32) * scale
    scores = jnp.where(allowed[None, None], scores, -1e30)
    top = jnp.max(scores, axis=-1, keepdims=True)
    expo = jnp.exp(scores - top)
    return expo / jnp.sum(expo, axis=-1, keepdims=True)


def swiglu_back(d_hidden, gate, up):
    sigma = jax.nn.sigmoid(gate)
    active = gate * sigma
    d_gate = (d_hidden * up * sigma * (1.0 + gate * (1.0 - sigma))).astype(jnp.bfloat16)
    d_up = (d_hidden * active).astype(jnp.bfloat16)
    return (d_gate, d_up)


def plain_device(
    layer_in,
    seg_ids,
    pad_mask,
    gain_attn,
    w_query,
    b_query,
    w_key,
    b_key,
    w_value,
    b_value,
    w_out,
    gain_mlp,
    w_gate,
    w_up,
    w_down,
    grad_out,
):
    rows, seg_len, width = layer_in.shape
    parts = lax.axis_size("narrow")
    row_len = seg_len * parts
    me = lax.axis_index("narrow")
    group = Q_HEADS // KV_HEADS
    scale = 1.0 / math.sqrt(HEAD)
    f32 = jnp.float32
    bf16 = jnp.bfloat16
    ids_all, pads_all = (
        lax.all_gather(seg_ids, "narrow", axis=1, tiled=True),
        lax.all_gather(pad_mask, "narrow", axis=1, tiled=True),
    )
    wq, wk, wv, wo, g_one, g_two, bq, bk, bv = (
        lax.all_gather(w_query, ("wide", "narrow"), axis=0, tiled=True),
        lax.all_gather(w_key, ("wide", "narrow"), axis=0, tiled=True),
        lax.all_gather(w_value, ("wide", "narrow"), axis=0, tiled=True),
        lax.all_gather(w_out, ("wide", "narrow"), axis=0, tiled=True),
        lax.all_gather(gain_attn, ("wide", "narrow"), axis=0, tiled=True),
        lax.all_gather(gain_mlp, ("wide", "narrow"), axis=0, tiled=True),
        lax.all_gather(b_query, ("wide", "narrow"), axis=0, tiled=True),
        lax.all_gather(b_key, ("wide", "narrow"), axis=0, tiled=True),
        lax.all_gather(b_value, ("wide", "narrow"), axis=0, tiled=True),
    )
    wg, wu, wd = (
        lax.all_gather(w_gate, "wide", axis=0, tiled=True),
        lax.all_gather(w_up, "wide", axis=0, tiled=True),
        lax.all_gather(w_down, "wide", axis=1, tiled=True),
    )
    g_one = g_one.astype(f32)
    g_two = g_two.astype(f32)
    global_idx = me * seg_len + jnp.arange(seg_len, dtype=jnp.int32)
    begins = jnp.sum((ids_all[:, None, :] < seg_ids[:, :, None]).astype(jnp.int32), axis=-1)
    cosine, sine = angles(global_idx[None, :] - begins, HEAD)
    cosine = cosine[:, :, None, :]
    sine = sine[:, :, None, :]
    key_idx = jnp.arange(row_len, dtype=jnp.int32)
    allowed = (ids_all[:, None, :] == seg_ids[:, :, None]) & (
        key_idx[None, None, :] < global_idx[None, :, None]
    ) & (pads_all[:, None, :] == 1) | (key_idx[None, None, :] == global_idx[None, :, None])
    x_in = layer_in.astype(f32)
    unit_one, factor_one = norm_parts(x_in)
    h_one = (unit_one * g_one).astype(bf16)
    q_lin = jnp.dot(h_one, wq, preferred_element_type=f32) + bq.astype(f32)
    k_lin = jnp.dot(h_one, wk, preferred_element_type=f32) + bk.astype(f32)
    v_lin = jnp.dot(h_one, wv, preferred_element_type=f32) + bv.astype(f32)
    q_rot = rotate(q_lin.reshape(rows, seg_len, Q_HEADS, HEAD), cosine, sine).astype(bf16)
    k_rot = rotate(k_lin.reshape(rows, seg_len, KV_HEADS, HEAD), cosine, sine).astype(bf16)
    v_low = v_lin.astype(bf16)
    keys_all, values_all = (
        lax.all_gather(k_rot.reshape(rows, seg_len, HK), "narrow", axis=1, tiled=True),
        lax.all_gather(v_low, "narrow", axis=1, tiled=True),
    )
    keys_all = keys_all.reshape(rows, row_len, KV_HEADS, HEAD)
    values_all = values_all.reshape(rows, row_len, KV_HEADS, HEAD)
    queries = q_rot.reshape(rows, seg_len, KV_HEADS, group, HEAD)
    outputs = []
    for row in range(rows):
        probs = row_probs(queries[row], keys_all[row], allowed[row], scale)
        outputs.append(
            jnp.einsum(
                "hgqk,khd->qhgd", probs.astype(bf16), values_all[row], preferred_element_type=f32
            )
        )
    attended = jnp.stack(outputs).reshape(rows, seg_len, HQ).astype(bf16)
    x_mid = x_in + jnp.dot(attended, wo, preferred_element_type=f32)
    unit_two, factor_two = norm_parts(x_mid)
    h_two = (unit_two * g_two).astype(bf16)
    h_all = lax.all_gather(h_two, "narrow", axis=1, tiled=True)
    gate = jnp.dot(h_all, wg, preferred_element_type=f32)
    up = jnp.dot(h_all, wu, preferred_element_type=f32)
    hidden = (jax.nn.silu(gate) * up).astype(bf16)
    partial_value = jnp.dot(hidden, wd, preferred_element_type=f32)
    mixed = lax.psum_scatter(partial_value, "narrow", scatter_dimension=1, tiled=True)
    layer_out = (x_mid + mixed).astype(bf16)
    grad_all = lax.all_gather(grad_out, "narrow", axis=1, tiled=True)
    d_hidden = jnp.einsum("rtd,fd->rtf", grad_all, wd, preferred_element_type=f32)
    d_wd = jnp.einsum("rtf,rtd->fd", hidden, grad_all, preferred_element_type=f32)
    d_gate, d_up = swiglu_back(d_hidden, gate, up)
    d_wg = jnp.einsum("rtd,rtf->df", h_all, d_gate, preferred_element_type=f32)
    d_wu = jnp.einsum("rtd,rtf->df", h_all, d_up, preferred_element_type=f32)
    grad_w_gate, grad_w_up, grad_w_down = (
        lax.psum_scatter(d_wg, "wide", scatter_dimension=0, tiled=True),
        lax.psum_scatter(d_wu, "wide", scatter_dimension=0, tiled=True),
        lax.psum_scatter(d_wd, "wide", scatter_dimension=1, tiled=True),
    )
    d_h_part = jnp.einsum("rtf,df->rtd", d_gate, wg, preferred_element_type=f32) + jnp.einsum(
        "rtf,df->rtd", d_up, wu, preferred_element_type=f32
    )
    d_h_two = lax.psum_scatter(d_h_part, "narrow", scatter_dimension=1, tiled=True)
    d_g_two = jnp.sum(d_h_two * unit_two, axis=(0, 1))
    d_mid = grad_out.astype(f32) + norm_back(d_h_two, unit_two, factor_two, g_two)
    d_branch = d_mid.astype(bf16)
    d_wo = jnp.einsum("rsh,rsd->hd", attended, d_branch, preferred_element_type=f32)
    d_attended = jnp.einsum("rsd,hd->rsh", d_branch, wo, preferred_element_type=f32).astype(bf16)
    d_att_heads = d_attended.reshape(rows, seg_len, KV_HEADS, group, HEAD)
    query_grads = []
    key_grads = []
    value_grads = []
    for row in range(rows):
        probs = row_probs(queries[row], keys_all[row], allowed[row], scale)
        d_prob = jnp.einsum(
            "qhgd,khd->hgqk", d_att_heads[row], values_all[row], preferred_element_type=f32
        )
        delta = jnp.sum(probs * d_prob, axis=-1, keepdims=True)
        d_score = (scale * probs * (d_prob - delta)).astype(bf16)
        query_grads.append(
            jnp.einsum("hgqk,khd->qhgd", d_score, keys_all[row], preferred_element_type=f32)
        )
        key_grads.append(
            jnp.einsum("hgqk,qhgd->khd", d_score, queries[row], preferred_element_type=f32)
        )
        value_grads.append(
            jnp.einsum(
                "hgqk,qhgd->khd", probs.astype(bf16), d_att_heads[row], preferred_element_type=f32
            )
        )
    d_query = jnp.stack(query_grads).reshape(rows, seg_len, Q_HEADS, HEAD)
    d_keys_all = jnp.stack(key_grads).reshape(rows, row_len, HK)
    d_values_all = jnp.stack(value_grads).reshape(rows, row_len, HK)
    d_keys, d_values = (
        lax.psum_scatter(d_keys_all, "narrow", scatter_dimension=1, tiled=True),
        lax.psum_scatter(d_values_all, "narrow", scatter_dimension=1, tiled=True),
    )
    dq_lin = rotate(d_query, cosine, -sine).reshape(rows, seg_len, HQ).astype(bf16)
    dk_lin = (
        rotate(d_keys.reshape(rows, seg_len, KV_HEADS, HEAD), cosine, -sine)
        .reshape(rows, seg_len, HK)
        .astype(bf16)
    )
    dv_lin = d_values.astype(bf16)
    d_wq = jnp.einsum("rsd,rsh->dh", h_one, dq_lin, preferred_element_type=f32)
    d_wk = jnp.einsum("rsd,rsh->dh", h_one, dk_lin, preferred_element_type=f32)
    d_wv = jnp.einsum("rsd,rsh->dh", h_one, dv_lin, preferred_element_type=f32)
    d_bq = jnp.sum(dq_lin.astype(f32), axis=(0, 1))
    d_bk = jnp.sum(dk_lin.astype(f32), axis=(0, 1))
    d_bv = jnp.sum(dv_lin.astype(f32), axis=(0, 1))
    d_h_one = jnp.einsum("rsh,dh->rsd", dq_lin, wq, preferred_element_type=f32)
    d_h_one = d_h_one + jnp.einsum("rsh,dh->rsd", dk_lin, wk, preferred_element_type=f32)
    d_h_one = d_h_one + jnp.einsum("rsh,dh->rsd", dv_lin, wv, preferred_element_type=f32)
    d_g_one = jnp.sum(d_h_one * unit_one, axis=(0, 1))
    grad_in = (d_mid + norm_back(d_h_one, unit_one, factor_one, g_one)).astype(bf16)
    (
        grad_w_query,
        grad_w_key,
        grad_w_value,
        grad_w_out,
        grad_gain_attn,
        grad_gain_mlp,
        grad_b_query,
        grad_b_key,
        grad_b_value,
    ) = (
        lax.psum_scatter(d_wq, ("wide", "narrow"), scatter_dimension=0, tiled=True),
        lax.psum_scatter(d_wk, ("wide", "narrow"), scatter_dimension=0, tiled=True),
        lax.psum_scatter(d_wv, ("wide", "narrow"), scatter_dimension=0, tiled=True),
        lax.psum_scatter(d_wo, ("wide", "narrow"), scatter_dimension=0, tiled=True),
        lax.psum_scatter(d_g_one, ("wide", "narrow"), scatter_dimension=0, tiled=True),
        lax.psum_scatter(d_g_two, ("wide", "narrow"), scatter_dimension=0, tiled=True),
        lax.psum_scatter(d_bq, ("wide", "narrow"), scatter_dimension=0, tiled=True),
        lax.psum_scatter(d_bk, ("wide", "narrow"), scatter_dimension=0, tiled=True),
        lax.psum_scatter(d_bv, ("wide", "narrow"), scatter_dimension=0, tiled=True),
    )
    return (
        layer_out,
        grad_in,
        grad_gain_attn,
        grad_w_query,
        grad_b_query,
        grad_w_key,
        grad_b_key,
        grad_w_value,
        grad_b_value,
        grad_w_out,
        grad_gain_mlp,
        grad_w_gate,
        grad_w_up,
        grad_w_down,
    )


F32 = jnp.float32
BF16 = jnp.bfloat16
ROWS = 2
PARTS = 8
WIDE = 4
SEG = 128
SHARE = 48
GROUP = Q_HEADS // KV_HEADS
SCALE = 1.0 / math.sqrt(HEAD)
TOKENS = ROWS * SEG
ROW_LEN = SEG * PARTS
KV_COLUMNS = 2 * HK + 128
FIRST = KV_COLUMNS + 512
TILE = 512


def dot_nn(left, right):
    return lax.dot_general(left, right, (((1,), (0,)), ((), ())), preferred_element_type=F32)


def dot_nt(left, right):
    return lax.dot_general(left, right, (((1,), (1,)), ((), ())), preferred_element_type=F32)


def flipped(value):
    return value.astype(F32).T.astype(BF16)


class Links:
    def __init__(self):
        self.orders = ((2, 4, 1), (4, 2, 1))

    def hop(self, value, bit):
        return lax.ppermute(value, "narrow", [(i, i ^ bit) for i in range(PARTS)])

    def offsets(self, which):
        found = [0]
        for bit in self.orders[which]:
            found = found + [o ^ bit for o in found]
        return found

    def first(self, value, which):
        return self.hop(value, self.orders[which][0])

    def second(self, value, which):
        return self.hop(value, self.orders[which][1])

    def core(self, value):
        return self.hop(value, 1)

    def gather(self, value, which):
        near = jnp.concatenate([value, self.first(value, which)], axis=0)
        far = self.second(near, which)
        return [near, far, self.core(near), self.core(far)]

    def scatter_second(self, held, which):
        half = held.shape[0] // 2
        return held[:half], self.second(held[half:], which)

    def scatter_first(self, held, which):
        half = held.shape[0] // 2
        return held[:half], self.first(held[half:], which)

    def over_wide(self, value, step):
        return lax.ppermute(value, "wide", [(i, (i + step) % WIDE) for i in range(WIDE)])

    def direct_gather(self, value):
        return [value] + [self.over_wide(value, k) for k in range(1, WIDE)]

    def direct_scatter(self, held):
        slots = held.reshape((WIDE, held.shape[0] // WIDE) + held.shape[1:])
        total = slots[0].astype(F32)
        for k in range(1, WIDE):
            total = total + self.over_wide(slots[k], -k).astype(F32)
        return total


def tie(one, other):
    return lax.optimization_barrier((one, other))


def together(values):
    return list(lax.optimization_barrier(tuple(values)))


def in_vmem(count):
    return [pl.BlockSpec(memory_space=pltpu.VMEM)] * count


def in_smem(count):
    return [pl.BlockSpec(memory_space=pltpu.SMEM)] * count


def in_hbm(count):
    return [pl.BlockSpec(memory_space=pltpu.HBM)] * count


def call(body, outs, scratch, in_specs, out_specs, flops, nbytes, vmem, grid=None, name=None):
    return pl.pallas_call(
        body,
        out_shape=outs,
        grid=grid if grid is not None else (),
        in_specs=in_specs,
        out_specs=out_specs,
        scratch_shapes=scratch,
        name=name,
        compiler_params=pltpu.CompilerParams(vmem_limit_bytes=vmem * 1024 * 1024),
        cost_estimate=pl.CostEstimate(
            flops=int(flops), bytes_accessed=int(nbytes), transcendentals=0
        ),
    )


def shaped(*dims, dtype=BF16):
    return jax.ShapeDtypeStruct(dims, dtype)


def weight_copies(pieces, held, starts, sems, source, target):
    copies = []
    for i in range(PARTS * WIDE):
        copies.append(
            pltpu.make_async_copy(
                pieces[i // 8].at[pl.ds((i % 8) * SHARE, SHARE), source],
                held.at[pl.ds(pl.multiple_of(starts[i], 16), SHARE), target],
                sems.at[i],
            )
        )
    return copies


def grad_copies(held, own, other, starts, sems, columns):
    copies = []
    for i in range(PARTS * WIDE):
        target = own if i < 16 else other
        copies.append(
            pltpu.make_async_copy(
                held.at[pl.ds(pl.multiple_of(starts[i], 16), SHARE), columns],
                target.at[pl.ds((i % 16) * SHARE, SHARE), :],
                sems.at[i],
            )
        )
    return copies


def half_copies(pieces, held, starts_a, starts_b, sems):
    half = held.shape[1] // 2
    every = slice(None)
    return weight_copies(
        pieces[:4], held, starts_a, sems.at[0], every, slice(0, half)
    ) + weight_copies(pieces[4:], held, starts_b, sems.at[1], every, slice(half, 2 * half))


def query_copies(pieces, held, starts_a, starts_b, sems):
    cut = FIRST - KV_COLUMNS
    return weight_copies(
        pieces[:4], held, starts_a, sems.at[0], slice(KV_COLUMNS, FIRST), slice(0, cut)
    ) + weight_copies(pieces[4:], held, starts_b, sems.at[1], slice(None), slice(cut, HQ))


def half_grad_copies(held, outs, starts_a, starts_b, sems):
    half = held.shape[1] // 2
    return grad_copies(
        held, outs[0], outs[1], starts_a, sems.at[0], slice(0, half)
    ) + grad_copies(held, outs[2], outs[3], starts_b, sems.at[1], slice(half, 2 * half))


def turn(value, cosine, sine):
    return value * cosine + pltpu.roll(value, HEAD // 2, 1) * sine


def project_kv(starts, x, trig, picks, *refs):
    pieces, (kv_out, h_out, vec_out, whole, held, sems, out_sem) = refs[:4], refs[4:]
    copies = weight_copies(pieces, held, starts, sems, slice(0, KV_COLUMNS), slice(None))
    for copy in copies:
        copy.start()
    value = x[...].astype(F32)
    unit = value * lax.rsqrt(jnp.mean(value * value, axis=-1, keepdims=True) + EPS)
    for copy in copies:
        copy.wait()
    over = pltpu.make_async_copy(held, whole, out_sem)
    over.start()
    vec = held[:, 2 * HK :].astype(F32).T[:8, :]
    vec_out[...] = vec
    low = vec.astype(BF16)
    b_key = dot_nn(low, picks[:, :HK])[3:4, :]
    b_value = dot_nn(low, picks[:, HK:])[3:4, :]
    h_one = (unit * vec[0:1, :]).astype(BF16)
    h_out[...] = h_one
    lin = dot_nn(h_one, held[:, : 2 * HK])
    for head in range(KV_HEADS):
        cut = slice(head * HEAD, (head + 1) * HEAD)
        key = turn(lin[:, cut] + b_key[:, cut], trig[:, :HEAD], trig[:, HEAD:])
        kv_out[:, cut] = key.astype(BF16)
    kv_out[:, HK:] = (lin[:, HK:] + b_value).astype(BF16)
    over.wait()


def project_q(starts_a, starts_b, h_one, vec, trig, *refs):
    pieces, (q_out, whole, held, sems, out_sem) = refs[:8], refs[8:]
    copies = query_copies(pieces, held, starts_a, starts_b, sems)
    for copy in copies:
        copy.start()
    for copy in copies:
        copy.wait()
    over = pltpu.make_async_copy(held, whole, out_sem)
    over.start()
    lin = dot_nn(h_one[...], held[...]) + vec[2:3, :]
    for head in range(Q_HEADS):
        cut = slice(head * HEAD, (head + 1) * HEAD)
        q_out[:, cut] = turn(lin[:, cut], trig[:, :HEAD], trig[:, HEAD:]).astype(BF16)
    over.wait()


def stacked(ref, row, kv_head):
    first = kv_head * GROUP
    return jnp.concatenate(
        [
            ref[row * SEG : (row + 1) * SEG, (first + g) * HEAD : (first + g + 1) * HEAD]
            for g in range(GROUP)
        ],
        axis=0,
    )


def row_keys(pieces, row, column):
    return jnp.concatenate(
        [piece[:, column : column + HEAD] for piece in pieces[4 * row : 4 * row + 4]], axis=0
    )


def attend(q, barred, *refs):
    kv, (att_out, lse_out) = refs[:8], refs[8:]
    for row in range(ROWS):
        bar = barred[row]
        bar = jnp.concatenate([bar] * GROUP, axis=1)
        for kv_head in range(KV_HEADS):
            keys = row_keys(kv, row, kv_head * HEAD)
            values = row_keys(kv, row, HK + kv_head * HEAD)
            scores = dot_nt(keys, stacked(q, row, kv_head)) * SCALE + bar
            top = jnp.max(scores, axis=0, keepdims=True)
            expo = jnp.exp(scores - top)
            total = jnp.sum(expo, axis=0, keepdims=True)
            lse_out[row * KV_HEADS + kv_head] = top + jnp.log(total)
            probs = (expo / total).astype(BF16)
            out = dot_nn(flipped(values), probs)
            for g in range(GROUP):
                head = kv_head * GROUP + g
                att_out[row * SEG : (row + 1) * SEG, head * HEAD : (head + 1) * HEAD] = (
                    out[:, g * SEG : (g + 1) * SEG].T.astype(BF16)
                )


def branch(starts_a, starts_b, att, x, vec, *refs):
    pieces, (mid_out, h_out, whole, held, sems, out_sem) = refs[:8], refs[8:]
    copies = half_copies(pieces, held, starts_a, starts_b, sems)
    for copy in copies:
        copy.start()
    for copy in copies:
        copy.wait()
    over = pltpu.make_async_copy(held, whole, out_sem)
    over.start()
    mid = x[...].astype(F32) + dot_nn(att[...], held[...])
    mid_out[...] = mid
    factor = lax.rsqrt(jnp.mean(mid * mid, axis=-1, keepdims=True) + EPS)
    h_out[...] = (mid * factor * vec[1:2, :]).astype(BF16)
    over.wait()


def swiglu_parts(h, grad, weights):
    units = weights.shape[0] // 3
    d_hidden = dot_nt(grad, weights[:units, :])
    both = dot_nt(h, weights[units:, :])
    gate, up = both[:, :units], both[:, units:]
    sigma = jax.nn.sigmoid(gate)
    active = gate * sigma
    hidden = (active * up).astype(BF16)
    d_gate = (d_hidden * up * sigma * (1.0 + gate * (1.0 - sigma))).astype(BF16)
    d_up = (d_hidden * active).astype(BF16)
    return hidden, d_gate, d_up


def mlp_first(grad, *refs):
    h_pieces, weights, refs = refs[:8], refs[8], refs[9:]
    d_t_out, d_h_out, mixed_out, h_all, h_v, w_v, sems, w_sem, out_sems = refs
    step = pl.program_id(0)
    rows = h_pieces[0].shape[0]
    units = w_v.shape[0] // 3

    def pieces_in():
        return [
            pltpu.make_async_copy(h_pieces[i], h_v.at[pl.ds(i * rows, rows), :], sems.at[i])
            for i in range(8)
        ]

    def weights_in():
        return pltpu.make_async_copy(weights, w_v, w_sem.at[0])

    def h_over(tile):
        at = pl.ds(pl.multiple_of(tile * TILE, TILE), TILE)
        return pltpu.make_async_copy(h_v.at[at, :], h_all.at[at, :], out_sems.at[tile])

    @pl.when(step == 0)
    def _():
        held = pieces_in()
        for copy in held[:2] + [weights_in()] + held[2:]:
            copy.start()

    for tile in range(4):

        @pl.when(step == tile)
        def _(tile=tile):
            for copy in pieces_in()[2 * tile : 2 * tile + 2]:
                copy.wait()
            h_over(tile).start()

    @pl.when(step == 0)
    def _():
        weights_in().wait()

    h = h_v[pl.ds(pl.multiple_of(step * TILE, TILE), TILE), :]
    hidden, d_gate, d_up = swiglu_parts(h, grad[...], w_v)
    d_t_out[:units, :] = hidden.T
    d_t_out[units : 2 * units, :] = d_gate.T
    d_t_out[2 * units :, :] = d_up.T
    d_pair = jnp.concatenate([d_gate, d_up], axis=1)
    d_h_out[...] = dot_nn(d_pair, w_v[units:, :]).astype(BF16)
    mixed_out[...] = dot_nn(hidden, w_v[:units, :]).astype(BF16)

    @pl.when(step == 3)
    def _():
        for tile in range(4):
            h_over(tile).wait()


def put_halves(value, outs, step):
    if len(outs) == 1:
        outs[0][...] = value
        return
    half = value.shape[0] // 2
    outs[0][...] = value[:half, :]
    for row in range(ROWS):

        @pl.when(step == row)
        def _(row=row):
            outs[1 + row][...] = value[half:, :]


def mlp_second(grad, h, weights, *refs):
    count = 3 if len(refs) == 10 else 1
    added, d_t_out, hid_out = refs[: -5 - count], refs[-5 - count], refs[-4 - count]
    h_outs, (d_v, w_v, sems) = refs[-3 - count : -3], refs[-3:]
    step = pl.program_id(0)
    units = w_v.shape[0] // 3

    def weights_in():
        return [
            pltpu.make_async_copy(
                weights.at[pl.ds(i * units, (1 + i) * units), :],
                w_v.at[pl.ds(i * units, (1 + i) * units), :],
                sems.at[i],
            )
            for i in range(2)
        ]

    @pl.when(step == 0)
    def _():
        for copy in weights_in():
            copy.start()
        for copy in weights_in():
            copy.wait()

    hidden, d_gate, d_up = swiglu_parts(h[...], grad[...], w_v)
    hid_out[...] = hidden
    d_t_out[:units, :] = hidden.T
    d_t_out[units : 2 * units, :] = d_gate.T
    d_t_out[2 * units :, :] = d_up.T
    d_v[:, :units] = d_gate
    d_v[:, units:] = d_up
    d_h = dot_nn(d_v[...], w_v[units:, :])
    for ref in added:
        d_h = d_h + ref[...].astype(F32)
    put_halves(d_h.astype(BF16), h_outs, step)


def mlp_down(hid, weights, *refs):
    count = 3 if len(refs) == 5 else 1
    added, outs = refs[:-count], refs[-count:]
    mixed = dot_nn(hid[...], weights[...])
    for ref in added:
        mixed = mixed + ref[...].astype(F32)
    put_halves(mixed.astype(BF16), outs, pl.program_id(0))


def weight_grad(left_own, left_other, right_grad, right_h, out):
    half = left_own.shape[1]
    cut = out.shape[2]

    def put(right):
        found = dot_nn(left_own[...], right[:half, :]) + dot_nn(left_other[...], right[half:, :])
        found = found.astype(BF16)
        out[0] = found[:, :cut]
        out[1] = found[:, cut:]

    @pl.when(pl.program_id(1) == 0)
    def _():
        put(right_grad)

    @pl.when(pl.program_id(1) > 0)
    def _():
        put(right_h)


def branch_back(starts_a, starts_b, keep_a, got_a, keep_b, got_b, mid, grad, vec, att, weight, *refs):
    (d_mid_out, d_att_out, d_gain_out), outs = refs[:3], refs[3:7]
    held, held_d, sem, out_sems = refs[7:]
    copy = pltpu.make_async_copy(weight, held, sem)
    copy.start()
    d_h = jnp.concatenate(
        [
            keep_a[...].astype(F32) + got_a[...].astype(F32),
            keep_b[...].astype(F32) + got_b[...].astype(F32),
        ],
        axis=0,
    )
    x_mid = mid[...]
    factor = lax.rsqrt(jnp.mean(x_mid * x_mid, axis=-1, keepdims=True) + EPS)
    unit = x_mid * factor
    d_gain_out[...] = jnp.sum(d_h * unit, axis=0, keepdims=True)
    d_mid = grad[...].astype(F32) + norm_back(d_h, unit, factor, vec[1:2, :])
    d_mid_out[...] = d_mid
    d_branch = d_mid.astype(BF16)
    held_d[...] = dot_nn(flipped(att[...]), d_branch).astype(BF16)
    out_copies = half_grad_copies(held_d, outs, starts_a, starts_b, out_sems)
    for out_copy in out_copies:
        out_copy.start()
    copy.wait()
    d_att_out[...] = dot_nt(d_branch, held[...]).astype(BF16)
    for out_copy in out_copies:
        out_copy.wait()


def attend_back(row, q, d_att, trig, barred, lse, *refs):
    kv, (dq_out, own, other) = refs[:4], refs[4:]
    bar = jnp.concatenate([barred[row]] * GROUP, axis=1)
    at = slice(row * SEG, (row + 1) * SEG)
    for kv_head in range(KV_HEADS):
        keys = row_keys(kv, 0, kv_head * HEAD)
        values = row_keys(kv, 0, HK + kv_head * HEAD)
        queries = stacked(q, row, kv_head)
        d_out = stacked(d_att, row, kv_head)
        scores = dot_nt(keys, queries) * SCALE + bar
        probs = jnp.exp(scores - lse[row * KV_HEADS + kv_head])
        d_prob = dot_nt(values, d_out)
        delta = jnp.sum(probs * d_prob, axis=0, keepdims=True)
        d_score = (SCALE * probs * (d_prob - delta)).astype(BF16)
        d_value = dot_nn(probs.astype(BF16), d_out).astype(BF16)
        d_key = dot_nn(d_score, queries).astype(BF16)
        half = ROW_LEN // 2
        cut = slice(kv_head * HEAD, (kv_head + 1) * HEAD)
        cut_v = slice(HK + kv_head * HEAD, HK + (kv_head + 1) * HEAD)
        own[:, cut] = d_key[:half]
        other[:, cut] = d_key[half:]
        own[:, cut_v] = d_value[:half]
        other[:, cut_v] = d_value[half:]
        d_query = dot_nn(flipped(keys), d_score)
        for g in range(GROUP):
            head = kv_head * GROUP + g
            back = turn(d_query[:, g * SEG : (g + 1) * SEG].T, trig[at, :HEAD], -trig[at, HEAD:])
            dq_out[:, head * HEAD : (head + 1) * HEAD] = back.astype(BF16)


def query_back(starts_a, starts_b, dq_a, dq_b, h_one, weight, *refs):
    (d_h_out, d_bias_out), outs = refs[:2], refs[2:6]
    held, held_d, sem, out_sems = refs[6:]
    copy = pltpu.make_async_copy(weight, held, sem)
    copy.start()
    dq = jnp.concatenate([dq_a[...], dq_b[...]], axis=0)
    held_d[...] = dot_nn(flipped(h_one[...]), dq).astype(BF16)
    out_copies = half_grad_copies(held_d, outs, starts_a, starts_b, out_sems)
    for out_copy in out_copies:
        out_copy.start()
    d_bias_out[...] = jnp.sum(dq.astype(F32), axis=0, keepdims=True)
    copy.wait()
    d_h_out[...] = dot_nt(dq, held[...])
    for out_copy in out_copies:
        out_copy.wait()


def kv_back(
    starts, keep_a, got_a, keep_b, got_b, x, h_one, vec, trig, d_h_q, d_mid, d_gain, d_bias,
    picks, weight, *refs,
):
    grad_out, own, other, held_d, out_sems = refs
    d_kv = jnp.concatenate(
        [
            keep_a[...].astype(F32) + got_a[...].astype(F32),
            keep_b[...].astype(F32) + got_b[...].astype(F32),
        ],
        axis=0,
    )
    parts = [
        turn(d_kv[:, head * HEAD : (head + 1) * HEAD], trig[:, :HEAD], -trig[:, HEAD:])
        for head in range(KV_HEADS)
    ]
    d_lin = jnp.concatenate(parts + [d_kv[:, HK:]], axis=1).astype(BF16)
    held_d[:, : 2 * HK] = dot_nn(flipped(h_one[...]), d_lin).astype(BF16)
    d_small = jnp.sum(d_lin.astype(F32), axis=0, keepdims=True).astype(BF16)
    value = x[...].astype(F32)
    factor = lax.rsqrt(jnp.mean(value * value, axis=-1, keepdims=True) + EPS)
    unit = value * factor
    d_h = d_h_q[...] + dot_nt(d_lin, weight[:, : 2 * HK])
    packed = jnp.concatenate(
        [
            jnp.sum(d_h * unit, axis=0, keepdims=True),
            d_gain[...],
            d_bias[...],
            dot_nt(d_small[:, :HK], picks[:, :HK]) + dot_nt(d_small[:, HK:], picks[:, HK:]),
            jnp.zeros((124, HQ), F32),
        ],
        axis=0,
    )
    held_d[:, 2 * HK :] = packed.T.astype(BF16)
    out_copies = grad_copies(held_d, own, other, starts, out_sems, slice(None))
    for copy in out_copies:
        copy.start()
    grad_out[...] = (d_mid[...] + norm_back(d_h, unit, factor, vec[0:1, :])).astype(BF16)
    for copy in out_copies:
        copy.wait()


def fast_device(
    layer_in,
    seg_ids,
    pad_mask,
    gain_attn,
    w_query,
    b_query,
    w_key,
    b_key,
    w_value,
    b_value,
    w_out,
    gain_mlp,
    w_gate,
    w_up,
    w_down,
    grad_out,
):
    width = layer_in.shape[2]
    units = w_gate.shape[1]
    split = units * 4 // 7
    links = Links()
    here = lax.axis_index("wide")
    me = lax.axis_index("narrow")
    dma = pltpu.SemaphoreType.DMA
    order = [0, 1]
    x = layer_in.reshape(TOKENS, width)
    grad = grad_out.reshape(TOKENS, width)

    slots = jnp.arange(WIDE, dtype=jnp.int32)
    partners = [me ^ jnp.array(links.offsets(o), jnp.int32) for o in order]
    starts = [
        (p[:, None] + (slots * PARTS)[None, :]).reshape(-1) * SHARE for p in partners
    ]
    ends = [
        (p[:, None] + ((here - slots) % WIDE * PARTS)[None, :]).reshape(-1) * SHARE for p in partners
    ]
    cut = width // WIDE
    lanes = np.arange(HQ)
    small = b_key.shape[0]
    in_block = lanes % SHARE
    head_lane = lanes // SHARE * small + in_block
    pick_k = (in_block < small)[:, None] & (head_lane[:, None] == np.arange(HK))
    pick_v = ((in_block >= small) & (in_block < 2 * small))[:, None] & (
        (head_lane - small)[:, None] == np.arange(HK)
    )
    picks = jnp.asarray(np.concatenate([pick_k, pick_v], axis=1), BF16)

    half = HQ // 2
    rows = range(ROWS)
    both = range(2)
    at_row = [slice(r * SEG, (r + 1) * SEG) for r in rows]

    vectors = jnp.stack(
        [gain_attn, gain_mlp, b_query, jnp.pad(jnp.concatenate([b_key, b_value]), (0, SHARE - 2 * small))],
        axis=1,
    )
    vectors = jnp.pad(vectors, ((0, 0), (0, 124)))
    own = jnp.concatenate([w_key, w_value, vectors, w_query, w_out], axis=1)
    own, (seg_ids, pad_mask) = tie(own, (seg_ids, pad_mask))
    w_rows = lax.all_gather(own, "wide", axis=0, tiled=True)
    parts = [(0, split), (split, units)]
    own_parts = [
        jnp.concatenate([w_down[p:q], w_gate.T[p:q], w_up.T[p:q]], axis=0) for p, q in parts
    ]

    grad_own = [grad[at_row[r]] for r in rows]
    grad_one = [links.first(grad_own[r], order[r]) for r in rows]
    grad_one = together(grad_one)
    marks = jnp.stack([seg_ids, pad_mask])[None]
    marks = jnp.concatenate([marks, links.first(marks, 0)], axis=0)
    marks = jnp.concatenate([marks, links.second(marks, 0)], axis=0)
    marks = jnp.concatenate([marks, links.core(marks)], axis=0)
    grad_near = [jnp.concatenate([grad_own[r], grad_one[r]], axis=0) for r in rows]
    grad_far = [links.second(grad_near[r], order[r]) for r in rows]

    at = {o: i for i, o in enumerate(links.offsets(0))}
    marks = [jnp.stack([marks[at[o], :, r] for o in links.offsets(order[r])]) for r in rows]
    ids_all = jnp.stack([m[:, 0].reshape(ROW_LEN) for m in marks])
    pads_all = jnp.stack([m[:, 1].reshape(ROW_LEN) for m in marks])
    sources = jnp.array([links.offsets(o) for o in order], jnp.int32) ^ me
    key_idx = (
        sources[:, :, None] * SEG + jnp.arange(SEG, dtype=jnp.int32)[None, None, :]
    ).reshape(ROWS, ROW_LEN)
    own_idx = me * SEG + jnp.arange(SEG, dtype=jnp.int32)
    begins = jnp.sum((ids_all[:, None, :] < seg_ids[:, :, None]).astype(jnp.int32), axis=-1)
    cosine, sine = angles((own_idx[None, :] - begins).reshape(TOKENS), HEAD)
    trig = jnp.concatenate([cosine, cosine, -sine, sine], axis=-1)
    allowed = (ids_all[:, :, None] == seg_ids[:, None, :]) & (
        key_idx[:, :, None] < own_idx[None, None, :]
    ) & (pads_all[:, :, None] == 1) | (key_idx[:, :, None] == own_idx[None, None, :])
    barred = jnp.where(allowed, 0.0, -1e30).astype(F32)

    w_rows, (trig, barred, grad_far) = tie(w_rows, (trig, barred, grad_far))
    w_rows, own_parts[0] = tie(w_rows, own_parts[0])
    weights = [lax.all_gather(own_parts[0], "wide", axis=1, tiled=True)]
    bounds = (0, FIRST, KV_COLUMNS + HQ, KV_COLUMNS + HQ + half, KV_COLUMNS + HQ + width)
    w_slots = [w_rows[:, bounds[i] : bounds[i + 1]] for i in both]
    w_one = [links.first(w_slots[i], i) for i in both]
    w_one = together(w_one)
    w_near = [jnp.concatenate([w_slots[i], w_one[i]], axis=0) for i in both]
    w_far = [links.second(w_near[i], i) for i in both]
    w_far = together(w_far)
    grad_pieces = [p for r in rows for p in (grad_near[r], grad_far[r])]
    grad_pieces += [links.core(p) for p in grad_pieces]
    grad_all = jnp.concatenate(grad_pieces, axis=0)
    w_far, grad_all = tie(w_far, grad_all)
    w_pieces = [
        [w_near[i], w_far[i], links.core(w_near[i]), links.core(w_far[i])] for i in both
    ]
    o_slots = [w_rows[:, bounds[i + 2] : bounds[i + 3]] for i in both]
    o_slots, w_far = tie(o_slots, w_far)
    o_one = [links.first(o_slots[i], i) for i in both]
    o_one = together(o_one)
    kv, h_one, vec, w_kv = call(
        project_kv,
        [
            shaped(TOKENS, 2 * HK),
            shaped(TOKENS, width),
            shaped(8, width, dtype=F32),
            shaped(width, KV_COLUMNS),
        ],
        [pltpu.VMEM((width, KV_COLUMNS), BF16), dma((32,)), dma],
        in_smem(1) + in_vmem(3) + in_hbm(4),
        in_vmem(3) + in_hbm(1),
        2 * TOKENS * width * 2 * HK,
        4e6,
        60,
        name="project_kv",
    )(starts[0], x, trig, picks, *w_pieces[0])
    kv_own = [kv[at_row[r]] for r in rows]
    kv_one = [links.first(kv_own[r], order[r]) for r in rows]
    kv_one = together(kv_one)
    q, w_q = call(
        project_q,
        [shaped(TOKENS, HQ), shaped(width, HQ)],
        [pltpu.VMEM((width, HQ), BF16), dma((2, 32)), dma],
        in_smem(2) + in_vmem(3) + in_hbm(8),
        in_vmem(1) + in_hbm(1),
        2 * TOKENS * width * HQ,
        7e6,
        60,
        name="project_q",
    )(*starts, h_one, vec, trig, *w_pieces[0], *w_pieces[1])
    kv_near = [jnp.concatenate([kv_own[r], kv_one[r]], axis=0) for r in rows]
    kv_far = [links.second(kv_near[r], order[r]) for r in rows]
    kv_far = together(kv_far)
    kv_far, q = tie(kv_far, q)
    kv_rows = []
    for r in rows:
        kv_rows += [kv_near[r], kv_far[r], links.core(kv_near[r]), links.core(kv_far[r])]
    o_near = [jnp.concatenate([o_slots[i], o_one[i]], axis=0) for i in both]
    o_far = [links.second(o_near[i], i) for i in both]
    attended, lse = call(
        attend,
        [shaped(TOKENS, HQ), shaped(ROWS * KV_HEADS, 1, GROUP * SEG, dtype=F32)],
        [],
        in_vmem(2) + in_vmem(8),
        in_vmem(2),
        4 * TOKENS * ROW_LEN * HQ,
        4e6,
        40,
        name="attend",
    )(q, barred, *kv_rows)
    attended, o_far = tie(attended, o_far)
    o_weight = []
    for i in both:
        o_weight += [o_near[i], o_far[i], links.core(o_near[i]), links.core(o_far[i])]
    x_mid, h_two, w_o = call(
        branch,
        [shaped(TOKENS, width, dtype=F32), shaped(TOKENS, width), shaped(HQ, width)],
        [pltpu.VMEM((HQ, width), BF16), dma((2, 32)), dma],
        in_smem(2) + in_vmem(3) + in_hbm(8),
        in_vmem(2) + in_hbm(1),
        2 * TOKENS * width * HQ,
        8e6,
        60,
        name="branch",
    )(*starts, attended, x, vec, *o_weight)

    h_own = [h_two[at_row[r]] for r in rows]
    h_one_hop = [links.first(h_own[r], order[r]) for r in rows]
    h_one_hop = together(h_one_hop)
    h_one_hop, own_parts[1] = tie(h_one_hop, own_parts[1])
    weights.append(lax.all_gather(own_parts[1], "wide", axis=1, tiled=True))
    h_near = [jnp.concatenate([h_own[r], h_one_hop[r]], axis=0) for r in rows]
    h_far = [links.second(h_near[r], order[r]) for r in rows]
    h_far = together(h_far)
    h_pieces = [p for r in rows for p in (h_near[r], h_far[r])]
    h_pieces += [links.core(p) for p in h_pieces]
    many = ROWS * ROW_LEN
    tile_d = pl.BlockSpec((TILE, width), lambda t: (t, 0))
    size = 3 * split
    d_t, d_h, mixed, h_all = call(
        mlp_first,
        [shaped(size, many), shaped(many, width), shaped(many, width), shaped(many, width)],
        [
            pltpu.VMEM((many, width), BF16),
            pltpu.VMEM((size, width), BF16),
            dma((8,)),
            dma((1,)),
            dma((4,)),
        ],
        [tile_d] + in_hbm(9),
        [pl.BlockSpec((size, TILE), lambda t: (0, t)), tile_d, tile_d] + in_hbm(1),
        many * width * split,
        4e6,
        56,
        grid=(many // TILE,),
        name="mlp_first",
    )(grad_all, *h_pieces, weights[0])

    def grad_of(left_own, left_other, place):
        size = left_own.shape[0]
        block = size // 3
        half_t = [
            pl.BlockSpec((block, many // 2), lambda k, m, at=at: (m, at)) for at in (0, place)
        ]
        right = pl.BlockSpec((many, 2 * cut), lambda k, m: (0, k))
        return call(
            weight_grad,
            shaped(WIDE, size, cut),
            [],
            half_t + [right, right],
            pl.BlockSpec((2, block, cut), lambda k, m: (k, m, 0)),
            (2.0 if place == 0 else 0.2) * many * width * size,
            2e7 if place == 0 else 2e6,
            60,
            grid=(WIDE // 2, 3),
            name="weight_grad",
        )(left_own, left_other, grad_all, h_all)

    def sum_wide(slots):
        return lax.psum_scatter(slots, "wide", scatter_dimension=0, tiled=False)

    slots_a = grad_of(d_t, d_t, 1)
    sum_a = sum_wide(slots_a)
    grad_all, slots_a = tie(grad_all, slots_a)
    rest = units - split

    def sums(last):
        if not last:
            return [shaped(many // 2, width)], [pl.BlockSpec((TILE, width), lambda t: (t, 0))]
        size = TILE // 2
        return (
            [shaped(2 * size, width), shaped(size, width), shaped(size, width)],
            [pl.BlockSpec((size, width), lambda t: (t, 0))]
            + [pl.BlockSpec((size, width), lambda t: (0, 0))] * 2,
        )

    def half_of(place, got):
        tiles = many // TILE // 2
        tile_d = pl.BlockSpec((TILE, width), lambda t: (t + place * tiles, 0))
        tile_o = pl.BlockSpec((TILE, width), lambda t: (t, 0))
        shapes, specs = sums(bool(got))
        return call(
            mlp_second,
            [shaped(3 * rest, many // 2), shaped(many // 2, rest)] + shapes,
            [
                pltpu.VMEM((TILE, 2 * rest), BF16),
                pltpu.VMEM((3 * rest, width), BF16),
                dma((2,)),
            ],
            [tile_d, tile_d] + in_hbm(1) + [tile_d] + [tile_o] * len(got),
            [
                pl.BlockSpec((3 * rest, TILE), lambda t: (0, t)),
                pl.BlockSpec((TILE, rest), lambda t: (t, 0)),
            ]
            + specs,
            5 * many * width * rest,
            3e7,
            60,
            grid=(tiles,),
            name="mlp_second",
        )(grad_all, h_all, weights[1], d_h, *got)

    def down_of(hidden, place, got):
        tiles = many // TILE // 2
        tile_o = pl.BlockSpec((TILE, width), lambda t: (t, 0))
        shapes, specs = sums(bool(got))
        return call(
            mlp_down,
            shapes,
            [],
            [
                pl.BlockSpec((TILE, rest), lambda t: (t, 0)),
                pl.BlockSpec((rest, width), lambda t: (0, 0)),
                pl.BlockSpec((TILE, width), lambda t: (t + place * tiles, 0)),
            ]
            + [tile_o] * len(got),
            specs,
            many * width * rest,
            1e7,
            60,
            grid=(tiles,),
            name="mlp_down",
        )(hidden, weights[1], mixed, *got)

    def by_row(value):
        size = value.shape[0] // ROWS
        return [value[r * size : (r + 1) * size] for r in rows]

    def second_rows(held):
        found = [links.scatter_second(held[r], order[r]) for r in rows]
        return [f[0] for f in found], [f[1] for f in found]

    def first_rows(held):
        return [part for r in rows for part in links.scatter_first(held[r], order[r])]

    def added(keep, got):
        return [k + g for k, g in zip(keep, got)]

    d_other, hid_other, other_h = half_of(1, [])
    got_h = links.core(other_h)
    (other_m,) = down_of(hid_other, 1, [])
    got_m = links.core(other_m)
    got_h, other_m = tie(got_h, other_m)
    d_own, hid_own, keep_h, *send_h = half_of(0, [got_h])
    got_h = [links.second(send_h[r], order[r]) for r in rows]
    got_h = together(got_h)
    slots_b = grad_of(d_own, d_other, 0)
    sum_b = sum_wide(slots_b)
    keep_h, slots_b = tie(keep_h, slots_b)
    d_h = first_rows(added(by_row(keep_h), got_h))
    d_h[0], hid_own = tie(d_h[0], hid_own)
    keep_m, *send_m = down_of(hid_own, 0, [got_m])
    d_h[0], keep_m = tie(d_h[0], keep_m)
    send_m, d_h = tie(send_m, d_h)
    got_m = [links.second(send_m[r], order[r]) for r in rows]
    got_m = together(got_m)

    def last_sums(held):
        found = [links.scatter_first(held[i], i) for i in both]
        return [near + far for near, far in found]

    blocks_half = 16 * SHARE
    d_mid, d_att, d_gain, *halves_o = call(
        branch_back,
        [
            shaped(TOKENS, width, dtype=F32),
            shaped(TOKENS, HQ),
            shaped(1, width, dtype=F32),
        ]
        + [shaped(blocks_half, half)] * 4,
        [pltpu.VMEM((HQ, width), BF16), pltpu.VMEM((HQ, width), BF16), dma, dma((2, 32))],
        in_smem(2) + in_vmem(8) + in_hbm(1),
        in_vmem(3) + in_hbm(4),
        4 * TOKENS * width * HQ,
        1.5e7,
        60,
        name="branch_back",
    )(*ends, *d_h, x_mid, grad, vec, attended, w_o)
    own_o, other_o = halves_o[0::2], halves_o[1::2]
    got_o = [links.core(o) for o in other_o]
    def back_of(row, d_att):
        return call(
            functools.partial(attend_back, row),
            [shaped(SEG, HQ)] + [shaped(ROW_LEN // 2, 2 * HK)] * 2,
            [],
            in_vmem(5) + in_vmem(4),
            in_vmem(3),
            5 * TOKENS * ROW_LEN * HQ,
            5e6,
            48,
            name="attend_back",
        )(q, d_att, trig, barred, lse, *kv_rows[4 * row : 4 * row + 4])

    dq_a, own_a, other_a = back_of(0, d_att)
    got_a = links.core(other_a)
    own_o, dq_a = tie(own_o, dq_a)
    held_o = added(own_o, got_o)
    keep_o = [links.scatter_second(held_o[i], i) for i in both]
    d_att, held_o = tie(d_att, held_o)
    dq_b, own_b, other_b = back_of(1, d_att)
    dq_b, sum_a = tie(dq_b, sum_a)
    got_b = links.core(other_b)
    own_a, dq_b = tie(own_a, dq_b)
    keep_a, got_a = links.scatter_second(own_a + got_a, order[0])
    keep_a, dq_b = tie(keep_a, dq_b)
    d_h_q, d_bias, *halves_q = call(
        query_back,
        [shaped(TOKENS, width, dtype=F32), shaped(1, HQ, dtype=F32)] + [shaped(blocks_half, half)] * 4,
        [pltpu.VMEM((width, HQ), BF16), pltpu.VMEM((width, HQ), BF16), dma, dma((2, 32))],
        in_smem(2) + in_vmem(3) + in_hbm(1),
        in_vmem(2) + in_hbm(4),
        4 * TOKENS * width * HQ,
        1.2e7,
        60,
        name="query_back",
    )(*ends, dq_a, dq_b, h_one, w_q)
    own_q, other_q = halves_q[0::2], halves_q[1::2]
    got_q = [links.core(o) for o in other_q]
    own_b, d_h_q = tie(own_b, d_h_q)
    keep_b, got_b = links.scatter_second(own_b + got_b, order[1])
    keep_a, keep_b = tie(keep_a, keep_b)
    d_kv = list(links.scatter_first(keep_a + got_a, order[0]))
    own_q, d_kv = tie(own_q, d_kv)
    held_q = added(own_q, got_q)
    keep_b, held_q = tie(keep_b, held_q)
    d_kv += links.scatter_first(keep_b + got_b, order[1])
    keep_q = [links.scatter_second(held_q[i], i) for i in both]
    grad_in, own_w, other_w = call(
        kv_back,
        [shaped(TOKENS, width)] + [shaped(16 * SHARE, KV_COLUMNS)] * 2,
        [pltpu.VMEM((width, KV_COLUMNS), BF16), dma((32,))],
        in_smem(1) + in_vmem(14),
        in_vmem(1) + in_hbm(2),
        4 * TOKENS * width * 2 * HK,
        1e7,
        24,
        name="kv_back",
    )(
        ends[0], *d_kv, x, h_one, vec, trig, d_h_q, d_mid, d_gain, d_bias,
        picks, w_kv,
    )
    got_w = links.core(other_w)
    keep_o, d_h_q = tie(keep_o, d_h_q)
    sum_o = last_sums([k + g for k, g in keep_o])
    got_w, sum_o = tie(got_w, sum_o)
    got_w, keep_q = tie(got_w, keep_q)
    got_m, own_w = tie(got_m, own_w)
    mixed = first_rows(added(by_row(keep_m), got_m))
    keep_w, got_w = links.scatter_second(own_w + got_w, 0)
    grad_w_out = links.direct_scatter(jnp.concatenate(sum_o, axis=1))
    keep_w, keep_q = tie(keep_w, keep_q)
    near, far = links.scatter_first(keep_w + got_w, 0)
    sums_q = last_sums([k + g for k, g in keep_q])
    held_last = jnp.concatenate([near + far] + sums_q, axis=1)
    held_last, sum_b = tie(held_last, sum_b)
    last = links.direct_scatter(held_last)
    kv_sum, grad_w_query = last[:, :KV_COLUMNS], last[:, KV_COLUMNS:]
    layer_out = (
        x_mid
        + jnp.concatenate([mixed[0], mixed[2]], axis=0).astype(F32)
        + jnp.concatenate([mixed[1], mixed[3]], axis=0).astype(F32)
    ).astype(BF16)
    grad_w_down, grad_w_gate, grad_w_up = [
        jnp.concatenate(
            [sum_a[i * split : (i + 1) * split], sum_b[i * rest : (i + 1) * rest]], axis=0
        ).astype(F32)
        for i in range(3)
    ]
    last = kv_sum[:, 2 * HK : 2 * HK + 4]
    return (
        layer_out.reshape(layer_in.shape),
        grad_in.reshape(layer_in.shape),
        last[:, 0],
        grad_w_query,
        last[:, 2],
        kv_sum[:, :HK],
        last[:small, 3],
        kv_sum[:, HK : 2 * HK],
        last[small : 2 * small, 3],
        grad_w_out,
        last[:, 1],
        grad_w_gate.T,
        grad_w_up.T,
        grad_w_down,
    )


def choose(*args):
    rows, seg_len, _ = args[0].shape
    fits = (rows, seg_len, lax.axis_size("narrow"), lax.axis_size("wide"), args[4].shape[0]) == (
        ROWS,
        SEG,
        PARTS,
        WIDE,
        SHARE,
    )
    return (fast_device if fits else plain_device)(*args)


def solution(mesh):
    return jax.shard_map(
        choose,
        mesh=mesh,
        in_specs=(
            P("wide", "narrow", None),
            P("wide", "narrow"),
            P("wide", "narrow"),
            P(("wide", "narrow")),
            P(("wide", "narrow"), None),
            P(("wide", "narrow")),
            P(("wide", "narrow"), None),
            P(("wide", "narrow")),
            P(("wide", "narrow"), None),
            P(("wide", "narrow")),
            P(("wide", "narrow"), None),
            P(("wide", "narrow")),
            P("wide", "narrow"),
            P("wide", "narrow"),
            P("narrow", "wide"),
            P("wide", "narrow", None),
        ),
        out_specs=(
            P("wide", "narrow", None),
            P("wide", "narrow", None),
            P(("wide", "narrow")),
            P(("wide", "narrow"), None),
            P(("wide", "narrow")),
            P(("wide", "narrow"), None),
            P(("wide", "narrow")),
            P(("wide", "narrow"), None),
            P(("wide", "narrow")),
            P(("wide", "narrow"), None),
            P(("wide", "narrow")),
            P("wide", "narrow"),
            P("wide", "narrow"),
            P("narrow", "wide"),
        ),
        check_vma=False,
    )
```
